32 devices in a mesh: parts: 2 (over x), mag: 16 (over z, y, core).
Axes of the slice: x: 2, y: 2, z: 4, core: 2. Of those that a mesh axis runs over, the one named last changes fastest.
Arguments:
- density: float32 [128, 16, 128], P(('parts', 'mag')), parts along dimension 0, may hold values from 0.5 to 2
- velocity: float32 [3, 128, 16, 128], P(None, ('parts', 'mag')), parts along dimension 1, may hold values from -1.2 to 1.2
- mag_field: float32 [3, 128, 16, 128], P(None, ('parts', 'mag')), parts along dimension 1, may hold values from -2 to 2
- pressure: float32 [128, 16, 128], P(('parts', 'mag')), parts along dimension 0, may hold values from 0.5 to 2
- conductance: float32 [128, 2048], P(('parts', 'mag')), parts along dimension 0, may hold values from 0.5 to 5
- shell_cell: int32 [16384], P('mag'), may hold values from 0 to 8191
- foot_owner: int32 [16384, 1], replicated, may hold values from 0 to 15; in each aligned block of 1024 rows (0 to 1023, 1024 to 2047, ...) at most 160 rows name the same one
- foot_row: int32 [16384], replicated, may hold values from 0 to 3
- foot_lon: int32 [16384], replicated, may hold values from 0 to 2047
Outputs:
- new_density: float32 [128, 16, 128], P(('parts', 'mag')), parts along dimension 0
- new_velocity: float32 [3, 128, 16, 128], P(None, ('parts', 'mag')), parts along dimension 1
- new_field: float32 [3, 128, 16, 128], P(None, ('parts', 'mag')), parts along dimension 1
- new_pressure: float32 [128, 16, 128], P(('parts', 'mag')), parts along dimension 0
- potential: float32 [128, 2048], P(('parts', 'mag')), parts along dimension 0
- shell_potential: float32 [32768], P(('parts', 'mag')), parts along dimension 0
The draws below stay inside these ranges and needn't reach their ends.
There are 2 independent parts, one for each index of `parts`. The reference program is written for one: setup_inputs(seed, part) draws one part's arguments, and reference() takes and returns one part's arrays. A program takes and returns all parts, laid end to end along the dimension named above; an argument that names none is the same for every part. Nothing has to cross between parts.
Inputs may be any that keep to these rules, and one draw needn't show every extreme that they name: `foot_owner`: in each device's aligned block of 1024 rows no owner is named by more than 160 rows.
All inputs are finite; a program needn't handle non-finite values.
Results may differ from the reference program's by a relative error of at most 0.0003.
Values sent between devices are 32-bit elements; how exact they have to be, the bound alone decides.
No kernel may reach another device: no remote copies, remote signals or barrier semaphores. Data moves between devices by JAX's collectives and lax.ppermute only.
A program may use at most 64 MiB of HBM per device.

```python
import math
import jax
import jax.numpy as jnp
import numpy as np
from jax import lax

CX = 4
NY = 16
NZ = 128
LAT_DEV = 4
NLON = 2048
SHELL = 1024
SWEEPS = 4
CAP = 160
NX = 64
NLAT = 64
SHELL_TOTAL = 16384
N_MAG = 16


def touch_ends(values, key, smallest, largest):
    longest = values.shape.index(max(values.shape))
    spots = []
    for shift in (0, 1):
        where = [jax.random.randint(jax.random.fold_in(key, axis), (), 0, length) for axis, length in enumerate(values.shape)]
        where[longest] = (where[longest] + shift) % values.shape[longest]
        spots.append(tuple(where))
    return values.at[spots[0]].set(smallest).at[spots[1]].set(largest)


def block_levels(own_key, shape, shards, low, largest):
    factor_of, own = 1.0, jax.random.fold_in(own_key, 6)
    for position, blocks in shards:
        draws = jnp.exp(jax.random.uniform(jax.random.fold_in(own, position), (blocks,), jnp.float32, low / len(shards), largest / len(shards)))
        factor_of = factor_of * jnp.repeat(draws, shape[position] // blocks).reshape([-1 if axis == position else 1 for axis in range(len(shape))])
    return factor_of


def shared_out(stream_key, own, number, rows, count, top, most, skew):
    order = jax.random.permutation(stream_key, count)
    heavy_load, common = shares(count, rows * top, most, skew, True), shares(count, rows * top, most, skew, False)
    places = jnp.arange(count)

    def named(sizes, rotation):
        used = int((sizes > 0).sum())
        fixed = max(1, used // 4)
        passed = fixed + (places - fixed + rotation * (used - fixed)) % max(1, count - fixed)
        return jnp.zeros((count,), jnp.int32).at[order[jnp.where(places < fixed, places, passed)]].set(jnp.asarray(sizes, jnp.int32))

    sizes = jnp.where(number % 4 == 0, named(heavy_load, number // 4), named(common, number - number // 4 - 1))
    mixed = jax.random.permutation(jax.random.fold_in(own, 3), count)
    donor, receiver = mixed[0:count // 2 * 2:2], mixed[1:count // 2 * 2:2]
    margin = jnp.minimum(sizes[donor] - 1, most - sizes[receiver]) // 2
    margin = jnp.where((donor == order[0]) | (receiver == order[0]) | (sizes[receiver] == 0), 0, jnp.maximum(margin, 0))
    passed = jax.random.randint(jax.random.fold_in(own, 4), (count // 2,), 0, 1 << 20) % (margin + 1)
    sizes = sizes.at[donor].add(-passed).at[receiver].add(passed)
    items = jnp.searchsorted(jnp.cumsum(sizes), jnp.arange(rows * top), side="right").astype(jnp.int32)
    listing = items.reshape(top, rows).T
    listing = listing[jax.random.permutation(jax.random.fold_in(own, 1), rows)]
    rotation = jax.random.randint(jax.random.fold_in(own, 2), (rows, 1), 0, top)
    return jnp.take_along_axis(listing, (jnp.arange(top)[None, :] + rotation) % top, axis=1)


def shares(amount, total, limit, lean, full):
    loads = [(1 << 20) // math.isqrt(grade ** lean) + 1 for grade in range(1, amount + 1)]
    largest = limit if full else min(limit, max(-(-total // amount), total * loads[0] // sum(loads)))
    least = 1 if total - largest >= amount - 1 else 0
    given, rest = [largest] + [least] * (amount - 1), total - largest - least * (amount - 1)
    while rest > 0:
        movable = [i for i in range(1, amount) if given[i] < largest] or [i for i in range(1, amount) if given[i] < limit]
        mass, remaining = sum([loads[i] for i in movable]), rest
        for i in movable:
            more = min(limit - given[i], max(1, remaining * loads[i] // mass), rest)
            given[i] = given[i] + more
            rest = rest - more
    return np.array(given)


def gaussian(rng, shape, spread, most, cuts=(), kind=jnp.bfloat16):
    values = jax.random.normal(rng, shape, jnp.float32) * spread
    if len(cuts) > 0:
        values = block_levels(rng, shape, cuts, -0.22, 0.18) * values
    return jnp.clip(values, min=-most, max=most).astype(kind)


def setup_inputs(seed: int = 0, part: int = 0) -> dict:
    key_list = jax.random.split(jax.random.key(seed), 10)
    part_splits = jax.random.split(jax.random.fold_in(key_list[9], part), 10)
    density = jnp.clip(0.5 + 1.5 * jax.random.uniform(part_splits[0], (NX, NY, NZ), jnp.float32) ** block_levels(part_splits[0], (NX, NY, NZ), ((0, 16),), -0.2, 0.2), 0.5, 2.0)
    velocity = gaussian(part_splits[1], (3, NX, NY, NZ), 0.3, 1.2, ((1, 16),), jnp.float32)
    mag_field = gaussian(part_splits[2], (3, NX, NY, NZ), 0.5, 2.0, ((1, 16),), jnp.float32)
    pressure = jnp.clip(0.5 + 1.5 * jax.random.uniform(part_splits[3], (NX, NY, NZ), jnp.float32) ** block_levels(part_splits[3], (NX, NY, NZ), ((0, 16),), -0.2, 0.2), 0.5, 2.0)
    conductance = jnp.clip(jnp.exp(math.log(5.0) - 2.3025851 * jax.random.uniform(part_splits[4], (NLAT, NLON), jnp.float32) ** block_levels(part_splits[4], (NLAT, NLON), ((0, 16),), -0.2, 0.2)), 0.5, 5.0)
    shell_cell = touch_ends(jax.random.randint(key_list[5], (SHELL_TOTAL,), 0, CX * NY * NZ), jax.random.fold_in(key_list[5], 1), 0, (CX * NY * NZ) - 1).astype(jnp.int32)
    foot_owner_keys = jax.random.split(jax.random.fold_in(key_list[6], 1), SHELL_TOTAL // SHELL)
    foot_owner_turns = jax.random.permutation(jax.random.fold_in(key_list[6], 3), SHELL_TOTAL // SHELL)
    foot_owner = jax.vmap(lambda own, number: shared_out(jax.random.fold_in(key_list[6], 2), own, number, SHELL, N_MAG, 1, CAP, 2))(foot_owner_keys, foot_owner_turns).reshape((SHELL_TOTAL, 1))
    foot_row = touch_ends(jax.random.randint(key_list[7], (SHELL_TOTAL,), 0, LAT_DEV), jax.random.fold_in(key_list[7], 1), 0, LAT_DEV - 1).astype(jnp.int32)
    foot_lon = touch_ends(jax.random.randint(key_list[8], (SHELL_TOTAL,), 0, NLON), jax.random.fold_in(key_list[8], 1), 0, NLON - 1).astype(jnp.int32)
    return dict(density=density, velocity=velocity, mag_field=mag_field, pressure=pressure, conductance=conductance, shell_cell=shell_cell, foot_owner=foot_owner, foot_row=foot_row, foot_lon=foot_lon)


ADIABATIC = 5.0 / 3.0
TIME_STEP = 0.02
LON_WEIGHT = 0.25
LEAK_RATE = 0.05
SOURCE_GAIN = 10.0

def minmod(lower_diff, upper_diff):
    smaller = jnp.minimum(jnp.abs(lower_diff), jnp.abs(upper_diff))
    return jnp.where(lower_diff * upper_diff > 0.0, jnp.sign(lower_diff) * smaller, 0.0)

def conserved(primitives):
    density = primitives[0]
    velocity = primitives[1:4]
    field_part = primitives[4:7]
    kinetic = 0.5 * density * lax.optimization_barrier(jnp.sum(velocity * velocity, axis=0))
    magnetic = 0.5 * lax.optimization_barrier(jnp.sum(field_part * field_part, axis=0))
    energy = primitives[7] / (ADIABATIC - 1.0) + kinetic + magnetic
    return jnp.concatenate([density[None], density[None] * velocity, field_part, energy[None]], axis=0)

def primitive(states):
    density = states[0]
    velocity = states[1:4] / density
    field_part = states[4:7]
    kinetic = 0.5 * density * lax.optimization_barrier(jnp.sum(velocity * velocity, axis=0))
    magnetic = 0.5 * lax.optimization_barrier(jnp.sum(field_part * field_part, axis=0))
    pressure = (ADIABATIC - 1.0) * (states[7] - kinetic - magnetic)
    return jnp.concatenate([density[None], velocity, field_part, pressure[None]], axis=0)

def flux_of(primitives, states, normal):
    density = primitives[0]
    velocity = primitives[1:4]
    field_part = primitives[4:7]
    normal_speed = velocity[normal]
    normal_field = field_part[normal]
    total_pressure = primitives[7] + 0.5 * lax.optimization_barrier(jnp.sum(field_part * field_part, axis=0))
    momentum = density * normal_speed * velocity - normal_field * field_part
    momentum = momentum.at[normal].add(total_pressure)
    induction = normal_speed * field_part - normal_field * velocity
    energy = (states[7] + total_pressure) * normal_speed - normal_field * lax.optimization_barrier(jnp.sum(velocity * field_part, axis=0))
    return jnp.concatenate([(density * normal_speed)[None], momentum, induction, energy[None]], axis=0)

def wave_speed(primitives, normal):
    field_sq = lax.optimization_barrier(jnp.sum(primitives[4:7] * primitives[4:7], axis=0))
    return jnp.abs(primitives[1 + normal]) + jnp.sqrt((ADIABATIC * jnp.abs(primitives[7]) + field_sq) / primitives[0])

def interface(outer_left, left_cell, right_cell, outer_right, normal):
    left_state = left_cell + 0.5 * minmod(left_cell - outer_left, right_cell - left_cell)
    right_state = right_cell - 0.5 * minmod(right_cell - left_cell, outer_right - right_cell)
    left_cons = conserved(left_state)
    right_cons = conserved(right_state)
    fastest = jnp.maximum(wave_speed(left_state, normal), wave_speed(right_state, normal))
    average = 0.5 * (flux_of(left_state, left_cons, normal) + flux_of(right_state, right_cons, normal))
    return average - 0.5 * fastest * (right_cons - left_cons)

def tendency(padded):
    inner_width = padded.shape[1] - 4
    face_flux = interface(padded[:, 0:inner_width + 1], padded[:, 1:inner_width + 2], padded[:, 2:inner_width + 3], padded[:, 3:inner_width + 4], 0)
    change = face_flux[:, 1:] - face_flux[:, :-1]
    centre = padded[:, 2:inner_width + 2]
    for normal, roll_axis in ((1, 2), (2, 3)):
        face_flux = interface(jnp.roll(centre, 2, roll_axis), jnp.roll(centre, 1, roll_axis), centre, jnp.roll(centre, -1, roll_axis), normal)
        change = change + jnp.roll(face_flux, -1, roll_axis) - face_flux
    return -change

def parallel_current(field_pad):
    centre = field_pad[:, 1:-1]

    def along_x(values):
        return 0.5 * (values[2:] - values[:-2])

    def along_y(values):
        return 0.5 * (jnp.roll(values, -1, 1) - jnp.roll(values, 1, 1))

    def along_z(values):
        return 0.5 * (jnp.roll(values, -1, 2) - jnp.roll(values, 1, 2))
    current_x = along_y(centre[2]) - along_z(centre[1])
    current_y = along_z(centre[0]) - along_x(field_pad[2])
    current_z = along_x(field_pad[1]) - along_y(centre[0])
    aligned = current_x * centre[0] + current_y * centre[1] + current_z * centre[2]
    return aligned / jnp.sqrt(lax.optimization_barrier(jnp.sum(centre * centre, axis=0)) + 1.0)

def coefficients(cond_pad):
    conduct = cond_pad[1:-1]
    north_w = 0.5 * (conduct + cond_pad[:-2])
    south_w = 0.5 * (conduct + cond_pad[2:])
    east_w = LON_WEIGHT * 0.5 * (conduct + jnp.roll(conduct, -1, 1))
    west_w = LON_WEIGHT * 0.5 * (conduct + jnp.roll(conduct, 1, 1))
    diagonal = north_w + south_w + east_w + west_w + LEAK_RATE * conduct
    return (north_w, south_w, east_w, west_w, diagonal)

def relax_sweep(pot_pad, source, weights):
    north_w, south_w, east_w, west_w, diagonal = weights
    middle_rows = pot_pad[1:-1]
    numerator = source + north_w * pot_pad[:-2] + south_w * pot_pad[2:] + east_w * jnp.roll(middle_rows, -1, 1) + west_w * jnp.roll(middle_rows, 1, 1)
    return numerator / diagonal

def edge_pad(values, layers):
    return jnp.pad(values, ((0, 0), (layers, layers), (0, 0), (0, 0)), mode='edge')

def blockwise(padded):
    starts = jnp.arange(N_MAG, dtype=jnp.int32) * CX

    def one_block(begin_cell):
        return tendency(lax.dynamic_slice_in_dim(padded, begin_cell, CX + 4, 1))
    blocks = lax.map(one_block, starts)
    return jnp.moveaxis(blocks, 0, 1).reshape(8, N_MAG * CX, NY, NZ)

def reference(density, velocity, mag_field, pressure, conductance, shell_cell, foot_owner, foot_row, foot_lon):
    primitives = jnp.concatenate([density[None], velocity, mag_field, pressure[None]], axis=0)
    current = parallel_current(edge_pad(mag_field, 1))
    start_state = conserved(primitives)
    first_state = start_state + TIME_STEP * blockwise(edge_pad(primitives, 2))
    final_state = 0.5 * start_state + 0.5 * (first_state + TIME_STEP * blockwise(edge_pad(primitive(first_state), 2)))
    result = primitive(final_state)
    picked = jnp.take_along_axis(current.reshape(N_MAG, CX * NY * NZ), shell_cell.reshape(N_MAG, SHELL), axis=1)
    shell_current = SOURCE_GAIN * picked.reshape(-1)
    owners = foot_owner[:, 0]
    target = (owners * LAT_DEV + foot_row) * NLON + foot_lon
    source = jnp.zeros((NLAT * NLON,), jnp.float32).at[target].add(shell_current).reshape(NLAT, NLON)
    weights_all = coefficients(jnp.pad(conductance, ((1, 1), (0, 0))))
    potential = jnp.zeros((NLAT, NLON), jnp.float32)
    for sweep_index in range(SWEEPS):
        potential = relax_sweep(jnp.pad(potential, ((1, 1), (0, 0))), source, weights_all)
    shell_potential = potential.reshape(-1)[target]
    return (result[0], result[1:4], result[4:7], result[7], potential, shell_potential)
```

```python
import jax
import jax.numpy as jnp
from jax import lax
from jax.experimental import pallas as pl
from jax.experimental.pallas import tpu as pltpu
from jax.sharding import PartitionSpec as P

SWEEPS = 4
ADIABATIC = 5.0 / 3.0
TIME_STEP = 0.02
LON_WEIGHT = 0.25
LEAK_RATE = 0.05
SOURCE_GAIN = 10.0
LANES = 128
RIM = SWEEPS - 1

F32 = jnp.float32
BF16 = jnp.bfloat16
I32 = jnp.int32
VMEM = pl.BlockSpec(memory_space=pltpu.VMEM)
PARAMS = pltpu.CompilerParams(vmem_limit_bytes=48 * 1024 * 1024)


def call(kernel, outs, scratch=()):
    many = isinstance(outs, (list, tuple))
    return pl.pallas_call(
        kernel,
        out_shape=outs,
        out_specs=[VMEM] * len(outs) if many else VMEM,
        scratch_shapes=list(scratch),
        compiler_params=PARAMS,
    )


def pieces(values):
    first = values.astype(BF16)
    second = (values - first.astype(F32)).astype(BF16)
    return first, second


def rows_hot(key_row, count):
    keys = jnp.broadcast_to(key_row, (count, key_row.shape[1])).astype(BF16)
    index = lax.broadcasted_iota(I32, (count, key_row.shape[1]), 0).astype(F32).astype(BF16)
    return keys == index


def half_slope(lower, centre, upper):
    out = []
    for a, b, c in zip(lower, centre, upper):
        s, t = b - a, c - b
        out.append(0.5 * (jnp.maximum(jnp.minimum(s, t), 0.0) + jnp.minimum(jnp.maximum(s, t), 0.0)))
    return out


def dot3(a, b):
    return a[0] * b[0] + a[1] * b[1] + a[2] * b[2]


def conserved(q):
    rho, v, b, p = q[0], q[1:4], q[4:7], q[7]
    energy = p * (1.0 / (ADIABATIC - 1.0)) + 0.5 * rho * dot3(v, v) + 0.5 * dot3(b, b)
    return [rho, rho * v[0], rho * v[1], rho * v[2], b[0], b[1], b[2], energy]


def primitive(u):
    rho, b = u[0], u[4:7]
    inverse = 1.0 / rho
    v = [u[k] * inverse for k in (1, 2, 3)]
    p = (ADIABATIC - 1.0) * (u[7] - 0.5 * rho * dot3(v, v) - 0.5 * dot3(b, b))
    return [rho] + v + list(b) + [p]


def side(q, d):
    rho, v, b, p = q[0], q[1:4], q[4:7], q[7]
    b2 = dot3(b, b)
    half_b2 = 0.5 * b2
    total = p + half_b2
    mom = [rho * x for x in v]
    energy = p * (1.0 / (ADIABATIC - 1.0)) + 0.5 * dot3(mom, v) + half_b2
    vn, bn, mn = v[d], b[d], mom[d]
    flux = [mn]
    for k in range(3):
        f = mn * v[k] - bn * b[k]
        flux.append(f + total if k == d else f)
    for k in range(3):
        flux.append(None if k == d else vn * b[k] - bn * v[k])
    flux.append((energy + total) * vn - bn * dot3(v, b))
    speed = jnp.abs(vn) + jnp.sqrt((ADIABATIC * jnp.abs(p) + b2) / rho)
    return [rho] + mom + list(b) + [energy], flux, speed


def face(left, right, d):
    cons_l, flux_l, speed_l = side(left, d)
    cons_r, flux_r, speed_r = side(right, d)
    half_c = 0.5 * jnp.maximum(speed_l, speed_r)
    out = []
    for k in range(8):
        jump = half_c * (cons_r[k] - cons_l[k])
        out.append(-jump if flux_l[k] is None else 0.5 * (flux_l[k] + flux_r[k]) - jump)
    return out


def periodic(q, axis, d):
    size = q[0].shape[axis]
    back = [pltpu.roll(x, 1, axis) for x in q]
    ahead = [pltpu.roll(x, size - 1, axis) for x in q]
    slope = half_slope(back, q, ahead)
    left = [x + s for x, s in zip(q, slope)]
    right = [pltpu.roll(x - s, size - 1, axis) for x, s in zip(q, slope)]
    flux = face(left, right, d)
    return [pltpu.roll(f, 1, axis) - f for f in flux]


def add(a, b):
    return [x + y for x, y in zip(a, b)]


def plane(ref, x):
    return [ref[k, x] for k in range(8)]


def upper_face(ref, x):
    a, b, c, d = (plane(ref, x + k) for k in (-1, 0, 1, 2))
    left = add(b, half_slope(a, b, c))
    right = [v - s for v, s in zip(c, half_slope(b, c, d))]
    return face(left, right, 0)


def sweep_planes(ref, first, count, put):
    def body(step, below):
        x = first + step
        above = upper_face(ref, x)
        q = plane(ref, x)
        change = [f - g for f, g in zip(below, above)]
        change = add(change, periodic(q, 0, 1))
        change = add(change, periodic(q, 1, 2))
        put(x, step, q, change)
        return above

    lax.fori_loop(0, count, body, upper_face(ref, first - 1))


def stage_one(own_ref, low_ref, high_ref, next_ref, half_ref, pad_ref):
    me = lax.axis_index("mag")
    last = lax.axis_size("mag") - 1
    cx = own_ref.shape[1]
    for k in range(8):
        first_cell, last_cell = own_ref[k, 0], own_ref[k, cx - 1]
        for x in range(cx):
            pad_ref[k, x] = jnp.where(me == 0, first_cell, low_ref[k, x])
            pad_ref[k, cx + x] = own_ref[k, x]
            pad_ref[k, 2 * cx + x] = jnp.where(me == last, last_cell, high_ref[k, x])

    def put(x, step, q, change):
        start = conserved(q)
        first = [s + TIME_STEP * c for s, c in zip(start, change)]
        q1 = primitive(first)
        for k in range(8):
            next_ref[k, step] = q1[k]

        @pl.when(jnp.logical_and(step >= 2, step < cx + 2))
        def _():
            for k in range(8):
                half_ref[k, step - 2] = 0.5 * (start[k] + first[k])

    sweep_planes(pad_ref, cx - 2, cx + 4, put)

    @pl.when(me == 0)
    def _():
        for k in range(8):
            next_ref[k, 0] = next_ref[k, 2]
            next_ref[k, 1] = next_ref[k, 2]

    @pl.when(me == last)
    def _():
        for k in range(8):
            next_ref[k, cx + 2] = next_ref[k, cx + 1]
            next_ref[k, cx + 3] = next_ref[k, cx + 1]


def stage_two(next_ref, half_ref, rho_ref, vel_ref, mag_ref, prs_ref):
    cx = half_ref.shape[1]

    def put(x, step, q, change):
        final = [half_ref[k, step] + (0.5 * TIME_STEP) * change[k] for k in range(8)]
        q2 = primitive(final)
        rho_ref[step] = q2[0]
        for k in range(3):
            vel_ref[k, step] = q2[1 + k]
            mag_ref[k, step] = q2[4 + k]
        prs_ref[step] = q2[7]

    sweep_planes(next_ref, 2, cx, put)


def pick_current(own_ref, low_ref, high_ref, cell_ref, out_ref):
    me = lax.axis_index("mag")
    last = lax.axis_size("mag") - 1
    cx, ny, nz = own_ref.shape[1:]
    rows = []
    for x in range(cx):
        bx, by, bz = (own_ref[4 + k, x] for k in range(3))

        def neighbour(k, step):
            if 0 <= x + step < cx:
                return own_ref[4 + k, x + step]
            if step < 0:
                return jnp.where(me == 0, own_ref[4 + k, x], low_ref[4 + k, cx - 1])
            return jnp.where(me == last, own_ref[4 + k, x], high_ref[4 + k, 0])

        def along_x(k):
            return 0.5 * (neighbour(k, 1) - neighbour(k, -1))

        def along(v, axis):
            return 0.5 * (pltpu.roll(v, v.shape[axis] - 1, axis) - pltpu.roll(v, 1, axis))

        jx = along(bz, 0) - along(by, 1)
        jy = along(bx, 1) - along_x(2)
        jz = along_x(1) - along(bx, 0)
        norm = jnp.sqrt(bx * bx + by * by + bz * bz + 1.0)
        rows.append(SOURCE_GAIN * (jx * bx + jy * by + jz * bz) / norm)
    table = jnp.concatenate(rows, axis=0)
    count = table.shape[0]
    both = jnp.concatenate(pieces(table), axis=0)
    cells = cell_ref[...]
    hi, lo = cells // nz, (cells % nz).astype(F32)
    index = lax.broadcasted_iota(I32, (count, LANES), 0)
    one, zero = jnp.ones((), BF16), jnp.zeros((), BF16)
    for s in range(cells.shape[0]):
        hot = jnp.where(rows_hot(lo[s : s + 1], nz), one, zero)
        found = jnp.dot(both, hot, preferred_element_type=F32)
        found = found[:count] + found[count:]
        mine = jnp.where(index == hi[s : s + 1], found, 0.0)
        out_ref[s : s + 1, :] = jnp.sum(mine, axis=0, keepdims=True)


def east_of(v):
    lane = lax.broadcasted_iota(I32, v.shape, 2)
    turned = pltpu.roll(v, v.shape[2] - 1, 2)
    return jnp.where(lane == v.shape[2] - 1, pltpu.roll(turned, v.shape[1] - 1, 1), turned)


def west_of(v):
    lane = lax.broadcasted_iota(I32, v.shape, 2)
    turned = pltpu.roll(v, 1, 2)
    return jnp.where(lane == 0, pltpu.roll(turned, 1, 1), turned)


def solve(values_ref, owner_ref, row_ref, lon_ref, own_ref, low_ref, high_ref, phi_ref, flat_ref):
    me = lax.axis_index("mag")
    devices = lax.axis_size("mag")
    lat = own_ref.shape[1]
    strips = own_ref.shape[2]
    rows = lat + 2 * RIM
    count = rows * strips
    base = me * lat - RIM
    group = 8
    one, zero = jnp.ones((), BF16), jnp.zeros((), BF16)

    def body(step, total):
        at = pl.ds(pl.multiple_of(step * group, group), group)
        owner, row, lon = owner_ref[at, :], row_ref[at, :], lon_ref[at, :]
        hi = ((owner * lat + row - base) * strips + lon // LANES).astype(F32)
        lo = (lon % LANES).astype(F32)
        value = values_ref[at, :]
        high_piece = value.astype(BF16).astype(F32)
        low_piece = value - high_piece
        lefts, rights = [], []
        for s in range(group):
            lefts.append(jnp.where(rows_hot(hi[s : s + 1], count), one, zero))
            hot = rows_hot(lo[s : s + 1], LANES)
            two = []
            for piece in (high_piece, low_piece):
                wide = jnp.broadcast_to(piece[s : s + 1], (LANES, LANES)).astype(BF16)
                two.append(jnp.where(hot, wide, zero))
            rights.append(jnp.concatenate(two, axis=0))
        left = jnp.concatenate(lefts, axis=1)
        right = jnp.concatenate(rights, axis=1)
        return total + lax.dot_general(
            left, right, (((1,), (1,)), ((), ())), preferred_element_type=F32
        )

    steps = values_ref.shape[0] // group
    total = lax.fori_loop(0, steps, body, jnp.zeros((count, 2 * LANES), F32))
    source = (total[:, :LANES] + total[:, LANES:]).reshape(rows, strips, LANES)

    zeros = jnp.zeros((1, strips, LANES), F32)
    s_own, s_low, s_high = own_ref[8], low_ref[8], high_ref[8]
    s_low = jnp.where(me == 0, 0.0, s_low)
    s_high = jnp.where(me == devices - 1, 0.0, s_high)
    wide = jnp.concatenate([s_low[lat - RIM - 1 :], s_own, s_high[: RIM + 1]], axis=0)
    s = wide[1:-1]
    north = 0.5 * (s + wide[:-2])
    south = 0.5 * (s + wide[2:])
    east = (0.5 * LON_WEIGHT) * (s + east_of(s))
    west = (0.5 * LON_WEIGHT) * (s + west_of(s))
    diagonal = north + south + east + west + LEAK_RATE * s
    row = lax.broadcasted_iota(I32, s.shape, 0) + base
    inside = jnp.logical_and(row >= 0, row < devices * lat)
    inverse = jnp.where(inside, 1.0 / diagonal, 0.0)
    phi = source * inverse
    for sweep in range(1, SWEEPS):
        keep = slice(sweep, rows - sweep)
        middle = phi[1:-1]
        phi = (
            source[keep]
            + north[keep] * phi[:-2]
            + south[keep] * phi[2:]
            + east[keep] * east_of(middle)
            + west[keep] * west_of(middle)
        ) * inverse[keep]
    phi_ref[...] = phi
    for strip in range(strips):
        flat_ref[:, strip * LANES : (strip + 1) * LANES] = phi[:, strip, :]


def read_back(phi_ref, owner_ref, row_ref, lon_ref, out_ref):
    me = lax.axis_index("mag")
    total, strips = phi_ref.shape[:2]
    devices = lax.axis_size("mag")
    lat = total // devices
    block = min(256, total * strips)
    groups = total * strips // block
    table = phi_ref[...].reshape(groups, block, LANES)
    table = jnp.concatenate([table[g] for g in range(groups)], axis=1)
    both = jnp.concatenate(pieces(table), axis=0)
    mine = out_ref.shape[0]
    at = pl.ds(pl.multiple_of(me * mine, mine), mine)
    owner, row, lon = owner_ref[at, :], row_ref[at, :], lon_ref[at, :]
    hi = (owner * lat + row) * strips + lon // LANES
    group, hi, lo = hi // block, hi % block, lon % LANES
    one, zero = jnp.ones((), BF16), jnp.zeros((), BF16)
    index = lax.broadcasted_iota(I32, (block, LANES), 0)
    columns = []
    for s in range(mine):
        stack = []
        for g in range(groups):
            key = jnp.where(group[s : s + 1] == g, lo[s : s + 1], -1).astype(F32)
            stack.append(jnp.where(rows_hot(key, LANES), one, zero))
        columns.append(jnp.concatenate(stack, axis=0))
    found = jnp.dot(both, jnp.concatenate(columns, axis=1), preferred_element_type=F32)
    found = found[:block] + found[block:]
    for s in range(mine):
        part = found[:, s * LANES : (s + 1) * LANES]
        part = jnp.where(index == hi[s : s + 1], part, 0.0)
        out_ref[s : s + 1, :] = jnp.sum(part, axis=0, keepdims=True)


def shards(
    density, velocity, mag_field, pressure, conductance, shell_cell, foot_owner, foot_row, foot_lon
):
    devices = lax.axis_size("mag")
    cx, ny, nz = density.shape
    lat, columns = conductance.shape
    strips = columns // LANES
    shell_count = shell_cell.shape[0]
    shape = jax.ShapeDtypeStruct

    own = jnp.concatenate(
        [density[None], velocity, mag_field, pressure[None], conductance.reshape(1, lat, strips, LANES)],
        axis=0,
    )
    forward = [(i, i + 1) for i in range(devices - 1)]
    low = lax.ppermute(own, "mag", forward)
    high = lax.ppermute(own, "mag", [(b, a) for a, b in forward])

    cells = shell_cell.reshape(-1, LANES)
    owner = foot_owner.reshape(-1, LANES)
    row = foot_row.reshape(-1, LANES)
    lon = foot_lon.reshape(-1, LANES)

    currents = call(pick_current, shape(cells.shape, F32))(own, low, high, cells)
    values = lax.all_gather(currents, "mag", axis=0, tiled=True)

    slab = shape((8, cx, ny, nz), F32)
    following, half = call(
        stage_one,
        [shape((8, cx + 4, ny, nz), F32), slab],
        [pltpu.VMEM((8, 3 * cx, ny, nz), F32)],
    )(own, low, high)

    phi, potential = call(
        solve, [shape((lat, strips, LANES), F32), shape((lat, columns), F32)]
    )(values, owner, row, lon, own, low, high)
    all_phi = lax.all_gather(phi, "mag", axis=0, tiled=True)

    cell_shape = shape((cx, ny, nz), F32)
    vector_shape = shape((3, cx, ny, nz), F32)
    new_density, new_velocity, new_field, new_pressure = call(
        stage_two, [cell_shape, vector_shape, vector_shape, cell_shape]
    )(following, half)

    shell_potential = call(read_back, shape((shell_count // LANES, LANES), F32))(
        all_phi, owner, row, lon
    )
    return (
        new_density,
        new_velocity,
        new_field,
        new_pressure,
        potential,
        shell_potential.reshape(shell_count),
    )


def solution(mesh):
    both = ("parts", "mag")
    in_specs = (
        P(both, None, None),
        P(None, both, None, None),
        P(None, both, None, None),
        P(both, None, None),
        P(both, None),
        P("mag"),
        P(),
        P(),
        P(),
    )
    out_specs = (
        P(both, None, None),
        P(None, both, None, None),
        P(None, both, None, None),
        P(both, None, None),
        P(both, None),
        P(both),
    )
    return jax.shard_map(shards, mesh=mesh, in_specs=in_specs, out_specs=out_specs, check_vma=False)
```

```python
import jax
import jax.numpy as jnp
from jax import lax
from jax.experimental import pallas as pl
from jax.experimental.pallas import tpu as pltpu
from jax.sharding import PartitionSpec as P

SWEEPS = 4
ADIABATIC = 5.0 / 3.0
TIME_STEP = 0.02
LON_WEIGHT = 0.25
LEAK_RATE = 0.05
SOURCE_GAIN = 10.0
LANES = 128

F32 = jnp.float32
BF16 = jnp.bfloat16
I32 = jnp.int32
VMEM = pl.BlockSpec(memory_space=pltpu.VMEM)
MIB = 1024 * 1024


def call(kernel, outs, scratch=()):
    many = isinstance(outs, (list, tuple))
    return pl.pallas_call(
        kernel,
        out_shape=outs,
        out_specs=[VMEM] * len(outs) if many else VMEM,
        scratch_shapes=list(scratch),
        compiler_params=pltpu.CompilerParams(
            vmem_limit_bytes=(32 if lax.axis_size("mag") <= 32 else 60) * MIB
        ),
    )


def pieces(values):
    first = values.astype(BF16)
    second = (values - first.astype(F32)).astype(BF16)
    return first, second


def rows_hot(key_row, count, group=256):
    lanes = key_row.shape[1]
    out = []
    for first in range(0, count, group):
        size = min(group, count - first)
        key = jnp.broadcast_to(key_row - first, (16, lanes)).astype(BF16)
        keys = jnp.concatenate([key] * (size // 16), axis=0)
        index = lax.broadcasted_iota(I32, (size, lanes), 0).astype(F32).astype(BF16)
        out.append(jnp.where(keys == index, jnp.ones((), BF16), jnp.zeros((), BF16)))
    return jnp.concatenate(out, axis=0) if len(out) > 1 else out[0]


def half_slope(lower, centre, upper):
    out = []
    for a, b, c in zip(lower, centre, upper):
        s, t = b - a, c - b
        out.append(0.5 * (jnp.maximum(jnp.minimum(s, t), 0.0) + jnp.minimum(jnp.maximum(s, t), 0.0)))
    return out


def dot3(a, b):
    return a[0] * b[0] + a[1] * b[1] + a[2] * b[2]


def conserved(q):
    rho, v, b, p = q[0], q[1:4], q[4:7], q[7]
    energy = p * (1.0 / (ADIABATIC - 1.0)) + 0.5 * rho * dot3(v, v) + 0.5 * dot3(b, b)
    return [rho, rho * v[0], rho * v[1], rho * v[2], b[0], b[1], b[2], energy]


def primitive(u):
    rho, b = u[0], u[4:7]
    inverse = 1.0 / rho
    v = [u[k] * inverse for k in (1, 2, 3)]
    p = (ADIABATIC - 1.0) * (u[7] - 0.5 * rho * dot3(v, v) - 0.5 * dot3(b, b))
    return [rho] + v + list(b) + [p]


def side(q, d):
    rho, v, b, p = q[0], q[1:4], q[4:7], q[7]
    b2 = dot3(b, b)
    half_b2 = 0.5 * b2
    total = p + half_b2
    mom = [rho * x for x in v]
    energy = p * (1.0 / (ADIABATIC - 1.0)) + 0.5 * dot3(mom, v) + half_b2
    vn, bn, mn = v[d], b[d], mom[d]
    flux = [mn]
    for k in range(3):
        f = mn * v[k] - bn * b[k]
        flux.append(f + total if k == d else f)
    for k in range(3):
        flux.append(None if k == d else vn * b[k] - bn * v[k])
    flux.append((energy + total) * vn - bn * dot3(v, b))
    speed = jnp.abs(vn) + jnp.sqrt((ADIABATIC * jnp.abs(p) + b2) / rho)
    return [rho] + mom + list(b) + [energy], flux, speed


def face(left, right, d):
    cons_l, flux_l, speed_l = side(left, d)
    cons_r, flux_r, speed_r = side(right, d)
    half_c = 0.5 * jnp.maximum(speed_l, speed_r)
    out = []
    for k in range(8):
        jump = half_c * (cons_r[k] - cons_l[k])
        out.append(-jump if flux_l[k] is None else 0.5 * (flux_l[k] + flux_r[k]) - jump)
    return out


def periodic(q, axis, d):
    size = q[0].shape[axis]
    back = [pltpu.roll(x, 1, axis) for x in q]
    ahead = [pltpu.roll(x, size - 1, axis) for x in q]
    slope = half_slope(back, q, ahead)
    left = [x + s for x, s in zip(q, slope)]
    right = [pltpu.roll(x - s, size - 1, axis) for x, s in zip(q, slope)]
    flux = face(left, right, d)
    return [pltpu.roll(f, 1, axis) - f for f in flux]


def add(a, b):
    return [x + y for x, y in zip(a, b)]


def plane(ref, x):
    return [ref[k, x] for k in range(8)]


def upper_face(ref, x):
    a, b, c, d = (plane(ref, x + k) for k in (-1, 0, 1, 2))
    left = add(b, half_slope(a, b, c))
    right = [v - s for v, s in zip(c, half_slope(b, c, d))]
    return face(left, right, 0)


def sweep_planes(ref, first, count, put):
    def body(step, below):
        x = first + step
        above = upper_face(ref, x)
        q = plane(ref, x)
        change = [f - g for f, g in zip(below, above)]
        change = add(change, periodic(q, 0, 1))
        change = add(change, periodic(q, 1, 2))
        put(x, step, q, change)
        return above

    lax.fori_loop(0, count, body, upper_face(ref, first - 1))


def stage_one(
    rho_ref, vel_ref, mag_ref, prs_ref, mag_a, mag_b, five_a, five_b, next_ref, half_ref, pad_ref
):
    me = lax.axis_index("mag")
    last = lax.axis_size("mag") - 1
    even = me % 2 == 0
    cx = rho_ref.shape[0]

    def own(k, x):
        if k == 0:
            return rho_ref[x]
        if k == 7:
            return prs_ref[x]
        return vel_ref[k - 1, x] if k < 4 else mag_ref[k - 4, x]

    def partner(k, x, mag, five):
        if 4 <= k < 7:
            return mag[k - 4, x]
        return five[min(k, 4), x]

    for k in range(8):
        for x in range(cx):
            from_a, from_b = partner(k, x, mag_a, five_a), partner(k, x, mag_b, five_b)
            low = jnp.where(even, from_b, from_a)
            high = jnp.where(even, from_a, from_b)
            pad_ref[k, x] = jnp.where(me == 0, own(k, 0), low)
            pad_ref[k, cx + x] = own(k, x)
            pad_ref[k, 2 * cx + x] = jnp.where(me == last, own(k, cx - 1), high)

    def put(x, step, q, change):
        start = conserved(q)
        first = [s + TIME_STEP * c for s, c in zip(start, change)]
        q1 = primitive(first)
        for k in range(8):
            next_ref[k, step] = q1[k]

        @pl.when(jnp.logical_and(step >= 2, step < cx + 2))
        def _():
            for k in range(8):
                half_ref[k, step - 2] = 0.5 * (start[k] + first[k])

    sweep_planes(pad_ref, cx - 2, cx + 4, put)

    @pl.when(me == 0)
    def _():
        for k in range(8):
            next_ref[k, 0] = next_ref[k, 2]
            next_ref[k, 1] = next_ref[k, 2]

    @pl.when(me == last)
    def _():
        for k in range(8):
            next_ref[k, cx + 2] = next_ref[k, cx + 1]
            next_ref[k, cx + 3] = next_ref[k, cx + 1]


def stage_two(next_ref, half_ref, rho_ref, vel_ref, mag_ref, prs_ref):
    cx = half_ref.shape[1]

    def put(x, step, q, change):
        final = [half_ref[k, step] + (0.5 * TIME_STEP) * change[k] for k in range(8)]
        q2 = primitive(final)
        rho_ref[step] = q2[0]
        for k in range(3):
            vel_ref[k, step] = q2[1 + k]
            mag_ref[k, step] = q2[4 + k]
        prs_ref[step] = q2[7]

    sweep_planes(next_ref, 2, cx, put)


def pick_current(mag_ref, mag_a, mag_b, cell_ref, cond_ref, out_ref):
    me = lax.axis_index("mag")
    last = lax.axis_size("mag") - 1
    even = me % 2 == 0
    cx, ny, nz = mag_ref.shape[1:]
    rows = []
    for x in range(cx):
        bx, by, bz = (mag_ref[k, x] for k in range(3))

        def neighbour(k, step):
            if 0 <= x + step < cx:
                return mag_ref[k, x + step]
            if step < 0:
                below = jnp.where(even, mag_b[k, cx - 1], mag_a[k, cx - 1])
                return jnp.where(me == 0, mag_ref[k, x], below)
            above = jnp.where(even, mag_a[k, 0], mag_b[k, 0])
            return jnp.where(me == last, mag_ref[k, x], above)

        def along_x(k):
            return 0.5 * (neighbour(k, 1) - neighbour(k, -1))

        def along(v, axis):
            return 0.5 * (pltpu.roll(v, v.shape[axis] - 1, axis) - pltpu.roll(v, 1, axis))

        jx = along(bz, 0) - along(by, 1)
        jy = along(bx, 1) - along_x(2)
        jz = along_x(1) - along(bx, 0)
        norm = jnp.sqrt(bx * bx + by * by + bz * bz + 1.0)
        rows.append(SOURCE_GAIN * (jx * bx + jy * by + jz * bz) / norm)
    table = jnp.concatenate(rows, axis=0)
    count = table.shape[0]
    both = jnp.concatenate(pieces(table), axis=0)
    cells = cell_ref[...]
    hi, lo = cells // nz, (cells % nz).astype(F32)
    index = lax.broadcasted_iota(I32, (count, LANES), 0)
    points = cells.shape[0]
    for s in range(points):
        hot = rows_hot(lo[s : s + 1], nz)
        found = jnp.dot(both, hot, preferred_element_type=F32)
        found = found[:count] + found[count:]
        mine = jnp.where(index == hi[s : s + 1], found, 0.0)
        out_ref[s : s + 1, :] = jnp.sum(mine, axis=0, keepdims=True)
    lat, columns = cond_ref.shape
    strips = columns // LANES
    for r in range(lat):
        for strip in range(strips):
            place = points + r * strips + strip
            out_ref[place : place + 1, :] = cond_ref[
                r : r + 1, strip * LANES : (strip + 1) * LANES
            ]


def pack_five(rho_ref, vel_ref, prs_ref, out_ref):
    out_ref[0] = rho_ref[...]
    out_ref[1:4] = vel_ref[...]
    out_ref[4] = prs_ref[...]


def east_of(v):
    lane = lax.broadcasted_iota(I32, v.shape, 2)
    turned = pltpu.roll(v, v.shape[2] - 1, 2)
    return jnp.where(lane == v.shape[2] - 1, pltpu.roll(turned, v.shape[1] - 1, 1), turned)


def west_of(v):
    lane = lax.broadcasted_iota(I32, v.shape, 2)
    turned = pltpu.roll(v, 1, 2)
    return jnp.where(lane == 0, pltpu.roll(turned, 1, 1), turned)


def scatter_block(value, hi, lo, count):
    hi, lo = hi.astype(F32), lo.astype(F32)
    high_piece = value.astype(BF16).astype(F32)
    low_piece = value - high_piece
    lefts, rights = [], []
    for s in range(value.shape[0]):
        lefts.append(rows_hot(hi[s : s + 1], count))
        hot = rows_hot(lo[s : s + 1], LANES)
        two = []
        for piece in (high_piece, low_piece):
            wide = jnp.broadcast_to(piece[s : s + 1], (16, LANES)).astype(BF16)
            two.append(hot * jnp.concatenate([wide] * (LANES // 16), axis=0))
        rights.append(jnp.concatenate(two, axis=0))
    left = jnp.concatenate(lefts, axis=1)
    right = jnp.concatenate(rights, axis=1)
    return lax.dot_general(left, right, (((1,), (1,)), ((), ())), preferred_element_type=F32)


def repeat(count, body):
    if count <= 8:
        for i in range(count):
            body(i)
    else:
        lax.fori_loop(0, count, lambda i, carry: (body(i), carry)[1], 0)


def origin(me, devices, j):
    mask, bit, k = 0, devices // 2, 0
    while bit > 1:
        mask = mask + ((j >> k) & 1) * bit
        bit, k = bit // 2, k + 1
    return jnp.bitwise_xor(me, mask)


def scatter_new(first, blocks, points, lat, strips):
    def kernel(*refs):
        *total_in, load_ref, owner_ref, row_ref, lon_ref, out_ref = refs
        me = lax.axis_index("mag")
        devices = lax.axis_size("mag")
        count = out_ref.shape[0]
        rows = min(count, 1024)
        stride = load_ref.shape[0] // blocks

        def part(j, g, base_ref):
            device = origin(me, devices, first + j)
            at = pl.ds(pl.multiple_of(device * points, points), points)
            value = load_ref[pl.ds(pl.multiple_of(j * stride, 8), points), :]
            hi = (owner_ref[at, :] * lat + row_ref[at, :]) * strips + lon_ref[at, :] // LANES
            lo = lon_ref[at, :] % LANES
            new = scatter_block(value, hi - g * rows, lo, rows)
            place = pl.ds(pl.multiple_of(g * rows, rows), rows)
            out_ref[place, :] = new if base_ref is None else base_ref[place, :] + new

        def group(g):
            part(0, g, total_in[0] if total_in else None)
            repeat(blocks - 1, lambda j: part(j + 1, g, out_ref))

        repeat(count // rows, group)

    return kernel


def scatter_last(blocks, points, lat, strips):
    def kernel(total_ref, before_ref, load_ref, owner_ref, row_ref, lon_ref, out_ref, work_ref):
        half = blocks // 2
        scatter_new(half, half, points, lat, strips)(
            total_ref, load_ref, owner_ref, row_ref, lon_ref, work_ref
        )
        count = work_ref.shape[0]
        out_ref[:count, :] = work_ref[:, :LANES] + work_ref[:, LANES:]
        cells = lat * strips
        stride = points + cells
        for j in range(blocks):
            ref = before_ref if j < half else load_ref
            start = (j % half) * stride + points
            out_ref[count + j * cells : count + (j + 1) * cells, :] = ref[start : start + cells, :]

    return kernel


def solve_and_read(blocks, points, lat, strips):
    def kernel(
        mine_ref, their_ref, owner_ref, row_ref, lon_ref, flat_ref, out_ref, s_ref, w_ref, phi_ref
    ):
        me = lax.axis_index("mag")
        devices = lax.axis_size("mag")
        rows = devices * lat
        count = rows * strips
        cells = lat * strips
        zeros = jnp.zeros((1, strips, LANES), F32)
        for ref in (s_ref, phi_ref.at[0], phi_ref.at[1]):
            ref[0:1] = zeros
            ref[rows + 1 : rows + 2] = zeros

        def place(j):
            at = pl.ds(pl.multiple_of(count + j * cells, cells), cells)
            for ref, who in ((mine_ref, me), (their_ref, jnp.bitwise_xor(me, 1))):
                device = origin(who, devices, j)
                s_ref[pl.ds(device * lat + 1, lat)] = ref[at, :].reshape(lat, strips, LANES)

        repeat(blocks, place)
        chunk = min(8, rows)

        def prepare(i):
            r = i * chunk
            s, above, below = (s_ref[pl.ds(r + k, chunk)] for k in (1, 0, 2))
            north, south = 0.5 * (s + above), 0.5 * (s + below)
            east = (0.5 * LON_WEIGHT) * (s + east_of(s))
            west = (0.5 * LON_WEIGHT) * (s + west_of(s))
            inverse = 1.0 / (north + south + east + west + LEAK_RATE * s)
            at = pl.ds(pl.multiple_of(r * strips, 8), chunk * strips)
            source = (mine_ref[at, :] + their_ref[at, :]).reshape(chunk, strips, LANES)
            for k, value in enumerate((source, north, south, east, west)):
                w_ref[k, pl.ds(r, chunk)] = value * inverse
            phi_ref[0, pl.ds(r + 1, chunk)] = source * inverse

        repeat(rows // chunk, prepare)
        for sweep in range(SWEEPS - 1):
            old, new = sweep % 2, 1 - sweep % 2

            def relax(i):
                r = i * chunk
                phi, above, below = (phi_ref[old, pl.ds(r + k, chunk)] for k in (1, 0, 2))
                source, north, south, east, west = (w_ref[k, pl.ds(r, chunk)] for k in range(5))
                phi_ref[new, pl.ds(r + 1, chunk)] = (
                    source
                    + north * above
                    + south * below
                    + east * east_of(phi)
                    + west * west_of(phi)
                )

            repeat(rows // chunk, relax)
        last = (SWEEPS - 1) % 2
        own = phi_ref[last, pl.ds(me * lat + 1, lat)]
        for strip in range(strips):
            flat_ref[:, strip * LANES : (strip + 1) * LANES] = own[:, strip, :]

        block = min(256, count)
        groups = count // block
        table = phi_ref[last, pl.ds(1, rows)].reshape(count, LANES)
        table = jnp.concatenate([table[g * block : (g + 1) * block] for g in range(groups)], axis=1)
        both = jnp.concatenate(pieces(table), axis=0)
        at = pl.ds(pl.multiple_of(me * points, points), points)
        owner, row, lon = owner_ref[at, :], row_ref[at, :], lon_ref[at, :]
        hi = (owner * lat + row) * strips + lon // LANES
        group, hi, lo = hi // block, hi % block, lon % LANES
        index = lax.broadcasted_iota(I32, (block, LANES), 0)
        columns = []
        for p in range(points):
            stack = []
            for g in range(groups):
                key = jnp.where(group[p : p + 1] == g, lo[p : p + 1], -1).astype(F32)
                stack.append(rows_hot(key, LANES))
            columns.append(jnp.concatenate(stack, axis=0))
        found = jnp.dot(both, jnp.concatenate(columns, axis=1), preferred_element_type=F32)
        found = found[:block] + found[block:]
        for p in range(points):
            part = found[:, p * LANES : (p + 1) * LANES]
            part = jnp.where(index == hi[p : p + 1], part, 0.0)
            out_ref[p : p + 1, :] = jnp.sum(part, axis=0, keepdims=True)

    return kernel


def swap(values, bit):
    devices = lax.axis_size("mag")
    return lax.ppermute(values, "mag", [(i, i ^ bit) for i in range(devices)])


def swap_next(values):
    pairs = []
    for i in range(1, lax.axis_size("mag") - 1, 2):
        pairs += [(i, i + 1), (i + 1, i)]
    return lax.ppermute(values, "mag", pairs)


def shards(
    density, velocity, mag_field, pressure, conductance, shell_cell, foot_owner, foot_row, foot_lon
):
    devices = lax.axis_size("mag")
    cx, ny, nz = density.shape
    lat, columns = conductance.shape
    strips = columns // LANES
    shell_count = shell_cell.shape[0]
    points = shell_count // LANES
    cells = lat * strips
    count = devices * cells
    shape = jax.ShapeDtypeStruct

    mag_a, mag_b = swap(mag_field, 1), swap_next(mag_field)
    five = call(pack_five, shape((5, cx, ny, nz), F32))(density, velocity, pressure)

    owner = foot_owner.reshape(-1, LANES)
    row = foot_row.reshape(-1, LANES)
    lon = foot_lon.reshape(-1, LANES)

    load = call(pick_current, shape((points + cells, LANES), F32))(
        mag_field, mag_a, mag_b, shell_cell.reshape(-1, LANES), conductance
    )
    grid = shape((count, 2 * LANES), F32)
    total, new, blocks = (), load, 1
    bit = devices // 2
    while bit > 1:
        arrived = swap(load, bit)
        size = max(1, blocks // 2)
        kernel = scatter_new(blocks - size, size, points, lat, strips)
        total = (call(kernel, grid)(*total, new, owner, row, lon),)
        before, new = load, arrived
        load = jnp.concatenate([load, arrived], axis=0)
        blocks, bit = blocks * 2, bit // 2
    grids = shape((count + count // 2, LANES), F32)
    mine = call(
        scatter_last(blocks, points, lat, strips), grids, [pltpu.VMEM((count, 2 * LANES), F32)]
    )(*total, before, new, owner, row, lon)
    theirs = swap(mine, 1)

    five_a, five_b = swap(five, 1), swap_next(five)
    slab = shape((8, cx, ny, nz), F32)
    following, half = call(
        stage_one,
        [shape((8, cx + 4, ny, nz), F32), slab],
        [pltpu.VMEM((8, 3 * cx, ny, nz), F32)],
    )(density, velocity, mag_field, pressure, mag_a, mag_b, five_a, five_b)
    cell_shape = shape((cx, ny, nz), F32)
    vector_shape = shape((3, cx, ny, nz), F32)
    new_density, new_velocity, new_field, new_pressure = call(
        stage_two, [cell_shape, vector_shape, vector_shape, cell_shape]
    )(following, half)

    potential, shell_potential = call(
        solve_and_read(blocks, points, lat, strips),
        [shape((lat, columns), F32), shape((points, LANES), F32)],
        [
            pltpu.VMEM((devices * lat + 2, strips, LANES), F32),
            pltpu.VMEM((5, devices * lat, strips, LANES), F32),
            pltpu.VMEM((2, devices * lat + 2, strips, LANES), F32),
        ],
    )(mine, theirs, owner, row, lon)
    return (
        new_density,
        new_velocity,
        new_field,
        new_pressure,
        potential,
        shell_potential.reshape(shell_count),
    )


def solution(mesh):
    both = ("parts", "mag")
    in_specs = (
        P(both, None, None),
        P(None, both, None, None),
        P(None, both, None, None),
        P(both, None, None),
        P(both, None),
        P("mag"),
        P(),
        P(),
        P(),
    )
    out_specs = (
        P(both, None, None),
        P(None, both, None, None),
        P(None, both, None, None),
        P(both, None, None),
        P(both, None),
        P(both),
    )
    return jax.shard_map(shards, mesh=mesh, in_specs=in_specs, out_specs=out_specs, check_vma=False)
```

```python
import jax
import jax.numpy as jnp
from jax import lax
from jax.experimental import pallas as pl
from jax.experimental.pallas import tpu as pltpu
from jax.sharding import PartitionSpec as P

SWEEPS = 4
ADIABATIC = 5.0 / 3.0
TIME_STEP = 0.02
LON_WEIGHT = 0.25
LEAK_RATE = 0.05
SOURCE_GAIN = 10.0
LANES = 128

F32 = jnp.float32
BF16 = jnp.bfloat16
I32 = jnp.int32
VMEM = pl.BlockSpec(memory_space=pltpu.VMEM)
ANY = pl.BlockSpec(memory_space=pl.ANY)
HBM = pl.BlockSpec(memory_space=pltpu.HBM)
MIB = 1024 * 1024


def call(kernel, outs, scratch=(), specs=None, after=()):
    many = isinstance(outs, (list, tuple))

    def body(*refs):
        kernel(*refs[len(after) :])

    def run(*operands):
        in_specs = [ANY] * len(after) + list(specs or [VMEM] * len(operands))
        return pallas(body if after else kernel, outs, many, scratch, in_specs)(*after, *operands)

    return run


def pallas(kernel, outs, many, scratch, in_specs):
    return pl.pallas_call(
        kernel,
        in_specs=in_specs,
        out_shape=outs,
        out_specs=[VMEM] * len(outs) if many else VMEM,
        scratch_shapes=list(scratch),
        compiler_params=pltpu.CompilerParams(
            vmem_limit_bytes=(32 if lax.axis_size("mag") <= 32 else 60) * MIB
        ),
    )


def pieces(values):
    first = values.astype(BF16)
    second = (values - first.astype(F32)).astype(BF16)
    return first, second


def rows_hot(key_row, count, group=256):
    lanes = key_row.shape[1]
    out = []
    for first in range(0, count, group):
        size = min(group, count - first)
        key = jnp.broadcast_to(key_row - first, (16, lanes)).astype(BF16)
        keys = jnp.concatenate([key] * (size // 16), axis=0)
        index = lax.broadcasted_iota(I32, (size, lanes), 0).astype(F32).astype(BF16)
        out.append(jnp.where(keys == index, jnp.ones((), BF16), jnp.zeros((), BF16)))
    return jnp.concatenate(out, axis=0) if len(out) > 1 else out[0]


def half_slope(lower, centre, upper):
    out = []
    for a, b, c in zip(lower, centre, upper):
        s, t = b - a, c - b
        out.append(0.5 * (jnp.maximum(jnp.minimum(s, t), 0.0) + jnp.minimum(jnp.maximum(s, t), 0.0)))
    return out


def dot3(a, b):
    return a[0] * b[0] + a[1] * b[1] + a[2] * b[2]


def conserved(q):
    rho, v, b, p = q[0], q[1:4], q[4:7], q[7]
    energy = p * (1.0 / (ADIABATIC - 1.0)) + 0.5 * rho * dot3(v, v) + 0.5 * dot3(b, b)
    return [rho, rho * v[0], rho * v[1], rho * v[2], b[0], b[1], b[2], energy]


def primitive(u):
    rho, b = u[0], u[4:7]
    inverse = 1.0 / rho
    v = [u[k] * inverse for k in (1, 2, 3)]
    p = (ADIABATIC - 1.0) * (u[7] - 0.5 * rho * dot3(v, v) - 0.5 * dot3(b, b))
    return [rho] + v + list(b) + [p]


def side(q, d):
    rho, v, b, p = q[0], q[1:4], q[4:7], q[7]
    b2 = dot3(b, b)
    half_b2 = 0.5 * b2
    total = p + half_b2
    mom = [rho * x for x in v]
    energy = p * (1.0 / (ADIABATIC - 1.0)) + 0.5 * dot3(mom, v) + half_b2
    vn, bn, mn = v[d], b[d], mom[d]
    flux = [mn]
    for k in range(3):
        f = mn * v[k] - bn * b[k]
        flux.append(f + total if k == d else f)
    for k in range(3):
        flux.append(None if k == d else vn * b[k] - bn * v[k])
    flux.append((energy + total) * vn - bn * dot3(v, b))
    speed = jnp.abs(vn) + jnp.sqrt((ADIABATIC * jnp.abs(p) + b2) / rho)
    return [rho] + mom + list(b) + [energy], flux, speed


def face(left, right, d):
    cons_l, flux_l, speed_l = side(left, d)
    cons_r, flux_r, speed_r = side(right, d)
    half_c = 0.5 * jnp.maximum(speed_l, speed_r)
    out = []
    for k in range(8):
        jump = half_c * (cons_r[k] - cons_l[k])
        out.append(-jump if flux_l[k] is None else 0.5 * (flux_l[k] + flux_r[k]) - jump)
    return out


def periodic(q, axis, d):
    size = q[0].shape[axis]
    back = [pltpu.roll(x, 1, axis) for x in q]
    ahead = [pltpu.roll(x, size - 1, axis) for x in q]
    slope = half_slope(back, q, ahead)
    left = [x + s for x, s in zip(q, slope)]
    right = [pltpu.roll(x - s, size - 1, axis) for x, s in zip(q, slope)]
    flux = face(left, right, d)
    return [pltpu.roll(f, 1, axis) - f for f in flux]


def add(a, b):
    return [x + y for x, y in zip(a, b)]


def plane(ref, x):
    return [ref[k, x] for k in range(8)]


def upper_face(ref, x):
    a, b, c, d = (plane(ref, x + k) for k in (-1, 0, 1, 2))
    left = add(b, half_slope(a, b, c))
    right = [v - s for v, s in zip(c, half_slope(b, c, d))]
    return face(left, right, 0)


def sweep_planes(ref, first, count, put):
    def body(step, below):
        x = first + step
        above = upper_face(ref, x)
        q = plane(ref, x)
        change = [f - g for f, g in zip(below, above)]
        change = add(change, periodic(q, 0, 1))
        change = add(change, periodic(q, 1, 2))
        put(x, step, q, change)
        return above

    lax.fori_loop(0, count, body, upper_face(ref, first - 1))


def stage_one(mag_ref, five_ref, mag_a, mag_b, five_a, five_b, next_ref, half_ref, pad_ref):
    me = lax.axis_index("mag")
    last = lax.axis_size("mag") - 1
    even = me % 2 == 0
    cx = mag_ref.shape[1]

    def cell(k, x, mag, five):
        if 4 <= k < 7:
            return mag[k - 4, x]
        return five[min(k, 4), x]

    def own(k, x):
        return cell(k, x, mag_ref, five_ref)

    for k in range(8):
        for x in range(cx):
            from_a, from_b = cell(k, x, mag_a, five_a), cell(k, x, mag_b, five_b)
            low = jnp.where(even, from_b, from_a)
            high = jnp.where(even, from_a, from_b)
            pad_ref[k, x] = jnp.where(me == 0, own(k, 0), low)
            pad_ref[k, cx + x] = own(k, x)
            pad_ref[k, 2 * cx + x] = jnp.where(me == last, own(k, cx - 1), high)

    def put(x, step, q, change):
        start = conserved(q)
        first = [s + TIME_STEP * c for s, c in zip(start, change)]
        q1 = primitive(first)
        for k in range(8):
            next_ref[k, step] = q1[k]

        @pl.when(jnp.logical_and(step >= 2, step < cx + 2))
        def _():
            for k in range(8):
                half_ref[k, step - 2] = 0.5 * (start[k] + first[k])

    sweep_planes(pad_ref, cx - 2, cx + 4, put)

    @pl.when(me == 0)
    def _():
        for k in range(8):
            next_ref[k, 0] = next_ref[k, 2]
            next_ref[k, 1] = next_ref[k, 2]

    @pl.when(me == last)
    def _():
        for k in range(8):
            next_ref[k, cx + 2] = next_ref[k, cx + 1]
            next_ref[k, cx + 3] = next_ref[k, cx + 1]


def stage_two(next_ref, half_ref, rho_ref, vel_ref, mag_ref, prs_ref, end_ref):
    end_ref[...] = half_ref[0, 0, 0:8]
    cx = half_ref.shape[1]

    def put(x, step, q, change):
        final = [half_ref[k, step] + (0.5 * TIME_STEP) * change[k] for k in range(8)]
        q2 = primitive(final)
        rho_ref[step] = q2[0]
        for k in range(3):
            vel_ref[k, step] = q2[1 + k]
            mag_ref[k, step] = q2[4 + k]
        prs_ref[step] = q2[7]

    sweep_planes(next_ref, 2, cx, put)


def pick_current(mag_ref, cell_ref, strip_ref, mag_a, mag_b, five_ref, out_ref, five_out):
    me = lax.axis_index("mag")
    last = lax.axis_size("mag") - 1
    even = me % 2 == 0
    cx, ny, nz = mag_ref.shape[1:]
    rows = []
    for x in range(cx):
        bx, by, bz = (mag_ref[k, x] for k in range(3))

        def neighbour(k, step):
            if 0 <= x + step < cx:
                return mag_ref[k, x + step]
            if step < 0:
                below = jnp.where(even, mag_b[k, cx - 1], mag_a[k, cx - 1])
                return jnp.where(me == 0, mag_ref[k, x], below)
            above = jnp.where(even, mag_a[k, 0], mag_b[k, 0])
            return jnp.where(me == last, mag_ref[k, x], above)

        def along_x(k):
            return 0.5 * (neighbour(k, 1) - neighbour(k, -1))

        def along(v, axis):
            return 0.5 * (pltpu.roll(v, v.shape[axis] - 1, axis) - pltpu.roll(v, 1, axis))

        jx = along(bz, 0) - along(by, 1)
        jy = along(bx, 1) - along_x(2)
        jz = along_x(1) - along(bx, 0)
        norm = jnp.sqrt(bx * bx + by * by + bz * bz + 1.0)
        rows.append(SOURCE_GAIN * (jx * bx + jy * by + jz * bz) / norm)
    table = jnp.concatenate(rows, axis=0)
    count = table.shape[0]
    both = jnp.concatenate(pieces(table), axis=0)
    cells = cell_ref[...]
    hi, lo = cells // nz, (cells % nz).astype(F32)
    index = lax.broadcasted_iota(I32, (count, LANES), 0)
    points = cells.shape[0]
    for s in range(points):
        hot = rows_hot(lo[s : s + 1], nz)
        found = jnp.dot(both, hot, preferred_element_type=F32)
        found = found[:count] + found[count:]
        mine = jnp.where(index == hi[s : s + 1], found, 0.0)
        out_ref[s : s + 1, :] = jnp.sum(mine, axis=0, keepdims=True)
    out_ref[points:, :] = strip_ref[...]
    five_out[...] = five_ref[...]


def load_arguments(
    rho_ref, vel_ref, mag_ref, prs_ref, cell_ref, cond_ref, mag_out, cell_out, strip_out, five_out, rows, sems
):
    copies = [
        pltpu.make_async_copy(source, target, sems.at[k])
        for k, (source, target) in enumerate(
            [
                (cond_ref, rows),
                (mag_ref, mag_out),
                (cell_ref, cell_out),
                (rho_ref, five_out.at[0]),
                (vel_ref, five_out.at[pl.ds(1, 3)]),
                (prs_ref, five_out.at[4]),
            ]
        )
    ]
    for copy in copies:
        copy.start()
    copies[0].wait()
    lat, columns = rows.shape
    strips = columns // LANES
    for r in range(lat):
        for strip in range(strips):
            place = r * strips + strip
            strip_out[place : place + 1, :] = rows[r : r + 1, strip * LANES : (strip + 1) * LANES]
    for copy in copies[1:]:
        copy.wait()


def east_of(v):
    lane = lax.broadcasted_iota(I32, v.shape, 2)
    turned = pltpu.roll(v, v.shape[2] - 1, 2)
    return jnp.where(lane == v.shape[2] - 1, pltpu.roll(turned, v.shape[1] - 1, 1), turned)


def west_of(v):
    lane = lax.broadcasted_iota(I32, v.shape, 2)
    turned = pltpu.roll(v, 1, 2)
    return jnp.where(lane == 0, pltpu.roll(turned, 1, 1), turned)


def scatter_block(value, hi, lo, count):
    hi, lo = hi.astype(F32), lo.astype(F32)
    high_piece = value.astype(BF16).astype(F32)
    low_piece = value - high_piece
    lefts, rights = [], []
    for s in range(value.shape[0]):
        lefts.append(rows_hot(hi[s : s + 1], count))
        hot = rows_hot(lo[s : s + 1], LANES)
        two = []
        for piece in (high_piece, low_piece):
            wide = jnp.broadcast_to(piece[s : s + 1], (16, LANES)).astype(BF16)
            two.append(hot * jnp.concatenate([wide] * (LANES // 16), axis=0))
        rights.append(jnp.concatenate(two, axis=0))
    left = jnp.concatenate(lefts, axis=1)
    right = jnp.concatenate(rights, axis=1)
    return lax.dot_general(left, right, (((1,), (1,)), ((), ())), preferred_element_type=F32)


def repeat(count, body):
    if count <= 8:
        for i in range(count):
            body(i)
    else:
        lax.fori_loop(0, count, lambda i, carry: (body(i), carry)[1], 0)


def origin(me, devices, j):
    mask, bit, k = 0, devices // 2, 0
    while bit > 1:
        mask = mask + ((j >> k) & 1) * bit
        bit, k = bit // 2, k + 1
    return jnp.bitwise_xor(me, mask)


def scatter_new(first, blocks, points, lat, strips):
    def kernel(*refs):
        *total_in, load_ref, owner_ref, row_ref, lon_ref, out_ref = refs
        me = lax.axis_index("mag")
        devices = lax.axis_size("mag")
        count = out_ref.shape[0]
        rows = min(count, 1024)
        stride = load_ref.shape[0] // blocks

        def part(j, g, base_ref):
            device = origin(me, devices, first + j)
            at = pl.ds(pl.multiple_of(device * points, points), points)
            value = load_ref[pl.ds(pl.multiple_of(j * stride, 8), points), :]
            hi = (owner_ref[at, :] * lat + row_ref[at, :]) * strips + lon_ref[at, :] // LANES
            lo = lon_ref[at, :] % LANES
            new = scatter_block(value, hi - g * rows, lo, rows)
            place = pl.ds(pl.multiple_of(g * rows, rows), rows)
            out_ref[place, :] = new if base_ref is None else base_ref[place, :] + new

        def group(g):
            part(0, g, total_in[0] if total_in else None)
            repeat(blocks - 1, lambda j: part(j + 1, g, out_ref))

        repeat(count // rows, group)

    return kernel


def handing_on(kernel, count):
    def run(*refs):
        outs = count + 1
        given = refs[-outs - count : -outs]
        for source, target in zip(given, refs[-count:]):
            target[...] = source[...]
        kernel(*refs[: -outs - count], refs[-outs])

    return run


def scatter_last(blocks, points, lat, strips):
    def kernel(total_ref, before_ref, load_ref, owner_ref, row_ref, lon_ref, out_ref, work_ref):
        half = blocks // 2
        scatter_new(half, half, points, lat, strips)(
            total_ref, load_ref, owner_ref, row_ref, lon_ref, work_ref
        )
        count = work_ref.shape[0]
        out_ref[:count, :] = work_ref[:, :LANES] + work_ref[:, LANES:]
        cells = lat * strips
        stride = points + cells
        for j in range(blocks):
            ref = before_ref if j < half else load_ref
            start = (j % half) * stride + points
            out_ref[count + j * cells : count + (j + 1) * cells, :] = ref[start : start + cells, :]

    return kernel


def solve_and_read(blocks, points, lat, strips):
    def kernel(
        mine_ref, their_ref, owner_ref, row_ref, lon_ref, flat_ref, out_ref, s_ref, w_ref, phi_ref
    ):
        me = lax.axis_index("mag")
        devices = lax.axis_size("mag")
        rows = devices * lat
        count = rows * strips
        cells = lat * strips
        zeros = jnp.zeros((1, strips, LANES), F32)
        for ref in (s_ref, phi_ref.at[0], phi_ref.at[1]):
            ref[0:1] = zeros
            ref[rows + 1 : rows + 2] = zeros

        def place(j):
            at = pl.ds(pl.multiple_of(count + j * cells, cells), cells)
            for ref, who in ((mine_ref, me), (their_ref, jnp.bitwise_xor(me, 1))):
                device = origin(who, devices, j)
                s_ref[pl.ds(device * lat + 1, lat)] = ref[at, :].reshape(lat, strips, LANES)

        repeat(blocks, place)
        chunk = min(8, rows)

        def prepare(i):
            r = i * chunk
            s, above, below = (s_ref[pl.ds(r + k, chunk)] for k in (1, 0, 2))
            north, south = 0.5 * (s + above), 0.5 * (s + below)
            east = (0.5 * LON_WEIGHT) * (s + east_of(s))
            west = (0.5 * LON_WEIGHT) * (s + west_of(s))
            inverse = 1.0 / (north + south + east + west + LEAK_RATE * s)
            at = pl.ds(pl.multiple_of(r * strips, 8), chunk * strips)
            source = (mine_ref[at, :] + their_ref[at, :]).reshape(chunk, strips, LANES)
            for k, value in enumerate((source, north, south, east, west)):
                w_ref[k, pl.ds(r, chunk)] = value * inverse
            phi_ref[0, pl.ds(r + 1, chunk)] = source * inverse

        repeat(rows // chunk, prepare)
        for sweep in range(SWEEPS - 1):
            old, new = sweep % 2, 1 - sweep % 2

            def relax(i):
                r = i * chunk
                phi, above, below = (phi_ref[old, pl.ds(r + k, chunk)] for k in (1, 0, 2))
                source, north, south, east, west = (w_ref[k, pl.ds(r, chunk)] for k in range(5))
                phi_ref[new, pl.ds(r + 1, chunk)] = (
                    source
                    + north * above
                    + south * below
                    + east * east_of(phi)
                    + west * west_of(phi)
                )

            repeat(rows // chunk, relax)
        last = (SWEEPS - 1) % 2
        own = phi_ref[last, pl.ds(me * lat + 1, lat)]
        for strip in range(strips):
            flat_ref[:, strip * LANES : (strip + 1) * LANES] = own[:, strip, :]

        block = min(256, count)
        groups = count // block
        table = phi_ref[last, pl.ds(1, rows)].reshape(count, LANES)
        table = jnp.concatenate([table[g * block : (g + 1) * block] for g in range(groups)], axis=1)
        both = jnp.concatenate(pieces(table), axis=0)
        at = pl.ds(pl.multiple_of(me * points, points), points)
        owner, row, lon = owner_ref[at, :], row_ref[at, :], lon_ref[at, :]
        hi = (owner * lat + row) * strips + lon // LANES
        group, hi, lo = hi // block, hi % block, lon % LANES
        index = lax.broadcasted_iota(I32, (block, LANES), 0)
        columns = []
        for p in range(points):
            stack = []
            for g in range(groups):
                key = jnp.where(group[p : p + 1] == g, lo[p : p + 1], -1).astype(F32)
                stack.append(rows_hot(key, LANES))
            columns.append(jnp.concatenate(stack, axis=0))
        found = jnp.dot(both, jnp.concatenate(columns, axis=1), preferred_element_type=F32)
        found = found[:block] + found[block:]
        for p in range(points):
            part = found[:, p * LANES : (p + 1) * LANES]
            part = jnp.where(index == hi[p : p + 1], part, 0.0)
            out_ref[p : p + 1, :] = jnp.sum(part, axis=0, keepdims=True)

    return kernel


def swap(values, bit):
    devices = lax.axis_size("mag")
    return lax.ppermute(values, "mag", [(i, i ^ bit) for i in range(devices)])


def swap_next(values):
    pairs = []
    for i in range(1, lax.axis_size("mag") - 1, 2):
        pairs += [(i, i + 1), (i + 1, i)]
    return lax.ppermute(values, "mag", pairs)


def shards(
    density, velocity, mag_field, pressure, conductance, shell_cell, foot_owner, foot_row, foot_lon
):
    devices = lax.axis_size("mag")
    cx, ny, nz = density.shape
    lat, columns = conductance.shape
    strips = columns // LANES
    shell_count = shell_cell.shape[0]
    points = shell_count // LANES
    cells = lat * strips
    count = devices * cells
    shape = jax.ShapeDtypeStruct

    mag_a, mag_b = swap(mag_field, 1), swap_next(mag_field)
    tile = shape((points, LANES), I32)
    mag, cell, strip, five = call(
        load_arguments,
        [shape(mag_field.shape, F32), tile, shape((cells, LANES), F32), shape((5, cx, ny, nz), F32)],
        [pltpu.VMEM((lat, columns), F32), pltpu.SemaphoreType.DMA((6,))],
        [HBM] * 6,
    )(density, velocity, mag_field, pressure, shell_cell.reshape(-1, LANES), conductance)

    owner = foot_owner.reshape(-1, LANES)
    row = foot_row.reshape(-1, LANES)
    lon = foot_lon.reshape(-1, LANES)

    load, five = call(
        pick_current, [shape((points + cells, LANES), F32), shape(five.shape, F32)]
    )(mag, cell, strip, mag_a, mag_b, five)
    five_a, five_b = swap(five, 1), swap_next(five)

    grid = shape((count, 2 * LANES), F32)
    total, blocks, done = (), 1, 0
    bit = devices // 2
    while bit > 1:
        arrived = swap(load, bit)
        if blocks > 1:
            kernel = handing_on(scatter_new(done, blocks - done, points, lat, strips), 1)
            total, load = call(kernel, [grid, shape(load.shape, F32)])(
                *total, new, owner, row, lon, load
            )
            total, done = (total,), blocks
        before, new = load, arrived
        load = jnp.concatenate([load, arrived], axis=0)
        if blocks == 1:
            new = load
        blocks, bit = blocks * 2, bit // 2

    slab = shape((8, cx, ny, nz), F32)
    following, half = call(
        stage_one,
        [shape((8, cx + 4, ny, nz), F32), slab],
        [pltpu.VMEM((8, 3 * cx, ny, nz), F32)],
    )(mag, five, mag_a, mag_b, five_a, five_b)

    grids = shape((count + count // 2, LANES), F32)
    mine = call(
        scatter_last(blocks, points, lat, strips),
        grids,
        [pltpu.VMEM((count, 2 * LANES), F32)],
        after=(half,),
    )(*total, before, new, owner, row, lon)
    theirs = swap(mine, 1)

    cell_shape = shape((cx, ny, nz), F32)
    vector_shape = shape((3, cx, ny, nz), F32)
    new_density, new_velocity, new_field, new_pressure, end = call(
        stage_two, [cell_shape, vector_shape, vector_shape, cell_shape, shape((8, LANES), F32)]
    )(following, half)

    potential, shell_potential = call(
        solve_and_read(blocks, points, lat, strips),
        [shape((lat, columns), F32), shape((points, LANES), F32)],
        [
            pltpu.VMEM((devices * lat + 2, strips, LANES), F32),
            pltpu.VMEM((5, devices * lat, strips, LANES), F32),
            pltpu.VMEM((2, devices * lat + 2, strips, LANES), F32),
        ],
        after=(end,),
    )(mine, theirs, owner, row, lon)
    return (
        new_density,
        new_velocity,
        new_field,
        new_pressure,
        potential,
        shell_potential.reshape(shell_count),
    )


def solution(mesh):
    both = ("parts", "mag")
    in_specs = (
        P(both, None, None),
        P(None, both, None, None),
        P(None, both, None, None),
        P(both, None, None),
        P(both, None),
        P("mag"),
        P(),
        P(),
        P(),
    )
    out_specs = (
        P(both, None, None),
        P(None, both, None, None),
        P(None, both, None, None),
        P(both, None, None),
        P(both, None),
        P(both),
    )
    return jax.shard_map(shards, mesh=mesh, in_specs=in_specs, out_specs=out_specs, check_vma=False)
```

```python
import jax
import jax.numpy as jnp
from jax import lax
from jax.experimental import pallas as pl
from jax.experimental.pallas import tpu as pltpu
from jax.sharding import PartitionSpec as P

SWEEPS = 4
ADIABATIC = 5.0 / 3.0
TIME_STEP = 0.02
LON_WEIGHT = 0.25
LEAK_RATE = 0.05
SOURCE_GAIN = 10.0
LANES = 128

F32 = jnp.float32
BF16 = jnp.bfloat16
I32 = jnp.int32
VMEM = pl.BlockSpec(memory_space=pltpu.VMEM)
ANY = pl.BlockSpec(memory_space=pl.ANY)
HBM = pl.BlockSpec(memory_space=pltpu.HBM)
MIB = 1024 * 1024


def call(kernel, outs, scratch=(), specs=None, after=()):
    many = isinstance(outs, (list, tuple))

    def body(*refs):
        kernel(*refs[len(after) :])

    def run(*operands):
        in_specs = [ANY] * len(after) + list(specs or [VMEM] * len(operands))
        return pallas(body if after else kernel, outs, many, scratch, in_specs)(*after, *operands)

    return run


def pallas(kernel, outs, many, scratch, in_specs):
    return pl.pallas_call(
        kernel,
        in_specs=in_specs,
        out_shape=outs,
        out_specs=[VMEM] * len(outs) if many else VMEM,
        scratch_shapes=list(scratch),
        compiler_params=pltpu.CompilerParams(
            vmem_limit_bytes=(32 if lax.axis_size("mag") <= 32 else 60) * MIB
        ),
    )


def pieces(values):
    first = values.astype(BF16)
    second = (values - first.astype(F32)).astype(BF16)
    return first, second


def rows_hot(key_row, count, group=256):
    lanes = key_row.shape[1]
    out = []
    for first in range(0, count, group):
        size = min(group, count - first)
        key = jnp.broadcast_to(key_row - first, (16, lanes)).astype(BF16)
        keys = jnp.concatenate([key] * (size // 16), axis=0)
        index = lax.broadcasted_iota(I32, (size, lanes), 0).astype(F32).astype(BF16)
        out.append(jnp.where(keys == index, jnp.ones((), BF16), jnp.zeros((), BF16)))
    return jnp.concatenate(out, axis=0) if len(out) > 1 else out[0]


def half_slope(lower, centre, upper):
    out = []
    for a, b, c in zip(lower, centre, upper):
        s, t = b - a, c - b
        out.append(0.5 * (jnp.maximum(jnp.minimum(s, t), 0.0) + jnp.minimum(jnp.maximum(s, t), 0.0)))
    return out


def dot3(a, b):
    return a[0] * b[0] + a[1] * b[1] + a[2] * b[2]


def conserved(q):
    rho, v, b, p = q[0], q[1:4], q[4:7], q[7]
    energy = p * (1.0 / (ADIABATIC - 1.0)) + 0.5 * rho * dot3(v, v) + 0.5 * dot3(b, b)
    return [rho, rho * v[0], rho * v[1], rho * v[2], b[0], b[1], b[2], energy]


def primitive(u):
    rho, b = u[0], u[4:7]
    inverse = 1.0 / rho
    v = [u[k] * inverse for k in (1, 2, 3)]
    p = (ADIABATIC - 1.0) * (u[7] - 0.5 * rho * dot3(v, v) - 0.5 * dot3(b, b))
    return [rho] + v + list(b) + [p]


def side(q, d):
    rho, v, b, p = q[0], q[1:4], q[4:7], q[7]
    b2 = dot3(b, b)
    half_b2 = 0.5 * b2
    total = p + half_b2
    mom = [rho * x for x in v]
    energy = p * (1.0 / (ADIABATIC - 1.0)) + 0.5 * dot3(mom, v) + half_b2
    vn, bn, mn = v[d], b[d], mom[d]
    flux = [mn]
    for k in range(3):
        f = mn * v[k] - bn * b[k]
        flux.append(f + total if k == d else f)
    for k in range(3):
        flux.append(None if k == d else vn * b[k] - bn * v[k])
    flux.append((energy + total) * vn - bn * dot3(v, b))
    speed = jnp.abs(vn) + jnp.sqrt((ADIABATIC * jnp.abs(p) + b2) / rho)
    return [rho] + mom + list(b) + [energy], flux, speed


def face(left, right, d):
    cons_l, flux_l, speed_l = side(left, d)
    cons_r, flux_r, speed_r = side(right, d)
    half_c = 0.5 * jnp.maximum(speed_l, speed_r)
    out = []
    for k in range(8):
        jump = half_c * (cons_r[k] - cons_l[k])
        out.append(-jump if flux_l[k] is None else 0.5 * (flux_l[k] + flux_r[k]) - jump)
    return out


def periodic(q, axis, d):
    size = q[0].shape[axis]
    back = [pltpu.roll(x, 1, axis) for x in q]
    ahead = [pltpu.roll(x, size - 1, axis) for x in q]
    slope = half_slope(back, q, ahead)
    left = [x + s for x, s in zip(q, slope)]
    right = [pltpu.roll(x - s, size - 1, axis) for x, s in zip(q, slope)]
    flux = face(left, right, d)
    return [pltpu.roll(f, 1, axis) - f for f in flux]


def add(a, b):
    return [x + y for x, y in zip(a, b)]


def plane(ref, x):
    return [ref[k, x] for k in range(8)]


def upper_face(ref, x):
    a, b, c, d = (plane(ref, x + k) for k in (-1, 0, 1, 2))
    left = add(b, half_slope(a, b, c))
    right = [v - s for v, s in zip(c, half_slope(b, c, d))]
    return face(left, right, 0)


def sideways(q):
    return add(periodic(q, 0, 1), periodic(q, 1, 2))


def sweep_planes(ref, first, count, put, others):
    def body(step, below):
        x = first + step
        above = upper_face(ref, x)
        q = plane(ref, x)
        change = [f - g for f, g in zip(below, above)]
        put(x, step, q, add(change, others(step, q)))
        return above

    lax.fori_loop(0, count, body, upper_face(ref, first - 1))


def stage_own(own_ref, side_ref):
    def body(x, carry):
        for k, value in enumerate(sideways(plane(own_ref, x))):
            side_ref[k, x] = value
        return carry

    lax.fori_loop(0, own_ref.shape[1], body, 0)


def stage_one(own_ref, eight_a, eight_b, own_side_ref, next_ref, half_ref, pad_ref, side_ref):
    me = lax.axis_index("mag")
    last = lax.axis_size("mag") - 1
    even = me % 2 == 0
    cx = own_ref.shape[1]
    for k in range(8):
        for x in range(cx):
            low = jnp.where(even, eight_b[k, x], eight_a[k, x])
            high = jnp.where(even, eight_a[k, x], eight_b[k, x])
            pad_ref[k, x] = jnp.where(me == 0, own_ref[k, 0], low)
            pad_ref[k, cx + x] = own_ref[k, x]
            pad_ref[k, 2 * cx + x] = jnp.where(me == last, own_ref[k, cx - 1], high)
            side_ref[k, 2 + x] = own_side_ref[k, x]

    def beside(i, carry):
        step = jnp.where(i < 2, i, cx + i)
        for k, value in enumerate(sideways(plane(pad_ref, cx - 2 + step))):
            side_ref[k, step] = value
        return carry

    lax.fori_loop(0, 4, beside, 0)

    def put(x, step, q, change):
        start = conserved(q)
        first = [s + TIME_STEP * c for s, c in zip(start, change)]
        q1 = primitive(first)
        for k in range(8):
            next_ref[k, step] = q1[k]

        @pl.when(jnp.logical_and(step >= 2, step < cx + 2))
        def _():
            for k in range(8):
                half_ref[k, step - 2] = 0.5 * (start[k] + first[k])

    sweep_planes(pad_ref, cx - 2, cx + 4, put, lambda step, q: plane(side_ref, step))

    @pl.when(me == 0)
    def _():
        for k in range(8):
            next_ref[k, 0] = next_ref[k, 2]
            next_ref[k, 1] = next_ref[k, 2]

    @pl.when(me == last)
    def _():
        for k in range(8):
            next_ref[k, cx + 2] = next_ref[k, cx + 1]
            next_ref[k, cx + 3] = next_ref[k, cx + 1]


def stage_two(next_ref, half_ref, rho_ref, vel_ref, mag_ref, prs_ref, end_ref):
    end_ref[...] = half_ref[0, 0, 0:8]
    cx = half_ref.shape[1]

    def put(x, step, q, change):
        final = [half_ref[k, step] + (0.5 * TIME_STEP) * change[k] for k in range(8)]
        q2 = primitive(final)
        rho_ref[step] = q2[0]
        for k in range(3):
            vel_ref[k, step] = q2[1 + k]
            mag_ref[k, step] = q2[4 + k]
        prs_ref[step] = q2[7]

    sweep_planes(next_ref, 2, cx, put, lambda step, q: sideways(q))


def pick_current(own_ref, cell_ref, strip_ref, edge_a, edge_b, out_ref, own_out):
    me = lax.axis_index("mag")
    last = lax.axis_size("mag") - 1
    even = me % 2 == 0
    cx, ny, nz = own_ref.shape[1:]
    own_out[...] = own_ref[...]
    rows = []
    for x in range(cx):
        bx, by, bz = (own_ref[4 + k, x] for k in range(3))

        def neighbour(k, step):
            if 0 <= x + step < cx:
                return own_ref[4 + k, x + step]
            if step < 0:
                below = jnp.where(even, edge_b[k - 1, 1], edge_a[k - 1, 1])
                return jnp.where(me == 0, own_ref[4 + k, x], below)
            above = jnp.where(even, edge_a[k - 1, 0], edge_b[k - 1, 0])
            return jnp.where(me == last, own_ref[4 + k, x], above)

        def along_x(k):
            return 0.5 * (neighbour(k, 1) - neighbour(k, -1))

        def along(v, axis):
            return 0.5 * (pltpu.roll(v, v.shape[axis] - 1, axis) - pltpu.roll(v, 1, axis))

        jx = along(bz, 0) - along(by, 1)
        jy = along(bx, 1) - along_x(2)
        jz = along_x(1) - along(bx, 0)
        norm = jnp.sqrt(bx * bx + by * by + bz * bz + 1.0)
        rows.append(SOURCE_GAIN * (jx * bx + jy * by + jz * bz) / norm)
    table = jnp.concatenate(rows, axis=0)
    count = table.shape[0]
    both = jnp.concatenate(pieces(table), axis=0)
    cells = cell_ref[...]
    hi, lo = cells // nz, (cells % nz).astype(F32)
    index = lax.broadcasted_iota(I32, (count, LANES), 0)
    points = cells.shape[0]
    for s in range(points):
        hot = rows_hot(lo[s : s + 1], nz)
        found = jnp.dot(both, hot, preferred_element_type=F32)
        found = found[:count] + found[count:]
        mine = jnp.where(index == hi[s : s + 1], found, 0.0)
        out_ref[s : s + 1, :] = jnp.sum(mine, axis=0, keepdims=True)
    out_ref[points:, :] = strip_ref[...]


def load_arguments(
    rho_ref, vel_ref, mag_ref, prs_ref, cell_ref, cond_ref, own_out, edge_out, cell_out, strip_out, rows, sems
):
    last = mag_ref.shape[1] - 1
    pairs = [
        (cond_ref, rows),
        (mag_ref.at[pl.ds(1, 2), pl.ds(0, 1)], edge_out.at[:, pl.ds(0, 1)]),
        (mag_ref.at[pl.ds(1, 2), pl.ds(last, 1)], edge_out.at[:, pl.ds(1, 1)]),
        (cell_ref, cell_out),
        (rho_ref, own_out.at[0]),
        (vel_ref, own_out.at[pl.ds(1, 3)]),
        (mag_ref, own_out.at[pl.ds(4, 3)]),
        (prs_ref, own_out.at[7]),
    ]
    copies = [
        pltpu.make_async_copy(source, target, sems.at[k])
        for k, (source, target) in enumerate(pairs)
    ]
    for copy in copies:
        copy.start()
    copies[0].wait()
    lat, columns = rows.shape
    strips = columns // LANES
    for r in range(lat):
        for strip in range(strips):
            place = r * strips + strip
            strip_out[place : place + 1, :] = rows[r : r + 1, strip * LANES : (strip + 1) * LANES]
    for copy in copies[1:]:
        copy.wait()


def east_of(v):
    lane = lax.broadcasted_iota(I32, v.shape, 2)
    turned = pltpu.roll(v, v.shape[2] - 1, 2)
    return jnp.where(lane == v.shape[2] - 1, pltpu.roll(turned, v.shape[1] - 1, 1), turned)


def west_of(v):
    lane = lax.broadcasted_iota(I32, v.shape, 2)
    turned = pltpu.roll(v, 1, 2)
    return jnp.where(lane == 0, pltpu.roll(turned, 1, 1), turned)


def scatter_block(value, hi, lo, count):
    hi, lo = hi.astype(F32), lo.astype(F32)
    high_piece = value.astype(BF16).astype(F32)
    low_piece = value - high_piece
    lefts, rights = [], []
    for s in range(value.shape[0]):
        lefts.append(rows_hot(hi[s : s + 1], count))
        hot = rows_hot(lo[s : s + 1], LANES)
        two = []
        for piece in (high_piece, low_piece):
            wide = jnp.broadcast_to(piece[s : s + 1], (16, LANES)).astype(BF16)
            two.append(hot * jnp.concatenate([wide] * (LANES // 16), axis=0))
        rights.append(jnp.concatenate(two, axis=0))
    left = jnp.concatenate(lefts, axis=1)
    right = jnp.concatenate(rights, axis=1)
    return lax.dot_general(left, right, (((1,), (1,)), ((), ())), preferred_element_type=F32)


def repeat(count, body):
    if count <= 8:
        for i in range(count):
            body(i)
    else:
        lax.fori_loop(0, count, lambda i, carry: (body(i), carry)[1], 0)


def origin(me, devices, j):
    mask, bit, k = 0, devices // 2, 0
    while bit > 1:
        mask = mask + ((j >> k) & 1) * bit
        bit, k = bit // 2, k + 1
    return jnp.bitwise_xor(me, mask)


def scatter_new(first, blocks, points, lat, strips):
    def kernel(*refs):
        *total_in, load_ref, owner_ref, row_ref, lon_ref, out_ref = refs
        me = lax.axis_index("mag")
        devices = lax.axis_size("mag")
        count = out_ref.shape[0]
        rows = min(count, 1024)
        stride = load_ref.shape[0] // blocks

        def part(j, g, base_ref):
            device = origin(me, devices, first + j)
            at = pl.ds(pl.multiple_of(device * points, points), points)
            value = load_ref[pl.ds(pl.multiple_of(j * stride, 8), points), :]
            hi = (owner_ref[at, :] * lat + row_ref[at, :]) * strips + lon_ref[at, :] // LANES
            lo = lon_ref[at, :] % LANES
            new = scatter_block(value, hi - g * rows, lo, rows)
            place = pl.ds(pl.multiple_of(g * rows, rows), rows)
            out_ref[place, :] = new if base_ref is None else base_ref[place, :] + new

        def group(g):
            part(0, g, total_in[0] if total_in else None)
            repeat(blocks - 1, lambda j: part(j + 1, g, out_ref))

        repeat(count // rows, group)

    return kernel


def handing_on(kernel, count):
    def run(*refs):
        outs = count + 1
        given = refs[-outs - count : -outs]
        for source, target in zip(given, refs[-count:]):
            target[...] = source[...]
        kernel(*refs[: -outs - count], refs[-outs])

    return run


def scatter_last(blocks, points, lat, strips):
    def kernel(total_ref, before_ref, load_ref, owner_ref, row_ref, lon_ref, out_ref, work_ref):
        half = blocks // 2
        scatter_new(half, half, points, lat, strips)(
            total_ref, load_ref, owner_ref, row_ref, lon_ref, work_ref
        )
        count = work_ref.shape[0]
        out_ref[:count, :] = work_ref[:, :LANES] + work_ref[:, LANES:]
        cells = lat * strips
        stride = points + cells
        for j in range(blocks):
            ref = before_ref if j < half else load_ref
            start = (j % half) * stride + points
            out_ref[count + j * cells : count + (j + 1) * cells, :] = ref[start : start + cells, :]

    return kernel


def solve_and_read(blocks, points, lat, strips):
    def kernel(
        mine_ref, their_ref, owner_ref, row_ref, lon_ref, flat_ref, out_ref, s_ref, w_ref, phi_ref
    ):
        me = lax.axis_index("mag")
        devices = lax.axis_size("mag")
        rows = devices * lat
        count = rows * strips
        cells = lat * strips
        zeros = jnp.zeros((1, strips, LANES), F32)
        for ref in (s_ref, phi_ref.at[0], phi_ref.at[1]):
            ref[0:1] = zeros
            ref[rows + 1 : rows + 2] = zeros

        def place(j):
            at = pl.ds(pl.multiple_of(count + j * cells, cells), cells)
            for ref, who in ((mine_ref, me), (their_ref, jnp.bitwise_xor(me, 1))):
                device = origin(who, devices, j)
                s_ref[pl.ds(device * lat + 1, lat)] = ref[at, :].reshape(lat, strips, LANES)

        repeat(blocks, place)
        chunk = min(8, rows)

        def prepare(i):
            r = i * chunk
            s, above, below = (s_ref[pl.ds(r + k, chunk)] for k in (1, 0, 2))
            north, south = 0.5 * (s + above), 0.5 * (s + below)
            east = (0.5 * LON_WEIGHT) * (s + east_of(s))
            west = (0.5 * LON_WEIGHT) * (s + west_of(s))
            inverse = 1.0 / (north + south + east + west + LEAK_RATE * s)
            at = pl.ds(pl.multiple_of(r * strips, 8), chunk * strips)
            source = (mine_ref[at, :] + their_ref[at, :]).reshape(chunk, strips, LANES)
            for k, value in enumerate((source, north, south, east, west)):
                w_ref[k, pl.ds(r, chunk)] = value * inverse
            phi_ref[0, pl.ds(r + 1, chunk)] = source * inverse

        repeat(rows // chunk, prepare)
        for sweep in range(SWEEPS - 1):
            old, new = sweep % 2, 1 - sweep % 2

            def relax(i):
                r = i * chunk
                phi, above, below = (phi_ref[old, pl.ds(r + k, chunk)] for k in (1, 0, 2))
                source, north, south, east, west = (w_ref[k, pl.ds(r, chunk)] for k in range(5))
                phi_ref[new, pl.ds(r + 1, chunk)] = (
                    source
                    + north * above
                    + south * below
                    + east * east_of(phi)
                    + west * west_of(phi)
                )

            repeat(rows // chunk, relax)
        last = (SWEEPS - 1) % 2
        own = phi_ref[last, pl.ds(me * lat + 1, lat)]
        for strip in range(strips):
            flat_ref[:, strip * LANES : (strip + 1) * LANES] = own[:, strip, :]

        block = min(256, count)
        groups = count // block
        table = phi_ref[last, pl.ds(1, rows)].reshape(count, LANES)
        table = jnp.concatenate([table[g * block : (g + 1) * block] for g in range(groups)], axis=1)
        both = jnp.concatenate(pieces(table), axis=0)
        at = pl.ds(pl.multiple_of(me * points, points), points)
        owner, row, lon = owner_ref[at, :], row_ref[at, :], lon_ref[at, :]
        hi = (owner * lat + row) * strips + lon // LANES
        group, hi, lo = hi // block, hi % block, lon % LANES
        index = lax.broadcasted_iota(I32, (block, LANES), 0)
        columns = []
        for p in range(points):
            stack = []
            for g in range(groups):
                key = jnp.where(group[p : p + 1] == g, lo[p : p + 1], -1).astype(F32)
                stack.append(rows_hot(key, LANES))
            columns.append(jnp.concatenate(stack, axis=0))
        found = jnp.dot(both, jnp.concatenate(columns, axis=1), preferred_element_type=F32)
        found = found[:block] + found[block:]
        for p in range(points):
            part = found[:, p * LANES : (p + 1) * LANES]
            part = jnp.where(index == hi[p : p + 1], part, 0.0)
            out_ref[p : p + 1, :] = jnp.sum(part, axis=0, keepdims=True)

    return kernel


def swap(values, bit):
    devices = lax.axis_size("mag")
    return lax.ppermute(values, "mag", [(i, i ^ bit) for i in range(devices)])


def swap_next(values):
    pairs = []
    for i in range(1, lax.axis_size("mag") - 1, 2):
        pairs += [(i, i + 1), (i + 1, i)]
    return lax.ppermute(values, "mag", pairs)


def shards(
    density, velocity, mag_field, pressure, conductance, shell_cell, foot_owner, foot_row, foot_lon
):
    devices = lax.axis_size("mag")
    cx, ny, nz = density.shape
    lat, columns = conductance.shape
    strips = columns // LANES
    shell_count = shell_cell.shape[0]
    points = shell_count // LANES
    cells = lat * strips
    count = devices * cells
    shape = jax.ShapeDtypeStruct

    tile = shape((points, LANES), I32)
    slab = shape((8, cx, ny, nz), F32)
    own, edge, cell, strip = call(
        load_arguments,
        [slab, shape((2, 2, ny, nz), F32), tile, shape((cells, LANES), F32)],
        [pltpu.VMEM((lat, columns), F32), pltpu.SemaphoreType.DMA((8,))],
        [HBM] * 6,
    )(
        *(
            pltpu.with_memory_space_constraint(x, pltpu.HBM)
            for x in (
                density,
                velocity,
                mag_field,
                pressure,
                shell_cell.reshape(-1, LANES),
                conductance,
            )
        )
    )
    edge_a, edge_b = swap(edge, 1), swap_next(edge)
    own_side = call(stage_own, slab)(own)

    owner = foot_owner.reshape(-1, LANES)
    row = foot_row.reshape(-1, LANES)
    lon = foot_lon.reshape(-1, LANES)

    load, own = call(
        pick_current, [shape((points + cells, LANES), F32), slab], after=(own_side,)
    )(own, cell, strip, edge_a, edge_b)
    eight_a, eight_b = swap(own, 1), swap_next(own)

    grid = shape((count, 2 * LANES), F32)
    total, blocks, done = (), 1, 0
    bit = devices // 2
    while bit > 1:
        arrived = swap(load, bit)
        if blocks > 1:
            kernel = handing_on(scatter_new(done, blocks - done, points, lat, strips), 1)
            total, load = call(kernel, [grid, shape(load.shape, F32)])(
                *total, new, owner, row, lon, load
            )
            total, done = (total,), blocks
        before, new = load, arrived
        load = jnp.concatenate([load, arrived], axis=0)
        if blocks == 1:
            new = load
        blocks, bit = blocks * 2, bit // 2

    following, half = call(
        stage_one,
        [shape((8, cx + 4, ny, nz), F32), slab],
        [pltpu.VMEM((8, 3 * cx, ny, nz), F32), pltpu.VMEM((8, cx + 4, ny, nz), F32)],
    )(own, eight_a, eight_b, own_side)

    grids = shape((count + count // 2, LANES), F32)
    mine = call(
        scatter_last(blocks, points, lat, strips),
        grids,
        [pltpu.VMEM((count, 2 * LANES), F32)],
        after=(half,),
    )(*total, before, new, owner, row, lon)
    theirs = swap(mine, 1)

    cell_shape = shape((cx, ny, nz), F32)
    vector_shape = shape((3, cx, ny, nz), F32)
    new_density, new_velocity, new_field, new_pressure, end = call(
        stage_two, [cell_shape, vector_shape, vector_shape, cell_shape, shape((8, LANES), F32)]
    )(following, half)

    potential, shell_potential = call(
        solve_and_read(blocks, points, lat, strips),
        [shape((lat, columns), F32), shape((points, LANES), F32)],
        [
            pltpu.VMEM((devices * lat + 2, strips, LANES), F32),
            pltpu.VMEM((5, devices * lat, strips, LANES), F32),
            pltpu.VMEM((2, devices * lat + 2, strips, LANES), F32),
        ],
        after=(end,),
    )(mine, theirs, owner, row, lon)
    return (
        new_density,
        new_velocity,
        new_field,
        new_pressure,
        potential,
        shell_potential.reshape(shell_count),
    )


def solution(mesh):
    both = ("parts", "mag")
    in_specs = (
        P(both, None, None),
        P(None, both, None, None),
        P(None, both, None, None),
        P(both, None, None),
        P(both, None),
        P("mag"),
        P(),
        P(),
        P(),
    )
    out_specs = (
        P(both, None, None),
        P(None, both, None, None),
        P(None, both, None, None),
        P(both, None, None),
        P(both, None),
        P(both),
    )
    return jax.shard_map(shards, mesh=mesh, in_specs=in_specs, out_specs=out_specs, check_vma=False)
```

```python
import jax
import jax.numpy as jnp
from jax import lax
from jax.experimental import pallas as pl
from jax.experimental.pallas import tpu as pltpu
from jax.sharding import PartitionSpec as P

SWEEPS = 4
ADIABATIC = 5.0 / 3.0
TIME_STEP = 0.02
LON_WEIGHT = 0.25
LEAK_RATE = 0.05
SOURCE_GAIN = 10.0
LANES = 128

F32 = jnp.float32
BF16 = jnp.bfloat16
I32 = jnp.int32
VMEM = pl.BlockSpec(memory_space=pltpu.VMEM)
ANY = pl.BlockSpec(memory_space=pl.ANY)
HBM = pl.BlockSpec(memory_space=pltpu.HBM)
MIB = 1024 * 1024


def call(kernel, outs, scratch=(), specs=None, after=()):
    many = isinstance(outs, (list, tuple))

    def body(*refs):
        kernel(*refs[len(after) :])

    def run(*operands):
        in_specs = [ANY] * len(after) + list(specs or [VMEM] * len(operands))
        return pallas(body if after else kernel, outs, many, scratch, in_specs)(*after, *operands)

    return run


def pallas(kernel, outs, many, scratch, in_specs):
    return pl.pallas_call(
        kernel,
        in_specs=in_specs,
        out_shape=outs,
        out_specs=[VMEM] * len(outs) if many else VMEM,
        scratch_shapes=list(scratch),
        compiler_params=pltpu.CompilerParams(
            vmem_limit_bytes=(32 if lax.axis_size("mag") <= 32 else 60) * MIB
        ),
    )


def pieces(values):
    first = values.astype(BF16)
    second = (values - first.astype(F32)).astype(BF16)
    return first, second


def rows_hot(key_row, count, group=256):
    lanes = key_row.shape[1]
    out = []
    for first in range(0, count, group):
        size = min(group, count - first)
        key = jnp.broadcast_to(key_row - first, (16, lanes)).astype(BF16)
        keys = jnp.concatenate([key] * (size // 16), axis=0)
        index = lax.broadcasted_iota(I32, (size, lanes), 0).astype(F32).astype(BF16)
        out.append(jnp.where(keys == index, jnp.ones((), BF16), jnp.zeros((), BF16)))
    return jnp.concatenate(out, axis=0) if len(out) > 1 else out[0]


def half_slope(lower, centre, upper):
    out = []
    for a, b, c in zip(lower, centre, upper):
        s, t = b - a, c - b
        out.append(0.5 * (jnp.maximum(jnp.minimum(s, t), 0.0) + jnp.minimum(jnp.maximum(s, t), 0.0)))
    return out


def dot3(a, b):
    return a[0] * b[0] + a[1] * b[1] + a[2] * b[2]


def conserved(q):
    rho, v, b, p = q[0], q[1:4], q[4:7], q[7]
    energy = p * (1.0 / (ADIABATIC - 1.0)) + 0.5 * rho * dot3(v, v) + 0.5 * dot3(b, b)
    return [rho, rho * v[0], rho * v[1], rho * v[2], b[0], b[1], b[2], energy]


def primitive(u):
    rho, b = u[0], u[4:7]
    inverse = 1.0 / rho
    v = [u[k] * inverse for k in (1, 2, 3)]
    p = (ADIABATIC - 1.0) * (u[7] - 0.5 * rho * dot3(v, v) - 0.5 * dot3(b, b))
    return [rho] + v + list(b) + [p]


def side(q, d):
    rho, v, b, p = q[0], q[1:4], q[4:7], q[7]
    b2 = dot3(b, b)
    half_b2 = 0.5 * b2
    total = p + half_b2
    mom = [rho * x for x in v]
    energy = p * (1.0 / (ADIABATIC - 1.0)) + 0.5 * dot3(mom, v) + half_b2
    vn, bn, mn = v[d], b[d], mom[d]
    flux = [mn]
    for k in range(3):
        f = mn * v[k] - bn * b[k]
        flux.append(f + total if k == d else f)
    for k in range(3):
        flux.append(None if k == d else vn * b[k] - bn * v[k])
    flux.append((energy + total) * vn - bn * dot3(v, b))
    speed = jnp.abs(vn) + jnp.sqrt((ADIABATIC * jnp.abs(p) + b2) / rho)
    return [rho] + mom + list(b) + [energy], flux, speed


def face(left, right, d):
    cons_l, flux_l, speed_l = side(left, d)
    cons_r, flux_r, speed_r = side(right, d)
    half_c = 0.5 * jnp.maximum(speed_l, speed_r)
    out = []
    for k in range(8):
        jump = half_c * (cons_r[k] - cons_l[k])
        out.append(-jump if flux_l[k] is None else 0.5 * (flux_l[k] + flux_r[k]) - jump)
    return out


def periodic(q, axis, d):
    size = q[0].shape[axis]
    back = [pltpu.roll(x, 1, axis) for x in q]
    ahead = [pltpu.roll(x, size - 1, axis) for x in q]
    slope = half_slope(back, q, ahead)
    left = [x + s for x, s in zip(q, slope)]
    right = [pltpu.roll(x - s, size - 1, axis) for x, s in zip(q, slope)]
    flux = face(left, right, d)
    return [pltpu.roll(f, 1, axis) - f for f in flux]


def add(a, b):
    return [x + y for x, y in zip(a, b)]


def plane(ref, x):
    return [ref[k, x] for k in range(8)]


def upper_face(ref, x):
    a, b, c, d = (plane(ref, x + k) for k in (-1, 0, 1, 2))
    left = add(b, half_slope(a, b, c))
    right = [v - s for v, s in zip(c, half_slope(b, c, d))]
    return face(left, right, 0)


def sideways(q):
    return add(periodic(q, 0, 1), periodic(q, 1, 2))


def sweep_planes(ref, first, count, put, others):
    def body(step, below):
        x = first + step
        above = upper_face(ref, x)
        q = plane(ref, x)
        change = [f - g for f, g in zip(below, above)]
        put(x, step, q, add(change, others(step, q)))
        return above

    lax.fori_loop(0, count, body, upper_face(ref, first - 1))


def stage_own(own_ref, side_ref):
    def body(x, carry):
        for k, value in enumerate(sideways(plane(own_ref, x))):
            side_ref[k, x] = value
        return carry

    lax.fori_loop(0, own_ref.shape[1], body, 0)


def stage_one(own_ref, eight_a, eight_b, own_side_ref, next_ref, half_ref, pad_ref, side_ref):
    me = lax.axis_index("mag")
    last = lax.axis_size("mag") - 1
    even = me % 2 == 0
    cx = own_ref.shape[1]
    for k in range(8):
        for x in range(cx):
            low = jnp.where(even, eight_b[k, x], eight_a[k, x])
            high = jnp.where(even, eight_a[k, x], eight_b[k, x])
            pad_ref[k, x] = jnp.where(me == 0, own_ref[k, 0], low)
            pad_ref[k, cx + x] = own_ref[k, x]
            pad_ref[k, 2 * cx + x] = jnp.where(me == last, own_ref[k, cx - 1], high)
            side_ref[k, 2 + x] = own_side_ref[k, x]

    def beside(i, carry):
        step = jnp.where(i < 2, i, cx + i)
        for k, value in enumerate(sideways(plane(pad_ref, cx - 2 + step))):
            side_ref[k, step] = value
        return carry

    lax.fori_loop(0, 4, beside, 0)

    def put(x, step, q, change):
        start = conserved(q)
        first = [s + TIME_STEP * c for s, c in zip(start, change)]
        q1 = primitive(first)
        for k in range(8):
            next_ref[k, step] = q1[k]

        @pl.when(jnp.logical_and(step >= 2, step < cx + 2))
        def _():
            for k in range(8):
                half_ref[k, step - 2] = 0.5 * (start[k] + first[k])

    sweep_planes(pad_ref, cx - 2, cx + 4, put, lambda step, q: plane(side_ref, step))

    @pl.when(me == 0)
    def _():
        for k in range(8):
            next_ref[k, 0] = next_ref[k, 2]
            next_ref[k, 1] = next_ref[k, 2]

    @pl.when(me == last)
    def _():
        for k in range(8):
            next_ref[k, cx + 2] = next_ref[k, cx + 1]
            next_ref[k, cx + 3] = next_ref[k, cx + 1]


def stage_two(next_ref, half_ref, rho_ref, vel_ref, mag_ref, prs_ref, end_ref):
    end_ref[...] = half_ref[0, 0, 0:8]
    cx = half_ref.shape[1]

    def put(x, step, q, change):
        final = [half_ref[k, step] + (0.5 * TIME_STEP) * change[k] for k in range(8)]
        q2 = primitive(final)
        rho_ref[step] = q2[0]
        for k in range(3):
            vel_ref[k, step] = q2[1 + k]
            mag_ref[k, step] = q2[4 + k]
        prs_ref[step] = q2[7]

    sweep_planes(next_ref, 2, cx, put, lambda step, q: sideways(q))


def pick_current(own_ref, cell_ref, strip_ref, edge_a, edge_b, out_ref, own_out):
    me = lax.axis_index("mag")
    last = lax.axis_size("mag") - 1
    even = me % 2 == 0
    cx, ny, nz = own_ref.shape[1:]
    own_out[...] = own_ref[...]
    rows = []
    for x in range(cx):
        bx, by, bz = (own_ref[4 + k, x] for k in range(3))

        def neighbour(k, step):
            if 0 <= x + step < cx:
                return own_ref[4 + k, x + step]
            if step < 0:
                below = jnp.where(even, edge_b[k - 1, 1], edge_a[k - 1, 1])
                return jnp.where(me == 0, own_ref[4 + k, x], below)
            above = jnp.where(even, edge_a[k - 1, 0], edge_b[k - 1, 0])
            return jnp.where(me == last, own_ref[4 + k, x], above)

        def along_x(k):
            return 0.5 * (neighbour(k, 1) - neighbour(k, -1))

        def along(v, axis):
            return 0.5 * (pltpu.roll(v, v.shape[axis] - 1, axis) - pltpu.roll(v, 1, axis))

        jx = along(bz, 0) - along(by, 1)
        jy = along(bx, 1) - along_x(2)
        jz = along_x(1) - along(bx, 0)
        norm = jnp.sqrt(bx * bx + by * by + bz * bz + 1.0)
        rows.append(SOURCE_GAIN * (jx * bx + jy * by + jz * bz) / norm)
    table = jnp.concatenate(rows, axis=0)
    count = table.shape[0]
    both = jnp.concatenate(pieces(table), axis=0)
    cells = cell_ref[...]
    hi, lo = cells // nz, (cells % nz).astype(F32)
    index = lax.broadcasted_iota(I32, (count, LANES), 0)
    points = cells.shape[0]
    for s in range(points):
        hot = rows_hot(lo[s : s + 1], nz)
        found = jnp.dot(both, hot, preferred_element_type=F32)
        found = found[:count] + found[count:]
        mine = jnp.where(index == hi[s : s + 1], found, 0.0)
        out_ref[s : s + 1, :] = jnp.sum(mine, axis=0, keepdims=True)
    out_ref[points:, :] = strip_ref[...]


def load_arguments(
    rho_ref, vel_ref, mag_ref, prs_ref, cell_ref, cond_ref, own_out, edge_out, cell_out, strip_out, rows, sems
):
    last = mag_ref.shape[1] - 1
    pairs = [
        (cond_ref, rows),
        (mag_ref.at[pl.ds(1, 2), pl.ds(0, 1)], edge_out.at[:, pl.ds(0, 1)]),
        (mag_ref.at[pl.ds(1, 2), pl.ds(last, 1)], edge_out.at[:, pl.ds(1, 1)]),
        (cell_ref, cell_out),
        (rho_ref, own_out.at[0]),
        (vel_ref, own_out.at[pl.ds(1, 3)]),
        (mag_ref, own_out.at[pl.ds(4, 3)]),
        (prs_ref, own_out.at[7]),
    ]
    copies = [
        pltpu.make_async_copy(source, target, sems.at[k])
        for k, (source, target) in enumerate(pairs)
    ]
    for copy in copies:
        copy.start()
    copies[0].wait()
    lat, columns = rows.shape
    strips = columns // LANES
    for r in range(lat):
        for strip in range(strips):
            place = r * strips + strip
            strip_out[place : place + 1, :] = rows[r : r + 1, strip * LANES : (strip + 1) * LANES]
    for copy in copies[1:]:
        copy.wait()


def east_of(v):
    lane = lax.broadcasted_iota(I32, v.shape, 2)
    turned = pltpu.roll(v, v.shape[2] - 1, 2)
    return jnp.where(lane == v.shape[2] - 1, pltpu.roll(turned, v.shape[1] - 1, 1), turned)


def west_of(v):
    lane = lax.broadcasted_iota(I32, v.shape, 2)
    turned = pltpu.roll(v, 1, 2)
    return jnp.where(lane == 0, pltpu.roll(turned, 1, 1), turned)


def scatter_block(value, hi, lo, count):
    hi, lo = hi.astype(F32), lo.astype(F32)
    high_piece = value.astype(BF16).astype(F32)
    low_piece = value - high_piece
    lefts, rights = [], []
    for s in range(value.shape[0]):
        lefts.append(rows_hot(hi[s : s + 1], count))
        hot = rows_hot(lo[s : s + 1], LANES)
        two = []
        for piece in (high_piece, low_piece):
            wide = jnp.broadcast_to(piece[s : s + 1], (16, LANES)).astype(BF16)
            two.append(hot * jnp.concatenate([wide] * (LANES // 16), axis=0))
        rights.append(jnp.concatenate(two, axis=0))
    left = jnp.concatenate(lefts, axis=1)
    right = jnp.concatenate(rights, axis=1)
    return lax.dot_general(left, right, (((1,), (1,)), ((), ())), preferred_element_type=F32)


def repeat(count, body):
    if count <= 8:
        for i in range(count):
            body(i)
    else:
        lax.fori_loop(0, count, lambda i, carry: (body(i), carry)[1], 0)


def origin(me, devices, j):
    mask, bit, k = 0, devices // 2, 0
    while bit > 1:
        mask = mask + ((j >> k) & 1) * bit
        bit, k = bit // 2, k + 1
    return jnp.bitwise_xor(me, mask)


def scatter_new(first, blocks, points, lat, strips):
    def kernel(*refs):
        *total_in, load_ref, owner_ref, row_ref, lon_ref, out_ref = refs
        me = lax.axis_index("mag")
        devices = lax.axis_size("mag")
        count = out_ref.shape[0]
        rows = min(count, 1024)
        stride = load_ref.shape[0] // blocks

        def part(j, g, base_ref):
            device = origin(me, devices, first + j)
            at = pl.ds(pl.multiple_of(device * points, points), points)
            value = load_ref[pl.ds(pl.multiple_of(j * stride, 8), points), :]
            hi = (owner_ref[at, :] * lat + row_ref[at, :]) * strips + lon_ref[at, :] // LANES
            lo = lon_ref[at, :] % LANES
            new = scatter_block(value, hi - g * rows, lo, rows)
            place = pl.ds(pl.multiple_of(g * rows, rows), rows)
            out_ref[place, :] = new if base_ref is None else base_ref[place, :] + new

        def group(g):
            part(0, g, total_in[0] if total_in else None)
            repeat(blocks - 1, lambda j: part(j + 1, g, out_ref))

        repeat(count // rows, group)

    return kernel


def handing_on(kernel, count):
    def run(*refs):
        outs = count + 1
        given = refs[-outs - count : -outs]
        for source, target in zip(given, refs[-count:]):
            target[...] = source[...]
        kernel(*refs[: -outs - count], refs[-outs])

    return run


def scatter_last(blocks, points, lat, strips):
    def kernel(total_ref, before_ref, load_ref, owner_ref, row_ref, lon_ref, out_ref, work_ref):
        half = blocks // 2
        scatter_new(half, half, points, lat, strips)(
            total_ref, load_ref, owner_ref, row_ref, lon_ref, work_ref
        )
        count = work_ref.shape[0]
        out_ref[:count, :] = work_ref[:, :LANES] + work_ref[:, LANES:]
        cells = lat * strips
        stride = points + cells
        for j in range(blocks):
            ref = before_ref if j < half else load_ref
            start = (j % half) * stride + points
            out_ref[count + j * cells : count + (j + 1) * cells, :] = ref[start : start + cells, :]

    return kernel


def solve_and_read(blocks, points, lat, strips):
    def kernel(
        mine_ref, their_ref, owner_ref, row_ref, lon_ref, flat_ref, out_ref, s_ref, w_ref, phi_ref
    ):
        me = lax.axis_index("mag")
        devices = lax.axis_size("mag")
        rows = devices * lat
        count = rows * strips
        cells = lat * strips
        zeros = jnp.zeros((1, strips, LANES), F32)
        for ref in (s_ref, phi_ref.at[0], phi_ref.at[1]):
            ref[0:1] = zeros
            ref[rows + 1 : rows + 2] = zeros

        def place(j):
            at = pl.ds(pl.multiple_of(count + j * cells, cells), cells)
            for ref, who in ((mine_ref, me), (their_ref, jnp.bitwise_xor(me, 1))):
                device = origin(who, devices, j)
                s_ref[pl.ds(device * lat + 1, lat)] = ref[at, :].reshape(lat, strips, LANES)

        repeat(blocks, place)
        chunk = min(8, rows)

        def prepare(i):
            r = i * chunk
            s, above, below = (s_ref[pl.ds(r + k, chunk)] for k in (1, 0, 2))
            north, south = 0.5 * (s + above), 0.5 * (s + below)
            east = (0.5 * LON_WEIGHT) * (s + east_of(s))
            west = (0.5 * LON_WEIGHT) * (s + west_of(s))
            inverse = 1.0 / (north + south + east + west + LEAK_RATE * s)
            at = pl.ds(pl.multiple_of(r * strips, 8), chunk * strips)
            source = (mine_ref[at, :] + their_ref[at, :]).reshape(chunk, strips, LANES)
            for k, value in enumerate((source, north, south, east, west)):
                w_ref[k, pl.ds(r, chunk)] = value * inverse
            phi_ref[0, pl.ds(r + 1, chunk)] = source * inverse

        repeat(rows // chunk, prepare)
        for sweep in range(SWEEPS - 1):
            old, new = sweep % 2, 1 - sweep % 2

            def relax(i):
                r = i * chunk
                phi, above, below = (phi_ref[old, pl.ds(r + k, chunk)] for k in (1, 0, 2))
                source, north, south, east, west = (w_ref[k, pl.ds(r, chunk)] for k in range(5))
                phi_ref[new, pl.ds(r + 1, chunk)] = (
                    source
                    + north * above
                    + south * below
                    + east * east_of(phi)
                    + west * west_of(phi)
                )

            repeat(rows // chunk, relax)
        last = (SWEEPS - 1) % 2
        own = phi_ref[last, pl.ds(me * lat + 1, lat)]
        for strip in range(strips):
            flat_ref[:, strip * LANES : (strip + 1) * LANES] = own[:, strip, :]

        block = min(256, count)
        groups = count // block
        table = phi_ref[last, pl.ds(1, rows)].reshape(count, LANES)
        table = jnp.concatenate([table[g * block : (g + 1) * block] for g in range(groups)], axis=1)
        both = jnp.concatenate(pieces(table), axis=0)
        at = pl.ds(pl.multiple_of(me * points, points), points)
        owner, row, lon = owner_ref[at, :], row_ref[at, :], lon_ref[at, :]
        hi = (owner * lat + row) * strips + lon // LANES
        group, hi, lo = hi // block, hi % block, lon % LANES
        index = lax.broadcasted_iota(I32, (block, LANES), 0)
        columns = []
        for p in range(points):
            stack = []
            for g in range(groups):
                key = jnp.where(group[p : p + 1] == g, lo[p : p + 1], -1).astype(F32)
                stack.append(rows_hot(key, LANES))
            columns.append(jnp.concatenate(stack, axis=0))
        found = jnp.dot(both, jnp.concatenate(columns, axis=1), preferred_element_type=F32)
        found = found[:block] + found[block:]
        for p in range(points):
            part = found[:, p * LANES : (p + 1) * LANES]
            part = jnp.where(index == hi[p : p + 1], part, 0.0)
            out_ref[p : p + 1, :] = jnp.sum(part, axis=0, keepdims=True)

    return kernel


def swap(values, bit):
    devices = lax.axis_size("mag")
    return lax.ppermute(values, "mag", [(i, i ^ bit) for i in range(devices)])


def swap_next(values):
    last = lax.axis_size("mag") - 1
    pairs = [(0, 0), (last, last)]
    for i in range(1, last, 2):
        pairs += [(i, i + 1), (i + 1, i)]
    return lax.ppermute(values, "mag", pairs)


def shards(
    density, velocity, mag_field, pressure, conductance, shell_cell, foot_owner, foot_row, foot_lon
):
    devices = lax.axis_size("mag")
    cx, ny, nz = density.shape
    lat, columns = conductance.shape
    strips = columns // LANES
    shell_count = shell_cell.shape[0]
    points = shell_count // LANES
    cells = lat * strips
    count = devices * cells
    shape = jax.ShapeDtypeStruct

    tile = shape((points, LANES), I32)
    slab = shape((8, cx, ny, nz), F32)
    own, edge, cell, strip = call(
        load_arguments,
        [slab, shape((2, 2, ny, nz), F32), tile, shape((cells, LANES), F32)],
        [pltpu.VMEM((lat, columns), F32), pltpu.SemaphoreType.DMA((8,))],
        [HBM] * 6,
    )(
        *(
            pltpu.with_memory_space_constraint(x, pltpu.HBM)
            for x in (
                density,
                velocity,
                mag_field,
                pressure,
                shell_cell.reshape(-1, LANES),
                conductance,
            )
        )
    )
    edge_a, edge_b = swap(edge, 1), swap_next(edge)
    own_side = call(stage_own, slab)(own)

    owner = foot_owner.reshape(-1, LANES)
    row = foot_row.reshape(-1, LANES)
    lon = foot_lon.reshape(-1, LANES)

    load, own = call(
        pick_current, [shape((points + cells, LANES), F32), slab], after=(own_side,)
    )(own, cell, strip, edge_a, edge_b)
    eight_a, eight_b = swap(own, 1), swap_next(own)

    grid = shape((count, 2 * LANES), F32)
    total, blocks, done = (), 1, 0
    bit = devices // 2
    while bit > 1:
        arrived = swap(load, bit)
        if blocks > 1:
            kernel = handing_on(scatter_new(done, blocks - done, points, lat, strips), 1)
            total, load = call(kernel, [grid, shape(load.shape, F32)])(
                *total, new, owner, row, lon, load
            )
            total, done = (total,), blocks
        before, new = load, arrived
        load = jnp.concatenate([load, arrived], axis=0)
        if blocks == 1:
            new = load
        blocks, bit = blocks * 2, bit // 2

    following, half = call(
        stage_one,
        [shape((8, cx + 4, ny, nz), F32), slab],
        [pltpu.VMEM((8, 3 * cx, ny, nz), F32), pltpu.VMEM((8, cx + 4, ny, nz), F32)],
    )(own, eight_a, eight_b, own_side)

    grids = shape((count + count // 2, LANES), F32)
    mine = call(
        scatter_last(blocks, points, lat, strips),
        grids,
        [pltpu.VMEM((count, 2 * LANES), F32)],
        after=(half,),
    )(*total, before, new, owner, row, lon)
    theirs = swap(mine, 1)

    cell_shape = shape((cx, ny, nz), F32)
    vector_shape = shape((3, cx, ny, nz), F32)
    new_density, new_velocity, new_field, new_pressure, end = call(
        stage_two, [cell_shape, vector_shape, vector_shape, cell_shape, shape((8, LANES), F32)]
    )(following, half)

    potential, shell_potential = call(
        solve_and_read(blocks, points, lat, strips),
        [shape((lat, columns), F32), shape((points, LANES), F32)],
        [
            pltpu.VMEM((devices * lat + 2, strips, LANES), F32),
            pltpu.VMEM((5, devices * lat, strips, LANES), F32),
            pltpu.VMEM((2, devices * lat + 2, strips, LANES), F32),
        ],
        after=(end,),
    )(mine, theirs, owner, row, lon)
    return (
        new_density,
        new_velocity,
        new_field,
        new_pressure,
        potential,
        shell_potential.reshape(shell_count),
    )


def solution(mesh):
    both = ("parts", "mag")
    in_specs = (
        P(both, None, None),
        P(None, both, None, None),
        P(None, both, None, None),
        P(both, None, None),
        P(both, None),
        P("mag"),
        P(),
        P(),
        P(),
    )
    out_specs = (
        P(both, None, None),
        P(None, both, None, None),
        P(None, both, None, None),
        P(both, None, None),
        P(both, None),
        P(both),
    )
    return jax.shard_map(shards, mesh=mesh, in_specs=in_specs, out_specs=out_specs, check_vma=False)
```

```python
import jax
import jax.numpy as jnp
from jax import lax
from jax.experimental import pallas as pl
from jax.experimental.pallas import tpu as pltpu
from jax.sharding import PartitionSpec as P

SWEEPS = 4
ADIABATIC = 5.0 / 3.0
TIME_STEP = 0.02
LON_WEIGHT = 0.25
LEAK_RATE = 0.05
SOURCE_GAIN = 10.0
LANES = 128

F32 = jnp.float32
BF16 = jnp.bfloat16
I32 = jnp.int32
VMEM = pl.BlockSpec(memory_space=pltpu.VMEM)
ANY = pl.BlockSpec(memory_space=pl.ANY)
HBM = pl.BlockSpec(memory_space=pltpu.HBM)
MIB = 1024 * 1024


def call(kernel, outs, scratch=(), specs=None, after=()):
    many = isinstance(outs, (list, tuple))

    def body(*refs):
        kernel(*refs[len(after) :])

    def run(*operands):
        in_specs = [ANY] * len(after) + list(specs or [VMEM] * len(operands))
        return pallas(body if after else kernel, outs, many, scratch, in_specs)(*after, *operands)

    return run


def pallas(kernel, outs, many, scratch, in_specs):
    return pl.pallas_call(
        kernel,
        in_specs=in_specs,
        out_shape=outs,
        out_specs=[VMEM] * len(outs) if many else VMEM,
        scratch_shapes=list(scratch),
        compiler_params=pltpu.CompilerParams(
            vmem_limit_bytes=(32 if lax.axis_size("mag") <= 32 else 60) * MIB
        ),
    )


def pieces(values):
    first = values.astype(BF16)
    second = (values - first.astype(F32)).astype(BF16)
    return first, second


def rows_hot(key_row, count, group=256):
    lanes = key_row.shape[1]
    out = []
    for first in range(0, count, group):
        size = min(group, count - first)
        key = jnp.broadcast_to(key_row - first, (16, lanes)).astype(BF16)
        keys = jnp.concatenate([key] * (size // 16), axis=0)
        index = lax.broadcasted_iota(I32, (size, lanes), 0).astype(F32).astype(BF16)
        out.append(jnp.where(keys == index, jnp.ones((), BF16), jnp.zeros((), BF16)))
    return jnp.concatenate(out, axis=0) if len(out) > 1 else out[0]


def half_slope(lower, centre, upper):
    out = []
    for a, b, c in zip(lower, centre, upper):
        s, t = b - a, c - b
        out.append(0.5 * (jnp.maximum(jnp.minimum(s, t), 0.0) + jnp.minimum(jnp.maximum(s, t), 0.0)))
    return out


def dot3(a, b):
    return a[0] * b[0] + a[1] * b[1] + a[2] * b[2]


def conserved(q):
    rho, v, b, p = q[0], q[1:4], q[4:7], q[7]
    energy = p * (1.0 / (ADIABATIC - 1.0)) + 0.5 * rho * dot3(v, v) + 0.5 * dot3(b, b)
    return [rho, rho * v[0], rho * v[1], rho * v[2], b[0], b[1], b[2], energy]


def primitive(u):
    rho, b = u[0], u[4:7]
    inverse = 1.0 / rho
    v = [u[k] * inverse for k in (1, 2, 3)]
    p = (ADIABATIC - 1.0) * (u[7] - 0.5 * rho * dot3(v, v) - 0.5 * dot3(b, b))
    return [rho] + v + list(b) + [p]


def side(q, d):
    rho, v, b, p = q[0], q[1:4], q[4:7], q[7]
    b2 = dot3(b, b)
    half_b2 = 0.5 * b2
    total = p + half_b2
    mom = [rho * x for x in v]
    energy = p * (1.0 / (ADIABATIC - 1.0)) + 0.5 * dot3(mom, v) + half_b2
    vn, bn, mn = v[d], b[d], mom[d]
    flux = [mn]
    for k in range(3):
        f = mn * v[k] - bn * b[k]
        flux.append(f + total if k == d else f)
    for k in range(3):
        flux.append(None if k == d else vn * b[k] - bn * v[k])
    flux.append((energy + total) * vn - bn * dot3(v, b))
    speed = jnp.abs(vn) + jnp.sqrt((ADIABATIC * jnp.abs(p) + b2) / rho)
    return [rho] + mom + list(b) + [energy], flux, speed


def face(left, right, d):
    cons_l, flux_l, speed_l = side(left, d)
    cons_r, flux_r, speed_r = side(right, d)
    half_c = 0.5 * jnp.maximum(speed_l, speed_r)
    out = []
    for k in range(8):
        jump = half_c * (cons_r[k] - cons_l[k])
        out.append(-jump if flux_l[k] is None else 0.5 * (flux_l[k] + flux_r[k]) - jump)
    return out


def periodic(q, axis, d):
    size = q[0].shape[axis]
    back = [pltpu.roll(x, 1, axis) for x in q]
    ahead = [pltpu.roll(x, size - 1, axis) for x in q]
    slope = half_slope(back, q, ahead)
    left = [x + s for x, s in zip(q, slope)]
    right = [pltpu.roll(x - s, size - 1, axis) for x, s in zip(q, slope)]
    flux = face(left, right, d)
    return [pltpu.roll(f, 1, axis) - f for f in flux]


def add(a, b):
    return [x + y for x, y in zip(a, b)]


def plane(ref, x):
    return [ref[k, x] for k in range(8)]


def upper_face(ref, x):
    a, b, c, d = (plane(ref, x + k) for k in (-1, 0, 1, 2))
    left = add(b, half_slope(a, b, c))
    right = [v - s for v, s in zip(c, half_slope(b, c, d))]
    return face(left, right, 0)


def sideways(q):
    return add(periodic(q, 0, 1), periodic(q, 1, 2))


def sweep_planes(ref, first, count, put, others):
    def body(step, below):
        x = first + step
        above = upper_face(ref, x)
        q = plane(ref, x)
        change = [f - g for f, g in zip(below, above)]
        put(x, step, q, add(change, others(step, q)))
        return above

    lax.fori_loop(0, count, body, upper_face(ref, first - 1))


def stage_own(own_ref, side_ref):
    def body(x, carry):
        for k, value in enumerate(sideways(plane(own_ref, x))):
            side_ref[k, x] = value
        return carry

    lax.fori_loop(0, own_ref.shape[1], body, 0)


def stage_one(own_ref, eight_a, eight_b, own_side_ref, next_ref, half_ref, pad_ref, side_ref):
    me = lax.axis_index("mag")
    last = lax.axis_size("mag") - 1
    even = me % 2 == 0
    cx = own_ref.shape[1]
    for k in range(8):
        for x in range(cx):
            low = jnp.where(even, eight_b[k, x], eight_a[k, x])
            high = jnp.where(even, eight_a[k, x], eight_b[k, x])
            pad_ref[k, x] = jnp.where(me == 0, own_ref[k, 0], low)
            pad_ref[k, cx + x] = own_ref[k, x]
            pad_ref[k, 2 * cx + x] = jnp.where(me == last, own_ref[k, cx - 1], high)
            side_ref[k, 2 + x] = own_side_ref[k, x]

    def beside(i, carry):
        step = jnp.where(i < 2, i, cx + i)
        for k, value in enumerate(sideways(plane(pad_ref, cx - 2 + step))):
            side_ref[k, step] = value
        return carry

    lax.fori_loop(0, 4, beside, 0)

    def put(x, step, q, change):
        start = conserved(q)
        first = [s + TIME_STEP * c for s, c in zip(start, change)]
        q1 = primitive(first)
        for k in range(8):
            next_ref[k, step] = q1[k]

        @pl.when(jnp.logical_and(step >= 2, step < cx + 2))
        def _():
            for k in range(8):
                half_ref[k, step - 2] = 0.5 * (start[k] + first[k])

    sweep_planes(pad_ref, cx - 2, cx + 4, put, lambda step, q: plane(side_ref, step))

    @pl.when(me == 0)
    def _():
        for k in range(8):
            next_ref[k, 0] = next_ref[k, 2]
            next_ref[k, 1] = next_ref[k, 2]

    @pl.when(me == last)
    def _():
        for k in range(8):
            next_ref[k, cx + 2] = next_ref[k, cx + 1]
            next_ref[k, cx + 3] = next_ref[k, cx + 1]


def stage_two(next_ref, half_ref, rho_ref, vel_ref, mag_ref, prs_ref, end_ref):
    end_ref[...] = half_ref[0, 0, 0:8]
    cx = half_ref.shape[1]

    def put(x, step, q, change):
        final = [half_ref[k, step] + (0.5 * TIME_STEP) * change[k] for k in range(8)]
        q2 = primitive(final)
        rho_ref[step] = q2[0]
        for k in range(3):
            vel_ref[k, step] = q2[1 + k]
            mag_ref[k, step] = q2[4 + k]
        prs_ref[step] = q2[7]

    sweep_planes(next_ref, 2, cx, put, lambda step, q: sideways(q))


def pick_current(own_ref, cell_ref, edge_a, *refs):
    *far, out_ref, own_out = refs
    me = lax.axis_index("mag")
    last = lax.axis_size("mag") - 1
    even = me % 2 == 0
    cx, ny, nz = own_ref.shape[1:]
    own_out[...] = own_ref[...]
    way = jnp.bitwise_xor(me, me + jnp.where(even, -1, 1))

    def edge_b(k, x):
        value = far[-1][k, x]
        for bits, ref in enumerate(far[:-1], 2):
            value = jnp.where(way == 2**bits - 1, ref[k, x], value)
        return value

    rows = []
    for x in range(cx):
        bx, by, bz = (own_ref[4 + k, x] for k in range(3))

        def neighbour(k, step):
            if 0 <= x + step < cx:
                return own_ref[4 + k, x + step]
            if step < 0:
                below = jnp.where(even, edge_b(k - 1, 1), edge_a[k - 1, 1])
                return jnp.where(me == 0, own_ref[4 + k, x], below)
            above = jnp.where(even, edge_a[k - 1, 0], edge_b(k - 1, 0))
            return jnp.where(me == last, own_ref[4 + k, x], above)

        def along_x(k):
            return 0.5 * (neighbour(k, 1) - neighbour(k, -1))

        def along(v, axis):
            return 0.5 * (pltpu.roll(v, v.shape[axis] - 1, axis) - pltpu.roll(v, 1, axis))

        jx = along(bz, 0) - along(by, 1)
        jy = along(bx, 1) - along_x(2)
        jz = along_x(1) - along(bx, 0)
        norm = jnp.sqrt(bx * bx + by * by + bz * bz + 1.0)
        rows.append(SOURCE_GAIN * (jx * bx + jy * by + jz * bz) / norm)
    table = jnp.concatenate(rows, axis=0)
    count = table.shape[0]
    both = jnp.concatenate(pieces(table), axis=0)
    cells = cell_ref[...]
    hi, lo = cells // nz, (cells % nz).astype(F32)
    index = lax.broadcasted_iota(I32, (count, LANES), 0)
    points = cells.shape[0]
    for s in range(points):
        hot = rows_hot(lo[s : s + 1], nz)
        found = jnp.dot(both, hot, preferred_element_type=F32)
        found = found[:count] + found[count:]
        mine = jnp.where(index == hi[s : s + 1], found, 0.0)
        out_ref[s : s + 1, :] = jnp.sum(mine, axis=0, keepdims=True)


def load_arguments(
    rho_ref, vel_ref, mag_ref, prs_ref, cell_ref, cond_ref, own_out, edge_out, cell_out, strip_out, rows, sems
):
    last = mag_ref.shape[1] - 1
    pairs = [
        (cond_ref, rows),
        (mag_ref.at[pl.ds(1, 2), pl.ds(0, 1)], edge_out.at[:, pl.ds(0, 1)]),
        (mag_ref.at[pl.ds(1, 2), pl.ds(last, 1)], edge_out.at[:, pl.ds(1, 1)]),
        (cell_ref, cell_out),
        (rho_ref, own_out.at[0]),
        (vel_ref, own_out.at[pl.ds(1, 3)]),
        (mag_ref, own_out.at[pl.ds(4, 3)]),
        (prs_ref, own_out.at[7]),
    ]
    copies = [
        pltpu.make_async_copy(source, target, sems.at[k])
        for k, (source, target) in enumerate(pairs)
    ]
    for copy in copies:
        copy.start()
    copies[0].wait()
    lat, columns = rows.shape
    strips = columns // LANES
    for r in range(lat):
        for strip in range(strips):
            place = r * strips + strip
            strip_out[place : place + 1, :] = rows[r : r + 1, strip * LANES : (strip + 1) * LANES]
    for copy in copies[1:]:
        copy.wait()


def east_of(v):
    lane = lax.broadcasted_iota(I32, v.shape, 2)
    turned = pltpu.roll(v, v.shape[2] - 1, 2)
    return jnp.where(lane == v.shape[2] - 1, pltpu.roll(turned, v.shape[1] - 1, 1), turned)


def west_of(v):
    lane = lax.broadcasted_iota(I32, v.shape, 2)
    turned = pltpu.roll(v, 1, 2)
    return jnp.where(lane == 0, pltpu.roll(turned, 1, 1), turned)


def scatter_block(value, hi, lo, count):
    hi, lo = hi.astype(F32), lo.astype(F32)
    high_piece = value.astype(BF16).astype(F32)
    low_piece = value - high_piece
    lefts, rights = [], []
    for s in range(value.shape[0]):
        lefts.append(rows_hot(hi[s : s + 1], count))
        hot = rows_hot(lo[s : s + 1], LANES)
        two = []
        for piece in (high_piece, low_piece):
            wide = jnp.broadcast_to(piece[s : s + 1], (16, LANES)).astype(BF16)
            two.append(hot * jnp.concatenate([wide] * (LANES // 16), axis=0))
        rights.append(jnp.concatenate(two, axis=0))
    left = jnp.concatenate(lefts, axis=1)
    right = jnp.concatenate(rights, axis=1)
    return lax.dot_general(left, right, (((1,), (1,)), ((), ())), preferred_element_type=F32)


def repeat(count, body):
    if count <= 8:
        for i in range(count):
            body(i)
    else:
        lax.fori_loop(0, count, lambda i, carry: (body(i), carry)[1], 0)


def origin(me, devices, j):
    mask, bit, k = 0, devices // 2, 0
    while bit > 1:
        mask = mask + ((j >> k) & 1) * bit
        bit, k = bit // 2, k + 1
    return jnp.bitwise_xor(me, mask)


def scatter_new(first, blocks, points, lat, strips):
    def kernel(*refs):
        *total_in, load_ref, owner_ref, row_ref, lon_ref, out_ref = refs
        me = lax.axis_index("mag")
        devices = lax.axis_size("mag")
        count = out_ref.shape[0]
        rows = min(count, 1024)
        stride = load_ref.shape[0] // blocks

        def part(j, g, base_ref):
            device = origin(me, devices, first + j)
            at = pl.ds(pl.multiple_of(device * points, points), points)
            value = load_ref[pl.ds(pl.multiple_of(j * stride, 8), points), :]
            hi = (owner_ref[at, :] * lat + row_ref[at, :]) * strips + lon_ref[at, :] // LANES
            lo = lon_ref[at, :] % LANES
            new = scatter_block(value, hi - g * rows, lo, rows)
            place = pl.ds(pl.multiple_of(g * rows, rows), rows)
            out_ref[place, :] = new if base_ref is None else base_ref[place, :] + new

        def group(g):
            part(0, g, total_in[0] if total_in else None)
            repeat(blocks - 1, lambda j: part(j + 1, g, out_ref))

        repeat(count // rows, group)

    return kernel


def handing_on(kernel, count):
    def run(*refs):
        outs = count + 1
        given = refs[-outs - count : -outs]
        for source, target in zip(given, refs[-count:]):
            target[...] = source[...]
        kernel(*refs[: -outs - count], refs[-outs])

    return run


def scatter_last(blocks, points, lat, strips):
    def kernel(total_ref, load_ref, owner_ref, row_ref, lon_ref, cond_ref, out_ref, work_ref):
        half = blocks // 2
        scatter_new(half, half, points, lat, strips)(
            total_ref, load_ref, owner_ref, row_ref, lon_ref, work_ref
        )
        count = work_ref.shape[0]
        out_ref[:count, :] = work_ref[:, :LANES] + work_ref[:, LANES:]
        out_ref[count:, :] = cond_ref[...]

    return kernel


def solve_and_read(blocks, points, lat, strips):
    def kernel(
        mine_ref, their_ref, owner_ref, row_ref, lon_ref, flat_ref, out_ref, s_ref, w_ref, phi_ref
    ):
        me = lax.axis_index("mag")
        devices = lax.axis_size("mag")
        rows = devices * lat
        count = rows * strips
        cells = lat * strips
        zeros = jnp.zeros((1, strips, LANES), F32)
        for ref in (s_ref, phi_ref.at[0], phi_ref.at[1]):
            ref[0:1] = zeros
            ref[rows + 1 : rows + 2] = zeros

        def place(j):
            at = pl.ds(pl.multiple_of(count + j * cells, cells), cells)
            for ref, who in ((mine_ref, me), (their_ref, jnp.bitwise_xor(me, 1))):
                device = origin(who, devices, j)
                s_ref[pl.ds(device * lat + 1, lat)] = ref[at, :].reshape(lat, strips, LANES)

        repeat(blocks, place)
        chunk = min(8, rows)

        def prepare(i):
            r = i * chunk
            s, above, below = (s_ref[pl.ds(r + k, chunk)] for k in (1, 0, 2))
            north, south = 0.5 * (s + above), 0.5 * (s + below)
            east = (0.5 * LON_WEIGHT) * (s + east_of(s))
            west = (0.5 * LON_WEIGHT) * (s + west_of(s))
            inverse = 1.0 / (north + south + east + west + LEAK_RATE * s)
            at = pl.ds(pl.multiple_of(r * strips, 8), chunk * strips)
            source = (mine_ref[at, :] + their_ref[at, :]).reshape(chunk, strips, LANES)
            for k, value in enumerate((source, north, south, east, west)):
                w_ref[k, pl.ds(r, chunk)] = value * inverse
            phi_ref[0, pl.ds(r + 1, chunk)] = source * inverse

        repeat(rows // chunk, prepare)
        for sweep in range(SWEEPS - 1):
            old, new = sweep % 2, 1 - sweep % 2

            def relax(i):
                r = i * chunk
                phi, above, below = (phi_ref[old, pl.ds(r + k, chunk)] for k in (1, 0, 2))
                source, north, south, east, west = (w_ref[k, pl.ds(r, chunk)] for k in range(5))
                phi_ref[new, pl.ds(r + 1, chunk)] = (
                    source
                    + north * above
                    + south * below
                    + east * east_of(phi)
                    + west * west_of(phi)
                )

            repeat(rows // chunk, relax)
        last = (SWEEPS - 1) % 2
        own = phi_ref[last, pl.ds(me * lat + 1, lat)]
        for strip in range(strips):
            flat_ref[:, strip * LANES : (strip + 1) * LANES] = own[:, strip, :]

        block = min(256, count)
        groups = count // block
        table = phi_ref[last, pl.ds(1, rows)].reshape(count, LANES)
        table = jnp.concatenate([table[g * block : (g + 1) * block] for g in range(groups)], axis=1)
        both = jnp.concatenate(pieces(table), axis=0)
        at = pl.ds(pl.multiple_of(me * points, points), points)
        owner, row, lon = owner_ref[at, :], row_ref[at, :], lon_ref[at, :]
        hi = (owner * lat + row) * strips + lon // LANES
        group, hi, lo = hi // block, hi % block, lon % LANES
        index = lax.broadcasted_iota(I32, (block, LANES), 0)
        columns = []
        for p in range(points):
            stack = []
            for g in range(groups):
                key = jnp.where(group[p : p + 1] == g, lo[p : p + 1], -1).astype(F32)
                stack.append(rows_hot(key, LANES))
            columns.append(jnp.concatenate(stack, axis=0))
        found = jnp.dot(both, jnp.concatenate(columns, axis=1), preferred_element_type=F32)
        found = found[:block] + found[block:]
        for p in range(points):
            part = found[:, p * LANES : (p + 1) * LANES]
            part = jnp.where(index == hi[p : p + 1], part, 0.0)
            out_ref[p : p + 1, :] = jnp.sum(part, axis=0, keepdims=True)

    return kernel


def swap(values, bit):
    devices = lax.axis_size("mag")
    return lax.ppermute(values, "mag", [(i, i ^ bit) for i in range(devices)])


def swap_next(values):
    last = lax.axis_size("mag") - 1
    pairs = [(0, 0), (last, last)]
    for i in range(1, last, 2):
        pairs += [(i, i + 1), (i + 1, i)]
    return lax.ppermute(values, "mag", pairs)


def shards(
    density, velocity, mag_field, pressure, conductance, shell_cell, foot_owner, foot_row, foot_lon
):
    devices = lax.axis_size("mag")
    cx, ny, nz = density.shape
    lat, columns = conductance.shape
    strips = columns // LANES
    shell_count = shell_cell.shape[0]
    points = shell_count // LANES
    cells = lat * strips
    count = devices * cells
    shape = jax.ShapeDtypeStruct

    tile = shape((points, LANES), I32)
    slab = shape((8, cx, ny, nz), F32)
    own, edge, cell, strip = call(
        load_arguments,
        [slab, shape((2, 2, ny, nz), F32), tile, shape((cells, LANES), F32)],
        [pltpu.VMEM((lat, columns), F32), pltpu.SemaphoreType.DMA((8,))],
        [HBM] * 6,
    )(
        *(
            pltpu.with_memory_space_constraint(x, pltpu.HBM)
            for x in (
                density,
                velocity,
                mag_field,
                pressure,
                shell_cell.reshape(-1, LANES),
                conductance,
            )
        )
    )
    far, bits, conds = [], [], [strip]
    bit = devices // 2
    while bit > 1:
        bits.append(bit)
        far.insert(0, swap(edge, 2 * bit - 1))
        bit //= 2
    edge_a = swap(edge, 1)
    for bit in bits:
        conds.append(jnp.concatenate([conds[-1], swap(conds[-1], bit)], axis=0))
    own_side = call(stage_own, slab)(own)

    owner = foot_owner.reshape(-1, LANES)
    row = foot_row.reshape(-1, LANES)
    lon = foot_lon.reshape(-1, LANES)

    load, own = call(
        pick_current, [shape((points, LANES), F32), slab], after=(own_side, conds[1])
    )(own, cell, edge_a, *far)
    eight_a, eight_b = swap(own, 1), swap_next(own)

    grid = shape((count, 2 * LANES), F32)
    total, blocks, done = (), 1, 0
    for turn, bit in enumerate(bits):
        arrived = swap(load, bit)
        if turn > 0:
            kernel = handing_on(scatter_new(done, blocks - done, points, lat, strips), 1)
            after = (conds[turn + 1],) if turn + 1 < len(bits) else ()
            total, load = call(kernel, [grid, shape(load.shape, F32)], after=after)(
                *total, new, owner, row, lon, load
            )
            total, done = (total,), blocks
        load = jnp.concatenate([load, arrived], axis=0)
        new = arrived if turn > 0 else load
        blocks *= 2

    following, half = call(
        stage_one,
        [shape((8, cx + 4, ny, nz), F32), slab],
        [pltpu.VMEM((8, 3 * cx, ny, nz), F32), pltpu.VMEM((8, cx + 4, ny, nz), F32)],
    )(own, eight_a, eight_b, own_side)

    grids = shape((count + count // 2, LANES), F32)
    mine = call(
        scatter_last(blocks, points, lat, strips),
        grids,
        [pltpu.VMEM((count, 2 * LANES), F32)],
        after=(half,),
    )(*total, new, owner, row, lon, conds[-1])
    theirs = swap(mine, 1)

    cell_shape = shape((cx, ny, nz), F32)
    vector_shape = shape((3, cx, ny, nz), F32)
    new_density, new_velocity, new_field, new_pressure, end = call(
        stage_two, [cell_shape, vector_shape, vector_shape, cell_shape, shape((8, LANES), F32)]
    )(following, half)

    potential, shell_potential = call(
        solve_and_read(blocks, points, lat, strips),
        [shape((lat, columns), F32), shape((points, LANES), F32)],
        [
            pltpu.VMEM((devices * lat + 2, strips, LANES), F32),
            pltpu.VMEM((5, devices * lat, strips, LANES), F32),
            pltpu.VMEM((2, devices * lat + 2, strips, LANES), F32),
        ],
        after=(end,),
    )(mine, theirs, owner, row, lon)
    return (
        new_density,
        new_velocity,
        new_field,
        new_pressure,
        potential,
        shell_potential.reshape(shell_count),
    )


def solution(mesh):
    both = ("parts", "mag")
    in_specs = (
        P(both, None, None),
        P(None, both, None, None),
        P(None, both, None, None),
        P(both, None, None),
        P(both, None),
        P("mag"),
        P(),
        P(),
        P(),
    )
    out_specs = (
        P(both, None, None),
        P(None, both, None, None),
        P(None, both, None, None),
        P(both, None, None),
        P(both, None),
        P(both),
    )
    return jax.shard_map(shards, mesh=mesh, in_specs=in_specs, out_specs=out_specs, check_vma=False)
```

```python
import jax
import jax.numpy as jnp
from jax import lax
from jax.experimental import pallas as pl
from jax.experimental.pallas import tpu as pltpu
from jax.sharding import PartitionSpec as P

SWEEPS = 4
ADIABATIC = 5.0 / 3.0
TIME_STEP = 0.02
LON_WEIGHT = 0.25
LEAK_RATE = 0.05
SOURCE_GAIN = 10.0
LANES = 128

F32 = jnp.float32
BF16 = jnp.bfloat16
I32 = jnp.int32
VMEM = pl.BlockSpec(memory_space=pltpu.VMEM)
ANY = pl.BlockSpec(memory_space=pl.ANY)
HBM = pl.BlockSpec(memory_space=pltpu.HBM)
MIB = 1024 * 1024


def call(kernel, outs, scratch=(), specs=None, after=()):
    many = isinstance(outs, (list, tuple))

    def body(*refs):
        kernel(*refs[len(after) :])

    def run(*operands):
        in_specs = [ANY] * len(after) + list(specs or [VMEM] * len(operands))
        return pallas(body if after else kernel, outs, many, scratch, in_specs)(*after, *operands)

    return run


def pallas(kernel, outs, many, scratch, in_specs):
    return pl.pallas_call(
        kernel,
        in_specs=in_specs,
        out_shape=outs,
        out_specs=[VMEM] * len(outs) if many else VMEM,
        scratch_shapes=list(scratch),
        compiler_params=pltpu.CompilerParams(
            vmem_limit_bytes=(32 if lax.axis_size("mag") <= 32 else 60) * MIB
        ),
    )


def pieces(values):
    first = values.astype(BF16)
    second = (values - first.astype(F32)).astype(BF16)
    return first, second


def rows_hot(key_row, count, group=256):
    lanes = key_row.shape[1]
    out = []
    for first in range(0, count, group):
        size = min(group, count - first)
        key = jnp.broadcast_to(key_row - first, (16, lanes)).astype(BF16)
        keys = jnp.concatenate([key] * (size // 16), axis=0)
        index = lax.broadcasted_iota(I32, (size, lanes), 0).astype(F32).astype(BF16)
        out.append(jnp.where(keys == index, jnp.ones((), BF16), jnp.zeros((), BF16)))
    return jnp.concatenate(out, axis=0) if len(out) > 1 else out[0]


def half_slope(lower, centre, upper):
    out = []
    for a, b, c in zip(lower, centre, upper):
        s, t = b - a, c - b
        out.append(0.5 * (jnp.maximum(jnp.minimum(s, t), 0.0) + jnp.minimum(jnp.maximum(s, t), 0.0)))
    return out


def dot3(a, b):
    return a[0] * b[0] + a[1] * b[1] + a[2] * b[2]


def conserved(q):
    rho, v, b, p = q[0], q[1:4], q[4:7], q[7]
    energy = p * (1.0 / (ADIABATIC - 1.0)) + 0.5 * rho * dot3(v, v) + 0.5 * dot3(b, b)
    return [rho, rho * v[0], rho * v[1], rho * v[2], b[0], b[1], b[2], energy]


def primitive(u):
    rho, b = u[0], u[4:7]
    inverse = 1.0 / rho
    v = [u[k] * inverse for k in (1, 2, 3)]
    p = (ADIABATIC - 1.0) * (u[7] - 0.5 * rho * dot3(v, v) - 0.5 * dot3(b, b))
    return [rho] + v + list(b) + [p]


def side(q, d):
    rho, v, b, p = q[0], q[1:4], q[4:7], q[7]
    b2 = dot3(b, b)
    half_b2 = 0.5 * b2
    total = p + half_b2
    mom = [rho * x for x in v]
    energy = p * (1.0 / (ADIABATIC - 1.0)) + 0.5 * dot3(mom, v) + half_b2
    vn, bn, mn = v[d], b[d], mom[d]
    flux = [mn]
    for k in range(3):
        f = mn * v[k] - bn * b[k]
        flux.append(f + total if k == d else f)
    for k in range(3):
        flux.append(None if k == d else vn * b[k] - bn * v[k])
    flux.append((energy + total) * vn - bn * dot3(v, b))
    speed = jnp.abs(vn) + jnp.sqrt((ADIABATIC * jnp.abs(p) + b2) / rho)
    return [rho] + mom + list(b) + [energy], flux, speed


def face(left, right, d):
    cons_l, flux_l, speed_l = side(left, d)
    cons_r, flux_r, speed_r = side(right, d)
    half_c = 0.5 * jnp.maximum(speed_l, speed_r)
    out = []
    for k in range(8):
        jump = half_c * (cons_r[k] - cons_l[k])
        out.append(-jump if flux_l[k] is None else 0.5 * (flux_l[k] + flux_r[k]) - jump)
    return out


def periodic(q, axis, d):
    size = q[0].shape[axis]
    back = [pltpu.roll(x, 1, axis) for x in q]
    ahead = [pltpu.roll(x, size - 1, axis) for x in q]
    slope = half_slope(back, q, ahead)
    left = [x + s for x, s in zip(q, slope)]
    right = [pltpu.roll(x - s, size - 1, axis) for x, s in zip(q, slope)]
    flux = face(left, right, d)
    return [pltpu.roll(f, 1, axis) - f for f in flux]


def add(a, b):
    return [x + y for x, y in zip(a, b)]


def plane(ref, x):
    return [ref[k, x] for k in range(8)]


def upper_face(ref, x):
    a, b, c, d = (plane(ref, x + k) for k in (-1, 0, 1, 2))
    left = add(b, half_slope(a, b, c))
    right = [v - s for v, s in zip(c, half_slope(b, c, d))]
    return face(left, right, 0)


def sideways(q):
    return add(periodic(q, 0, 1), periodic(q, 1, 2))


def sweep_planes(ref, first, count, put, others):
    def body(step, below):
        x = first + step
        above = upper_face(ref, x)
        q = plane(ref, x)
        change = [f - g for f, g in zip(below, above)]
        put(x, step, q, add(change, others(step, q)))
        return above

    lax.fori_loop(0, count, body, upper_face(ref, first - 1))


def stage_own(own_ref, side_ref):
    def body(x, carry):
        for k, value in enumerate(sideways(plane(own_ref, x))):
            side_ref[k, x] = value
        return carry

    lax.fori_loop(0, own_ref.shape[1], body, 0)


def split_planes(ref, out_a, out_b):
    odd = lax.axis_index("mag") % 2
    top = ref.shape[1] - 2
    for k in range(8):
        out_a[k] = ref[k, pl.ds((1 - odd) * top, 2)]
        out_b[k] = ref[k, pl.ds(odd * top, 2)]


def pad_planes(ref, from_a, from_b, pad_ref):
    me = lax.axis_index("mag")
    last = lax.axis_size("mag") - 1
    even = me % 2 == 0
    cx = ref.shape[1]
    for k in range(8):
        for x in range(2):
            low = jnp.where(even, from_b[k, x], from_a[k, x])
            high = jnp.where(even, from_a[k, x], from_b[k, x])
            pad_ref[k, x] = jnp.where(me == 0, ref[k, 0], low)
            pad_ref[k, cx + 2 + x] = jnp.where(me == last, ref[k, cx - 1], high)
        for x in range(cx):
            pad_ref[k, 2 + x] = ref[k, x]


def stage_one(own_ref, from_a, from_b, side_ref, load_ref, next_ref, half_ref, out_a, out_b, load_out, pad_ref):
    pad_planes(own_ref, from_a, from_b, pad_ref)
    load_out[...] = load_ref[...]

    def put(x, step, q, change):
        start = conserved(q)
        first = [s + TIME_STEP * c for s, c in zip(start, change)]
        q1 = primitive(first)
        for k in range(8):
            next_ref[k, step] = q1[k]
            half_ref[k, step] = 0.5 * (start[k] + first[k])

    sweep_planes(pad_ref, 2, own_ref.shape[1], put, lambda step, q: plane(side_ref, step))
    split_planes(next_ref, out_a, out_b)


def stage_two(pad_ref, half_ref, rho_ref, vel_ref, mag_ref, prs_ref, end_ref):
    end_ref[...] = half_ref[0, 0, 0:8]

    def put(x, step, q, change):
        final = [half_ref[k, step] + (0.5 * TIME_STEP) * change[k] for k in range(8)]
        q2 = primitive(final)
        rho_ref[step] = q2[0]
        for k in range(3):
            vel_ref[k, step] = q2[1 + k]
            mag_ref[k, step] = q2[4 + k]
        prs_ref[step] = q2[7]

    sweep_planes(pad_ref, 2, half_ref.shape[1], put, lambda step, q: sideways(q))


def pick_current(own_ref, cell_ref, strip_ref, from_a, from_b, out_ref):
    me = lax.axis_index("mag")
    last = lax.axis_size("mag") - 1
    even = me % 2 == 0
    cx, ny, nz = own_ref.shape[1:]
    rows = []
    for x in range(cx):
        bx, by, bz = (own_ref[4 + k, x] for k in range(3))

        def neighbour(k, step):
            if 0 <= x + step < cx:
                return own_ref[4 + k, x + step]
            if step < 0:
                below = jnp.where(even, from_b[4 + k, 1], from_a[4 + k, 1])
                return jnp.where(me == 0, own_ref[4 + k, x], below)
            above = jnp.where(even, from_a[4 + k, 0], from_b[4 + k, 0])
            return jnp.where(me == last, own_ref[4 + k, x], above)

        def along_x(k):
            return 0.5 * (neighbour(k, 1) - neighbour(k, -1))

        def along(v, axis):
            return 0.5 * (pltpu.roll(v, v.shape[axis] - 1, axis) - pltpu.roll(v, 1, axis))

        jx = along(bz, 0) - along(by, 1)
        jy = along(bx, 1) - along_x(2)
        jz = along_x(1) - along(bx, 0)
        norm = jnp.sqrt(bx * bx + by * by + bz * bz + 1.0)
        rows.append(SOURCE_GAIN * (jx * bx + jy * by + jz * bz) / norm)
    table = jnp.concatenate(rows, axis=0)
    count = table.shape[0]
    both = jnp.concatenate(pieces(table), axis=0)
    cells = cell_ref[...]
    hi, lo = cells // nz, (cells % nz).astype(F32)
    index = lax.broadcasted_iota(I32, (count, LANES), 0)
    points = cells.shape[0]
    for s in range(points):
        hot = rows_hot(lo[s : s + 1], nz)
        found = jnp.dot(both, hot, preferred_element_type=F32)
        found = found[:count] + found[count:]
        mine = jnp.where(index == hi[s : s + 1], found, 0.0)
        out_ref[s : s + 1, :] = jnp.sum(mine, axis=0, keepdims=True)
    out_ref[points:, :] = strip_ref[...]


def load_arguments(
    rho_ref, vel_ref, mag_ref, prs_ref, cell_ref, cond_ref, own_out, a_out, b_out, cell_out, strip_out, rows, sems
):
    pairs = [
        (cond_ref, rows),
        (cell_ref, cell_out),
        (rho_ref, own_out.at[0]),
        (vel_ref, own_out.at[pl.ds(1, 3)]),
        (mag_ref, own_out.at[pl.ds(4, 3)]),
        (prs_ref, own_out.at[7]),
    ]
    copies = [
        pltpu.make_async_copy(source, target, sems.at[k])
        for k, (source, target) in enumerate(pairs)
    ]
    for copy in copies:
        copy.start()
    copies[0].wait()
    lat, columns = rows.shape
    strips = columns // LANES
    for r in range(lat):
        for strip in range(strips):
            place = r * strips + strip
            strip_out[place : place + 1, :] = rows[r : r + 1, strip * LANES : (strip + 1) * LANES]
    for copy in copies[1:]:
        copy.wait()
    split_planes(own_out, a_out, b_out)


def east_of(v):
    lane = lax.broadcasted_iota(I32, v.shape, 2)
    turned = pltpu.roll(v, v.shape[2] - 1, 2)
    return jnp.where(lane == v.shape[2] - 1, pltpu.roll(turned, v.shape[1] - 1, 1), turned)


def west_of(v):
    lane = lax.broadcasted_iota(I32, v.shape, 2)
    turned = pltpu.roll(v, 1, 2)
    return jnp.where(lane == 0, pltpu.roll(turned, 1, 1), turned)


def scatter_block(value, hi, lo, count):
    hi, lo = hi.astype(F32), lo.astype(F32)
    high_piece = value.astype(BF16).astype(F32)
    low_piece = value - high_piece
    lefts, rights = [], []
    for s in range(value.shape[0]):
        lefts.append(rows_hot(hi[s : s + 1], count))
        hot = rows_hot(lo[s : s + 1], LANES)
        two = []
        for piece in (high_piece, low_piece):
            wide = jnp.broadcast_to(piece[s : s + 1], (16, LANES)).astype(BF16)
            two.append(hot * jnp.concatenate([wide] * (LANES // 16), axis=0))
        rights.append(jnp.concatenate(two, axis=0))
    left = jnp.concatenate(lefts, axis=1)
    right = jnp.concatenate(rights, axis=1)
    return lax.dot_general(left, right, (((1,), (1,)), ((), ())), preferred_element_type=F32)


def repeat(count, body):
    if count <= 8:
        for i in range(count):
            body(i)
    else:
        lax.fori_loop(0, count, lambda i, carry: (body(i), carry)[1], 0)


def origin(me, devices, j):
    mask, bit, k = 0, devices // 2, 0
    while bit > 1:
        mask = mask + ((j >> k) & 1) * bit
        bit, k = bit // 2, k + 1
    return jnp.bitwise_xor(me, mask)


def scatter_new(first, blocks, points, lat, strips):
    def kernel(*refs):
        *total_in, load_ref, owner_ref, row_ref, lon_ref, out_ref = refs
        me = lax.axis_index("mag")
        devices = lax.axis_size("mag")
        count = out_ref.shape[0]
        rows = min(count, 1024)
        stride = load_ref.shape[0] // blocks

        def part(j, g, base_ref):
            device = origin(me, devices, first + j)
            at = pl.ds(pl.multiple_of(device * points, points), points)
            value = load_ref[pl.ds(pl.multiple_of(j * stride, 8), points), :]
            hi = (owner_ref[at, :] * lat + row_ref[at, :]) * strips + lon_ref[at, :] // LANES
            lo = lon_ref[at, :] % LANES
            new = scatter_block(value, hi - g * rows, lo, rows)
            place = pl.ds(pl.multiple_of(g * rows, rows), rows)
            out_ref[place, :] = new if base_ref is None else base_ref[place, :] + new

        def group(g):
            part(0, g, total_in[0] if total_in else None)
            repeat(blocks - 1, lambda j: part(j + 1, g, out_ref))

        repeat(count // rows, group)

    return kernel


def handing_on(kernel, count):
    def run(*refs):
        outs = count + 1
        given = refs[-outs - count : -outs]
        for source, target in zip(given, refs[-count:]):
            target[...] = source[...]
        kernel(*refs[: -outs - count], refs[-outs])

    return run


def scatter_last(blocks, points, lat, strips):
    def kernel(total_ref, before_ref, load_ref, owner_ref, row_ref, lon_ref, out_ref, work_ref):
        half = blocks // 2
        scatter_new(half, half, points, lat, strips)(
            total_ref, load_ref, owner_ref, row_ref, lon_ref, work_ref
        )
        count = work_ref.shape[0]
        out_ref[:count, :] = work_ref[:, :LANES] + work_ref[:, LANES:]
        cells = lat * strips
        stride = points + cells
        for j in range(blocks):
            ref = before_ref if j < half else load_ref
            start = (j % half) * stride + points
            out_ref[count + j * cells : count + (j + 1) * cells, :] = ref[start : start + cells, :]

    return kernel


def solve_and_read(blocks, points, lat, strips):
    def kernel(
        mine_ref, their_ref, owner_ref, row_ref, lon_ref, flat_ref, out_ref, s_ref, w_ref, phi_ref
    ):
        me = lax.axis_index("mag")
        devices = lax.axis_size("mag")
        rows = devices * lat
        count = rows * strips
        cells = lat * strips
        zeros = jnp.zeros((1, strips, LANES), F32)
        for ref in (s_ref, phi_ref.at[0], phi_ref.at[1]):
            ref[0:1] = zeros
            ref[rows + 1 : rows + 2] = zeros

        def place(j):
            at = pl.ds(pl.multiple_of(count + j * cells, cells), cells)
            for ref, who in ((mine_ref, me), (their_ref, jnp.bitwise_xor(me, 1))):
                device = origin(who, devices, j)
                s_ref[pl.ds(device * lat + 1, lat)] = ref[at, :].reshape(lat, strips, LANES)

        repeat(blocks, place)
        chunk = min(8, rows)

        def prepare(i):
            r = i * chunk
            s, above, below = (s_ref[pl.ds(r + k, chunk)] for k in (1, 0, 2))
            north, south = 0.5 * (s + above), 0.5 * (s + below)
            east = (0.5 * LON_WEIGHT) * (s + east_of(s))
            west = (0.5 * LON_WEIGHT) * (s + west_of(s))
            inverse = 1.0 / (north + south + east + west + LEAK_RATE * s)
            at = pl.ds(pl.multiple_of(r * strips, 8), chunk * strips)
            source = (mine_ref[at, :] + their_ref[at, :]).reshape(chunk, strips, LANES)
            for k, value in enumerate((source, north, south, east, west)):
                w_ref[k, pl.ds(r, chunk)] = value * inverse
            phi_ref[0, pl.ds(r + 1, chunk)] = source * inverse

        repeat(rows // chunk, prepare)
        for sweep in range(SWEEPS - 1):
            old, new = sweep % 2, 1 - sweep % 2

            def relax(i):
                r = i * chunk
                phi, above, below = (phi_ref[old, pl.ds(r + k, chunk)] for k in (1, 0, 2))
                source, north, south, east, west = (w_ref[k, pl.ds(r, chunk)] for k in range(5))
                phi_ref[new, pl.ds(r + 1, chunk)] = (
                    source
                    + north * above
                    + south * below
                    + east * east_of(phi)
                    + west * west_of(phi)
                )

            repeat(rows // chunk, relax)
        last = (SWEEPS - 1) % 2
        own = phi_ref[last, pl.ds(me * lat + 1, lat)]
        for strip in range(strips):
            flat_ref[:, strip * LANES : (strip + 1) * LANES] = own[:, strip, :]

        block = min(256, count)
        groups = count // block
        table = phi_ref[last, pl.ds(1, rows)].reshape(count, LANES)
        table = jnp.concatenate([table[g * block : (g + 1) * block] for g in range(groups)], axis=1)
        both = jnp.concatenate(pieces(table), axis=0)
        at = pl.ds(pl.multiple_of(me * points, points), points)
        owner, row, lon = owner_ref[at, :], row_ref[at, :], lon_ref[at, :]
        hi = (owner * lat + row) * strips + lon // LANES
        group, hi, lo = hi // block, hi % block, lon % LANES
        index = lax.broadcasted_iota(I32, (block, LANES), 0)
        columns = []
        for p in range(points):
            stack = []
            for g in range(groups):
                key = jnp.where(group[p : p + 1] == g, lo[p : p + 1], -1).astype(F32)
                stack.append(rows_hot(key, LANES))
            columns.append(jnp.concatenate(stack, axis=0))
        found = jnp.dot(both, jnp.concatenate(columns, axis=1), preferred_element_type=F32)
        found = found[:block] + found[block:]
        for p in range(points):
            part = found[:, p * LANES : (p + 1) * LANES]
            part = jnp.where(index == hi[p : p + 1], part, 0.0)
            out_ref[p : p + 1, :] = jnp.sum(part, axis=0, keepdims=True)

    return kernel


def swap(values, bit):
    devices = lax.axis_size("mag")
    return lax.ppermute(values, "mag", [(i, i ^ bit) for i in range(devices)])


def swap_next(values):
    devices = lax.axis_size("mag")
    pairs = [(i, (i + (1 if i % 2 else -1)) % devices) for i in range(devices)]
    return lax.ppermute(values, "mag", pairs)


def shards(
    density, velocity, mag_field, pressure, conductance, shell_cell, foot_owner, foot_row, foot_lon
):
    devices = lax.axis_size("mag")
    cx, ny, nz = density.shape
    lat, columns = conductance.shape
    strips = columns // LANES
    shell_count = shell_cell.shape[0]
    points = shell_count // LANES
    cells = lat * strips
    count = devices * cells
    shape = jax.ShapeDtypeStruct

    tile = shape((points, LANES), I32)
    slab = shape((8, cx, ny, nz), F32)
    two = shape((8, 2, ny, nz), F32)
    own, to_a, to_b, cell, strip = call(
        load_arguments,
        [slab, two, two, tile, shape((cells, LANES), F32)],
        [pltpu.VMEM((lat, columns), F32), pltpu.SemaphoreType.DMA((6,))],
        [HBM] * 6,
    )(
        *(
            pltpu.with_memory_space_constraint(x, pltpu.HBM)
            for x in (
                density,
                velocity,
                mag_field,
                pressure,
                shell_cell.reshape(-1, LANES),
                conductance,
            )
        )
    )
    from_a, from_b = swap(to_a, 1), swap_next(to_b)
    own_side = call(stage_own, slab)(own)

    owner = foot_owner.reshape(-1, LANES)
    row = foot_row.reshape(-1, LANES)
    lon = foot_lon.reshape(-1, LANES)

    payload = shape((points + cells, LANES), F32)
    load = call(pick_current, payload, after=(own_side,))(own, cell, strip, from_a, from_b)
    pad = [pltpu.VMEM((8, cx + 4, ny, nz), F32)]
    following, half, next_a, next_b, after_one = call(
        stage_one, [slab, slab, two, two, payload], pad
    )(own, from_a, from_b, own_side, load)
    next_a, next_b = swap(next_a, 1), swap_next(next_b)

    grid = shape((count, 2 * LANES), F32)
    total, blocks, done = (), 1, 0
    bit = devices // 2
    while bit > 1:
        arrived = swap(load, bit)
        if blocks > 1:
            kernel = handing_on(scatter_new(done, blocks - done, points, lat, strips), 1)
            total, load = call(kernel, [grid, shape(load.shape, F32)])(
                *total, new, owner, row, lon, load
            )
            total, done = (total,), blocks
        before, new = load, arrived
        load = jnp.concatenate([after_one if blocks == 1 else load, arrived], axis=0)
        if blocks == 1:
            new = load
        blocks, bit = blocks * 2, bit // 2

    padded = call(pad_planes, shape((8, cx + 4, ny, nz), F32))(following, next_a, next_b)
    grids = shape((count + count // 2, LANES), F32)
    mine = call(
        scatter_last(blocks, points, lat, strips),
        grids,
        [pltpu.VMEM((count, 2 * LANES), F32)],
        after=(padded,),
    )(*total, before, new, owner, row, lon)
    theirs = swap(mine, 1)

    cell_shape = shape((cx, ny, nz), F32)
    vector_shape = shape((3, cx, ny, nz), F32)
    new_density, new_velocity, new_field, new_pressure, end = call(
        stage_two, [cell_shape, vector_shape, vector_shape, cell_shape, shape((8, LANES), F32)]
    )(padded, half)

    potential, shell_potential = call(
        solve_and_read(blocks, points, lat, strips),
        [shape((lat, columns), F32), shape((points, LANES), F32)],
        [
            pltpu.VMEM((devices * lat + 2, strips, LANES), F32),
            pltpu.VMEM((5, devices * lat, strips, LANES), F32),
            pltpu.VMEM((2, devices * lat + 2, strips, LANES), F32),
        ],
        after=(end,),
    )(mine, theirs, owner, row, lon)
    return (
        new_density,
        new_velocity,
        new_field,
        new_pressure,
        potential,
        shell_potential.reshape(shell_count),
    )


def solution(mesh):
    both = ("parts", "mag")
    in_specs = (
        P(both, None, None),
        P(None, both, None, None),
        P(None, both, None, None),
        P(both, None, None),
        P(both, None),
        P("mag"),
        P(),
        P(),
        P(),
    )
    out_specs = (
        P(both, None, None),
        P(None, both, None, None),
        P(None, both, None, None),
        P(both, None, None),
        P(both, None),
        P(both),
    )
    return jax.shard_map(shards, mesh=mesh, in_specs=in_specs, out_specs=out_specs, check_vma=False)
```

```python
import jax
import jax.numpy as jnp
from jax import lax
from jax.experimental import pallas as pl
from jax.experimental.pallas import tpu as pltpu
from jax.sharding import PartitionSpec as P

SWEEPS = 4
ADIABATIC = 5.0 / 3.0
TIME_STEP = 0.02
LON_WEIGHT = 0.25
LEAK_RATE = 0.05
SOURCE_GAIN = 10.0
LANES = 128

F32 = jnp.float32
BF16 = jnp.bfloat16
I32 = jnp.int32
VMEM = pl.BlockSpec(memory_space=pltpu.VMEM)
ANY = pl.BlockSpec(memory_space=pl.ANY)
HBM = pl.BlockSpec(memory_space=pltpu.HBM)
MIB = 1024 * 1024


def call(kernel, outs, scratch=(), specs=None, after=()):
    many = isinstance(outs, (list, tuple))

    def body(*refs):
        kernel(*refs[len(after) :])

    def run(*operands):
        in_specs = [ANY] * len(after) + list(specs or [VMEM] * len(operands))
        return pallas(body if after else kernel, outs, many, scratch, in_specs)(*after, *operands)

    return run


def pallas(kernel, outs, many, scratch, in_specs):
    return pl.pallas_call(
        kernel,
        in_specs=in_specs,
        out_shape=outs,
        out_specs=[VMEM] * len(outs) if many else VMEM,
        scratch_shapes=list(scratch),
        compiler_params=pltpu.CompilerParams(
            vmem_limit_bytes=(32 if lax.axis_size("mag") <= 32 else 60) * MIB
        ),
    )


def pieces(values):
    first = values.astype(BF16)
    second = (values - first.astype(F32)).astype(BF16)
    return first, second


def rows_hot(key_row, count, group=256):
    lanes = key_row.shape[1]
    out = []
    for first in range(0, count, group):
        size = min(group, count - first)
        key = jnp.broadcast_to(key_row - first, (16, lanes)).astype(BF16)
        keys = jnp.concatenate([key] * (size // 16), axis=0)
        index = lax.broadcasted_iota(I32, (size, lanes), 0).astype(F32).astype(BF16)
        out.append(jnp.where(keys == index, jnp.ones((), BF16), jnp.zeros((), BF16)))
    return jnp.concatenate(out, axis=0) if len(out) > 1 else out[0]


def half_slope(lower, centre, upper):
    out = []
    for a, b, c in zip(lower, centre, upper):
        s, t = b - a, c - b
        out.append(0.5 * (jnp.maximum(jnp.minimum(s, t), 0.0) + jnp.minimum(jnp.maximum(s, t), 0.0)))
    return out


def dot3(a, b):
    return a[0] * b[0] + a[1] * b[1] + a[2] * b[2]


def conserved(q):
    rho, v, b, p = q[0], q[1:4], q[4:7], q[7]
    energy = p * (1.0 / (ADIABATIC - 1.0)) + 0.5 * rho * dot3(v, v) + 0.5 * dot3(b, b)
    return [rho, rho * v[0], rho * v[1], rho * v[2], b[0], b[1], b[2], energy]


def primitive(u):
    rho, b = u[0], u[4:7]
    inverse = 1.0 / rho
    v = [u[k] * inverse for k in (1, 2, 3)]
    p = (ADIABATIC - 1.0) * (u[7] - 0.5 * rho * dot3(v, v) - 0.5 * dot3(b, b))
    return [rho] + v + list(b) + [p]


def side(q, d):
    rho, v, b, p = q[0], q[1:4], q[4:7], q[7]
    b2 = dot3(b, b)
    half_b2 = 0.5 * b2
    total = p + half_b2
    mom = [rho * x for x in v]
    energy = p * (1.0 / (ADIABATIC - 1.0)) + 0.5 * dot3(mom, v) + half_b2
    vn, bn, mn = v[d], b[d], mom[d]
    flux = [mn]
    for k in range(3):
        f = mn * v[k] - bn * b[k]
        flux.append(f + total if k == d else f)
    for k in range(3):
        flux.append(None if k == d else vn * b[k] - bn * v[k])
    flux.append((energy + total) * vn - bn * dot3(v, b))
    speed = jnp.abs(vn) + jnp.sqrt((ADIABATIC * jnp.abs(p) + b2) / rho)
    return [rho] + mom + list(b) + [energy], flux, speed


def face(left, right, d):
    cons_l, flux_l, speed_l = side(left, d)
    cons_r, flux_r, speed_r = side(right, d)
    half_c = 0.5 * jnp.maximum(speed_l, speed_r)
    out = []
    for k in range(8):
        jump = half_c * (cons_r[k] - cons_l[k])
        out.append(-jump if flux_l[k] is None else 0.5 * (flux_l[k] + flux_r[k]) - jump)
    return out


def periodic(q, axis, d):
    size = q[0].shape[axis]
    back = [pltpu.roll(x, 1, axis) for x in q]
    ahead = [pltpu.roll(x, size - 1, axis) for x in q]
    slope = half_slope(back, q, ahead)
    left = [x + s for x, s in zip(q, slope)]
    right = [pltpu.roll(x - s, size - 1, axis) for x, s in zip(q, slope)]
    flux = face(left, right, d)
    return [pltpu.roll(f, 1, axis) - f for f in flux]


def add(a, b):
    return [x + y for x, y in zip(a, b)]


def plane(ref, x):
    return [ref[k, x] for k in range(8)]


def upper_face(ref, x):
    a, b, c, d = (plane(ref, x + k) for k in (-1, 0, 1, 2))
    left = add(b, half_slope(a, b, c))
    right = [v - s for v, s in zip(c, half_slope(b, c, d))]
    return face(left, right, 0)


def sideways(q):
    return add(periodic(q, 0, 1), periodic(q, 1, 2))


def sweep_planes(ref, first, count, put, others):
    def body(step, below):
        x = first + step
        above = upper_face(ref, x)
        q = plane(ref, x)
        change = [f - g for f, g in zip(below, above)]
        put(x, step, q, add(change, others(step, q)))
        return above

    lax.fori_loop(0, count, body, upper_face(ref, first - 1))


def stage_own(own_ref, side_ref):
    def body(x, carry):
        for k, value in enumerate(sideways(plane(own_ref, x))):
            side_ref[k, x] = value
        return carry

    lax.fori_loop(0, own_ref.shape[1], body, 0)


def stage_one(own_ref, eight_a, eight_b, own_side_ref, next_ref, half_ref, pad_ref, side_ref):
    me = lax.axis_index("mag")
    last = lax.axis_size("mag") - 1
    even = me % 2 == 0
    cx = own_ref.shape[1]
    for k in range(8):
        for x in range(cx):
            low = jnp.where(even, eight_b[k, x], eight_a[k, x])
            high = jnp.where(even, eight_a[k, x], eight_b[k, x])
            pad_ref[k, x] = jnp.where(me == 0, own_ref[k, 0], low)
            pad_ref[k, cx + x] = own_ref[k, x]
            pad_ref[k, 2 * cx + x] = jnp.where(me == last, own_ref[k, cx - 1], high)
            side_ref[k, 2 + x] = own_side_ref[k, x]

    def beside(i, carry):
        step = jnp.where(i < 2, i, cx + i)
        for k, value in enumerate(sideways(plane(pad_ref, cx - 2 + step))):
            side_ref[k, step] = value
        return carry

    lax.fori_loop(0, 4, beside, 0)

    def put(x, step, q, change):
        start = conserved(q)
        first = [s + TIME_STEP * c for s, c in zip(start, change)]
        q1 = primitive(first)
        for k in range(8):
            next_ref[k, step] = q1[k]

        @pl.when(jnp.logical_and(step >= 2, step < cx + 2))
        def _():
            for k in range(8):
                half_ref[k, step - 2] = 0.5 * (start[k] + first[k])

    sweep_planes(pad_ref, cx - 2, cx + 4, put, lambda step, q: plane(side_ref, step))

    @pl.when(me == 0)
    def _():
        for k in range(8):
            next_ref[k, 0] = next_ref[k, 2]
            next_ref[k, 1] = next_ref[k, 2]

    @pl.when(me == last)
    def _():
        for k in range(8):
            next_ref[k, cx + 2] = next_ref[k, cx + 1]
            next_ref[k, cx + 3] = next_ref[k, cx + 1]


def stage_two(next_ref, half_ref, rho_ref, vel_ref, mag_ref, prs_ref, end_ref):
    end_ref[...] = half_ref[0, 0, 0:8]
    cx = half_ref.shape[1]

    def put(x, step, q, change):
        final = [half_ref[k, step] + (0.5 * TIME_STEP) * change[k] for k in range(8)]
        q2 = primitive(final)
        rho_ref[step] = q2[0]
        for k in range(3):
            vel_ref[k, step] = q2[1 + k]
            mag_ref[k, step] = q2[4 + k]
        prs_ref[step] = q2[7]

    sweep_planes(next_ref, 2, cx, put, lambda step, q: sideways(q))


def pick_current(own_ref, cell_ref, strip_ref, edge_a, edge_b, out_ref, own_out):
    me = lax.axis_index("mag")
    last = lax.axis_size("mag") - 1
    even = me % 2 == 0
    cx, ny, nz = own_ref.shape[1:]
    own_out[...] = own_ref[...]
    rows = []
    for x in range(cx):
        bx, by, bz = (own_ref[4 + k, x] for k in range(3))

        def neighbour(k, step):
            if 0 <= x + step < cx:
                return own_ref[4 + k, x + step]
            if step < 0:
                below = jnp.where(even, edge_b[k - 1, 1], edge_a[k - 1, 1])
                return jnp.where(me == 0, own_ref[4 + k, x], below)
            above = jnp.where(even, edge_a[k - 1, 0], edge_b[k - 1, 0])
            return jnp.where(me == last, own_ref[4 + k, x], above)

        def along_x(k):
            return 0.5 * (neighbour(k, 1) - neighbour(k, -1))

        def along(v, axis):
            return 0.5 * (pltpu.roll(v, v.shape[axis] - 1, axis) - pltpu.roll(v, 1, axis))

        jx = along(bz, 0) - along(by, 1)
        jy = along(bx, 1) - along_x(2)
        jz = along_x(1) - along(bx, 0)
        norm = jnp.sqrt(bx * bx + by * by + bz * bz + 1.0)
        rows.append(SOURCE_GAIN * (jx * bx + jy * by + jz * bz) / norm)
    table = jnp.concatenate(rows, axis=0)
    count = table.shape[0]
    both = jnp.concatenate(pieces(table), axis=0)
    cells = cell_ref[...]
    hi, lo = cells // nz, (cells % nz).astype(F32)
    index = lax.broadcasted_iota(I32, (count, LANES), 0)
    points = cells.shape[0]
    for s in range(points):
        hot = rows_hot(lo[s : s + 1], nz)
        found = jnp.dot(both, hot, preferred_element_type=F32)
        found = found[:count] + found[count:]
        mine = jnp.where(index == hi[s : s + 1], found, 0.0)
        out_ref[s : s + 1, :] = jnp.sum(mine, axis=0, keepdims=True)
    out_ref[points:, :] = strip_ref[...]


def load_arguments(
    rho_ref, vel_ref, mag_ref, prs_ref, cell_ref, cond_ref, own_out, edge_out, cell_out, strip_out, rows, sems
):
    last = mag_ref.shape[1] - 1
    pairs = [
        (cond_ref, rows),
        (mag_ref.at[pl.ds(1, 2), pl.ds(0, 1)], edge_out.at[:, pl.ds(0, 1)]),
        (mag_ref.at[pl.ds(1, 2), pl.ds(last, 1)], edge_out.at[:, pl.ds(1, 1)]),
        (cell_ref, cell_out),
        (rho_ref, own_out.at[0]),
        (vel_ref, own_out.at[pl.ds(1, 3)]),
        (mag_ref, own_out.at[pl.ds(4, 3)]),
        (prs_ref, own_out.at[7]),
    ]
    copies = [
        pltpu.make_async_copy(source, target, sems.at[k])
        for k, (source, target) in enumerate(pairs)
    ]
    for copy in copies:
        copy.start()
    copies[0].wait()
    lat, columns = rows.shape
    strips = columns // LANES
    for r in range(lat):
        for strip in range(strips):
            place = r * strips + strip
            strip_out[place : place + 1, :] = rows[r : r + 1, strip * LANES : (strip + 1) * LANES]
    for copy in copies[1:]:
        copy.wait()


def east_of(v):
    lane = lax.broadcasted_iota(I32, v.shape, 2)
    turned = pltpu.roll(v, v.shape[2] - 1, 2)
    return jnp.where(lane == v.shape[2] - 1, pltpu.roll(turned, v.shape[1] - 1, 1), turned)


def west_of(v):
    lane = lax.broadcasted_iota(I32, v.shape, 2)
    turned = pltpu.roll(v, 1, 2)
    return jnp.where(lane == 0, pltpu.roll(turned, 1, 1), turned)


def scatter_block(value, hi, lo, count):
    hi, lo = hi.astype(F32), lo.astype(F32)
    high_piece = value.astype(BF16).astype(F32)
    low_piece = value - high_piece
    lefts, rights = [], []
    for s in range(value.shape[0]):
        lefts.append(rows_hot(hi[s : s + 1], count))
        hot = rows_hot(lo[s : s + 1], LANES)
        two = []
        for piece in (high_piece, low_piece):
            wide = jnp.broadcast_to(piece[s : s + 1], (16, LANES)).astype(BF16)
            two.append(hot * jnp.concatenate([wide] * (LANES // 16), axis=0))
        rights.append(jnp.concatenate(two, axis=0))
    left = jnp.concatenate(lefts, axis=1)
    right = jnp.concatenate(rights, axis=1)
    return lax.dot_general(left, right, (((1,), (1,)), ((), ())), preferred_element_type=F32)


def repeat(count, body):
    if count <= 8:
        for i in range(count):
            body(i)
    else:
        lax.fori_loop(0, count, lambda i, carry: (body(i), carry)[1], 0)


def origin(me, devices, j):
    mask, bit, k = 0, devices // 2, 0
    while bit > 1:
        mask = mask + ((j >> k) & 1) * bit
        bit, k = bit // 2, k + 1
    return jnp.bitwise_xor(me, mask)


def scatter_new(first, blocks, points, lat, strips):
    def kernel(*refs):
        *total_in, load_ref, owner_ref, row_ref, lon_ref, out_ref = refs
        me = lax.axis_index("mag")
        devices = lax.axis_size("mag")
        count = out_ref.shape[0]
        rows = min(count, 1024)
        stride = load_ref.shape[0] // blocks

        def part(j, g, base_ref):
            device = origin(me, devices, first + j)
            at = pl.ds(pl.multiple_of(device * points, points), points)
            value = load_ref[pl.ds(pl.multiple_of(j * stride, 8), points), :]
            hi = (owner_ref[at, :] * lat + row_ref[at, :]) * strips + lon_ref[at, :] // LANES
            lo = lon_ref[at, :] % LANES
            new = scatter_block(value, hi - g * rows, lo, rows)
            place = pl.ds(pl.multiple_of(g * rows, rows), rows)
            out_ref[place, :] = new if base_ref is None else base_ref[place, :] + new

        def group(g):
            part(0, g, total_in[0] if total_in else None)
            repeat(blocks - 1, lambda j: part(j + 1, g, out_ref))

        repeat(count // rows, group)

    return kernel


def handing_on(kernel, count):
    def run(*refs):
        outs = count + 1
        given = refs[-outs - count : -outs]
        for source, target in zip(given, refs[-count:]):
            target[...] = source[...]
        kernel(*refs[: -outs - count], refs[-outs])

    return run


def scatter_last(blocks, points, lat, strips):
    def kernel(total_ref, before_ref, load_ref, owner_ref, row_ref, lon_ref, out_ref, work_ref):
        half = blocks // 2
        scatter_new(half, half, points, lat, strips)(
            total_ref, load_ref, owner_ref, row_ref, lon_ref, work_ref
        )
        count = work_ref.shape[0]
        out_ref[:count, :] = work_ref[:, :LANES] + work_ref[:, LANES:]
        cells = lat * strips
        stride = points + cells
        for j in range(blocks):
            ref = before_ref if j < half else load_ref
            start = (j % half) * stride + points
            out_ref[count + j * cells : count + (j + 1) * cells, :] = ref[start : start + cells, :]

    return kernel


def solve_and_read(blocks, points, lat, strips):
    def kernel(
        mine_ref, their_ref, owner_ref, row_ref, lon_ref, flat_ref, out_ref, s_ref, w_ref, phi_ref
    ):
        me = lax.axis_index("mag")
        devices = lax.axis_size("mag")
        rows = devices * lat
        count = rows * strips
        cells = lat * strips
        zeros = jnp.zeros((1, strips, LANES), F32)
        for ref in (s_ref, phi_ref.at[0], phi_ref.at[1]):
            ref[0:1] = zeros
            ref[rows + 1 : rows + 2] = zeros

        def place(j):
            at = pl.ds(pl.multiple_of(count + j * cells, cells), cells)
            for ref, who in ((mine_ref, me), (their_ref, jnp.bitwise_xor(me, 1))):
                device = origin(who, devices, j)
                s_ref[pl.ds(device * lat + 1, lat)] = ref[at, :].reshape(lat, strips, LANES)

        repeat(blocks, place)
        chunk = min(8, rows)

        def prepare(i):
            r = i * chunk
            s, above, below = (s_ref[pl.ds(r + k, chunk)] for k in (1, 0, 2))
            north, south = 0.5 * (s + above), 0.5 * (s + below)
            east = (0.5 * LON_WEIGHT) * (s + east_of(s))
            west = (0.5 * LON_WEIGHT) * (s + west_of(s))
            inverse = 1.0 / (north + south + east + west + LEAK_RATE * s)
            at = pl.ds(pl.multiple_of(r * strips, 8), chunk * strips)
            source = (mine_ref[at, :] + their_ref[at, :]).reshape(chunk, strips, LANES)
            for k, value in enumerate((source, north, south, east, west)):
                w_ref[k, pl.ds(r, chunk)] = value * inverse
            phi_ref[0, pl.ds(r + 1, chunk)] = source * inverse

        repeat(rows // chunk, prepare)
        for sweep in range(SWEEPS - 1):
            old, new = sweep % 2, 1 - sweep % 2

            def relax(i):
                r = i * chunk
                phi, above, below = (phi_ref[old, pl.ds(r + k, chunk)] for k in (1, 0, 2))
                source, north, south, east, west = (w_ref[k, pl.ds(r, chunk)] for k in range(5))
                phi_ref[new, pl.ds(r + 1, chunk)] = (
                    source
                    + north * above
                    + south * below
                    + east * east_of(phi)
                    + west * west_of(phi)
                )

            repeat(rows // chunk, relax)
        last = (SWEEPS - 1) % 2
        own = phi_ref[last, pl.ds(me * lat + 1, lat)]
        for strip in range(strips):
            flat_ref[:, strip * LANES : (strip + 1) * LANES] = own[:, strip, :]

        block = min(256, count)
        groups = count // block
        table = phi_ref[last, pl.ds(1, rows)].reshape(count, LANES)
        table = jnp.concatenate([table[g * block : (g + 1) * block] for g in range(groups)], axis=1)
        both = jnp.concatenate(pieces(table), axis=0)
        at = pl.ds(pl.multiple_of(me * points, points), points)
        owner, row, lon = owner_ref[at, :], row_ref[at, :], lon_ref[at, :]
        hi = (owner * lat + row) * strips + lon // LANES
        group, hi, lo = hi // block, hi % block, lon % LANES
        index = lax.broadcasted_iota(I32, (block, LANES), 0)
        columns = []
        for p in range(points):
            stack = []
            for g in range(groups):
                key = jnp.where(group[p : p + 1] == g, lo[p : p + 1], -1).astype(F32)
                stack.append(rows_hot(key, LANES))
            columns.append(jnp.concatenate(stack, axis=0))
        found = jnp.dot(both, jnp.concatenate(columns, axis=1), preferred_element_type=F32)
        found = found[:block] + found[block:]
        for p in range(points):
            part = found[:, p * LANES : (p + 1) * LANES]
            part = jnp.where(index == hi[p : p + 1], part, 0.0)
            out_ref[p : p + 1, :] = jnp.sum(part, axis=0, keepdims=True)

    return kernel


def swap(values, bit):
    devices = lax.axis_size("mag")
    return lax.ppermute(values, "mag", [(i, i ^ bit) for i in range(devices)])


def swap_next(values):
    devices = lax.axis_size("mag")
    pairs = [(i, (i + (1 if i % 2 else -1)) % devices) for i in range(devices)]
    return lax.ppermute(values, "mag", pairs)


def shards(
    density, velocity, mag_field, pressure, conductance, shell_cell, foot_owner, foot_row, foot_lon
):
    devices = lax.axis_size("mag")
    cx, ny, nz = density.shape
    lat, columns = conductance.shape
    strips = columns // LANES
    shell_count = shell_cell.shape[0]
    points = shell_count // LANES
    cells = lat * strips
    count = devices * cells
    shape = jax.ShapeDtypeStruct

    tile = shape((points, LANES), I32)
    slab = shape((8, cx, ny, nz), F32)
    own, edge, cell, strip = call(
        load_arguments,
        [slab, shape((2, 2, ny, nz), F32), tile, shape((cells, LANES), F32)],
        [pltpu.VMEM((lat, columns), F32), pltpu.SemaphoreType.DMA((8,))],
        [HBM] * 6,
    )(
        *(
            pltpu.with_memory_space_constraint(x, pltpu.HBM)
            for x in (
                density,
                velocity,
                mag_field,
                pressure,
                shell_cell.reshape(-1, LANES),
                conductance,
            )
        )
    )
    edge_a, edge_b = swap(edge, 1), swap_next(edge)
    own_side = call(stage_own, slab)(own)

    owner = foot_owner.reshape(-1, LANES)
    row = foot_row.reshape(-1, LANES)
    lon = foot_lon.reshape(-1, LANES)

    load, own = call(
        pick_current, [shape((points + cells, LANES), F32), slab], after=(own_side,)
    )(own, cell, strip, edge_a, edge_b)
    eight_a, eight_b = swap(own, 1), swap_next(own)

    grid = shape((count, 2 * LANES), F32)
    total, blocks, done = (), 1, 0
    bit = devices // 2
    while bit > 1:
        arrived = swap(load, bit)
        if blocks > 1:
            kernel = handing_on(scatter_new(done, blocks - done, points, lat, strips), 1)
            total, load = call(kernel, [grid, shape(load.shape, F32)])(
                *total, new, owner, row, lon, load
            )
            total, done = (total,), blocks
        before, new = load, arrived
        load = jnp.concatenate([load, arrived], axis=0)
        if blocks == 1:
            new = load
        blocks, bit = blocks * 2, bit // 2

    following, half = call(
        stage_one,
        [shape((8, cx + 4, ny, nz), F32), slab],
        [pltpu.VMEM((8, 3 * cx, ny, nz), F32), pltpu.VMEM((8, cx + 4, ny, nz), F32)],
    )(own, eight_a, eight_b, own_side)

    grids = shape((count + count // 2, LANES), F32)
    mine = call(
        scatter_last(blocks, points, lat, strips),
        grids,
        [pltpu.VMEM((count, 2 * LANES), F32)],
        after=(half,),
    )(*total, before, new, owner, row, lon)
    theirs = swap(mine, 1)

    cell_shape = shape((cx, ny, nz), F32)
    vector_shape = shape((3, cx, ny, nz), F32)
    new_density, new_velocity, new_field, new_pressure, end = call(
        stage_two, [cell_shape, vector_shape, vector_shape, cell_shape, shape((8, LANES), F32)]
    )(following, half)

    potential, shell_potential = call(
        solve_and_read(blocks, points, lat, strips),
        [shape((lat, columns), F32), shape((points, LANES), F32)],
        [
            pltpu.VMEM((devices * lat + 2, strips, LANES), F32),
            pltpu.VMEM((5, devices * lat, strips, LANES), F32),
            pltpu.VMEM((2, devices * lat + 2, strips, LANES), F32),
        ],
        after=(end,),
    )(mine, theirs, owner, row, lon)
    return (
        new_density,
        new_velocity,
        new_field,
        new_pressure,
        potential,
        shell_potential.reshape(shell_count),
    )


def solution(mesh):
    both = ("parts", "mag")
    in_specs = (
        P(both, None, None),
        P(None, both, None, None),
        P(None, both, None, None),
        P(both, None, None),
        P(both, None),
        P("mag"),
        P(),
        P(),
        P(),
    )
    out_specs = (
        P(both, None, None),
        P(None, both, None, None),
        P(None, both, None, None),
        P(both, None, None),
        P(both, None),
        P(both),
    )
    return jax.shard_map(shards, mesh=mesh, in_specs=in_specs, out_specs=out_specs, check_vma=False)
```

```python
import jax
import jax.numpy as jnp
from jax import lax
from jax.experimental import pallas as pl
from jax.experimental.pallas import tpu as pltpu
from jax.sharding import PartitionSpec as P

SWEEPS = 4
ADIABATIC = 5.0 / 3.0
TIME_STEP = 0.02
LON_WEIGHT = 0.25
LEAK_RATE = 0.05
SOURCE_GAIN = 10.0
LANES = 128

F32 = jnp.float32
BF16 = jnp.bfloat16
I32 = jnp.int32
VMEM = pl.BlockSpec(memory_space=pltpu.VMEM)
ANY = pl.BlockSpec(memory_space=pl.ANY)
HBM = pl.BlockSpec(memory_space=pltpu.HBM)
MIB = 1024 * 1024


def call(kernel, outs, scratch=(), specs=None, after=()):
    many = isinstance(outs, (list, tuple))

    def body(*refs):
        kernel(*refs[len(after) :])

    def run(*operands):
        in_specs = [ANY] * len(after) + list(specs or [VMEM] * len(operands))
        return pallas(body if after else kernel, outs, many, scratch, in_specs)(*after, *operands)

    return run


def pallas(kernel, outs, many, scratch, in_specs):
    return pl.pallas_call(
        kernel,
        in_specs=in_specs,
        out_shape=outs,
        out_specs=[VMEM] * len(outs) if many else VMEM,
        scratch_shapes=list(scratch),
        compiler_params=pltpu.CompilerParams(
            vmem_limit_bytes=(32 if lax.axis_size("mag") <= 32 else 60) * MIB
        ),
    )


def pieces(values):
    first = values.astype(BF16)
    second = (values - first.astype(F32)).astype(BF16)
    return first, second


def rows_hot(key_row, count, group=256):
    lanes = key_row.shape[1]
    out = []
    for first in range(0, count, group):
        size = min(group, count - first)
        key = jnp.broadcast_to(key_row - first, (16, lanes)).astype(BF16)
        keys = jnp.concatenate([key] * (size // 16), axis=0)
        index = lax.broadcasted_iota(I32, (size, lanes), 0).astype(F32).astype(BF16)
        out.append(jnp.where(keys == index, jnp.ones((), BF16), jnp.zeros((), BF16)))
    return jnp.concatenate(out, axis=0) if len(out) > 1 else out[0]


def half_slope(lower, centre, upper):
    out = []
    for a, b, c in zip(lower, centre, upper):
        s, t = b - a, c - b
        out.append(0.5 * (jnp.maximum(jnp.minimum(s, t), 0.0) + jnp.minimum(jnp.maximum(s, t), 0.0)))
    return out


def dot3(a, b):
    return a[0] * b[0] + a[1] * b[1] + a[2] * b[2]


def conserved(q):
    rho, v, b, p = q[0], q[1:4], q[4:7], q[7]
    energy = p * (1.0 / (ADIABATIC - 1.0)) + 0.5 * rho * dot3(v, v) + 0.5 * dot3(b, b)
    return [rho, rho * v[0], rho * v[1], rho * v[2], b[0], b[1], b[2], energy]


def primitive(u):
    rho, b = u[0], u[4:7]
    inverse = 1.0 / rho
    v = [u[k] * inverse for k in (1, 2, 3)]
    p = (ADIABATIC - 1.0) * (u[7] - 0.5 * rho * dot3(v, v) - 0.5 * dot3(b, b))
    return [rho] + v + list(b) + [p]


def side(q, d):
    rho, v, b, p = q[0], q[1:4], q[4:7], q[7]
    b2 = dot3(b, b)
    half_b2 = 0.5 * b2
    total = p + half_b2
    mom = [rho * x for x in v]
    energy = p * (1.0 / (ADIABATIC - 1.0)) + 0.5 * dot3(mom, v) + half_b2
    vn, bn, mn = v[d], b[d], mom[d]
    flux = [mn]
    for k in range(3):
        f = mn * v[k] - bn * b[k]
        flux.append(f + total if k == d else f)
    for k in range(3):
        flux.append(None if k == d else vn * b[k] - bn * v[k])
    flux.append((energy + total) * vn - bn * dot3(v, b))
    speed = jnp.abs(vn) + jnp.sqrt((ADIABATIC * jnp.abs(p) + b2) / rho)
    return [rho] + mom + list(b) + [energy], flux, speed


def face(left, right, d):
    cons_l, flux_l, speed_l = side(left, d)
    cons_r, flux_r, speed_r = side(right, d)
    half_c = 0.5 * jnp.maximum(speed_l, speed_r)
    out = []
    for k in range(8):
        jump = half_c * (cons_r[k] - cons_l[k])
        out.append(-jump if flux_l[k] is None else 0.5 * (flux_l[k] + flux_r[k]) - jump)
    return out


def periodic(q, axis, d):
    size = q[0].shape[axis]
    back = [pltpu.roll(x, 1, axis) for x in q]
    ahead = [pltpu.roll(x, size - 1, axis) for x in q]
    slope = half_slope(back, q, ahead)
    left = [x + s for x, s in zip(q, slope)]
    right = [pltpu.roll(x - s, size - 1, axis) for x, s in zip(q, slope)]
    flux = face(left, right, d)
    return [pltpu.roll(f, 1, axis) - f for f in flux]


def add(a, b):
    return [x + y for x, y in zip(a, b)]


def plane(ref, x):
    return [ref[k, x] for k in range(8)]


def upper_face(ref, x):
    a, b, c, d = (plane(ref, x + k) for k in (-1, 0, 1, 2))
    left = add(b, half_slope(a, b, c))
    right = [v - s for v, s in zip(c, half_slope(b, c, d))]
    return face(left, right, 0)


def sideways(q):
    return add(periodic(q, 0, 1), periodic(q, 1, 2))


def sweep_planes(ref, first, count, put, others):
    def body(step, below):
        x = first + step
        above = upper_face(ref, x)
        q = plane(ref, x)
        change = [f - g for f, g in zip(below, above)]
        put(x, step, q, add(change, others(step, q)))
        return above

    lax.fori_loop(0, count, body, upper_face(ref, first - 1))


def stage_own(own_ref, side_ref):
    def body(x, carry):
        for k, value in enumerate(sideways(plane(own_ref, x))):
            side_ref[k, x] = value
        return carry

    lax.fori_loop(0, own_ref.shape[1], body, 0)


def stage_one(own_ref, eight_a, eight_b, own_side_ref, next_ref, half_ref, pad_ref, side_ref):
    me = lax.axis_index("mag")
    last = lax.axis_size("mag") - 1
    even = me % 2 == 0
    cx = own_ref.shape[1]
    for k in range(8):
        for x in range(cx):
            low = jnp.where(even, eight_b[k, x], eight_a[k, x])
            high = jnp.where(even, eight_a[k, x], eight_b[k, x])
            pad_ref[k, x] = jnp.where(me == 0, own_ref[k, 0], low)
            pad_ref[k, cx + x] = own_ref[k, x]
            pad_ref[k, 2 * cx + x] = jnp.where(me == last, own_ref[k, cx - 1], high)
            side_ref[k, 2 + x] = own_side_ref[k, x]

    def beside(i, carry):
        step = jnp.where(i < 2, i, cx + i)
        for k, value in enumerate(sideways(plane(pad_ref, cx - 2 + step))):
            side_ref[k, step] = value
        return carry

    lax.fori_loop(0, 4, beside, 0)

    def put(x, step, q, change):
        start = conserved(q)
        first = [s + TIME_STEP * c for s, c in zip(start, change)]
        q1 = primitive(first)
        for k in range(8):
            next_ref[k, step] = q1[k]

        @pl.when(jnp.logical_and(step >= 2, step < cx + 2))
        def _():
            for k in range(8):
                half_ref[k, step - 2] = 0.5 * (start[k] + first[k])

    sweep_planes(pad_ref, cx - 2, cx + 4, put, lambda step, q: plane(side_ref, step))

    @pl.when(me == 0)
    def _():
        for k in range(8):
            next_ref[k, 0] = next_ref[k, 2]
            next_ref[k, 1] = next_ref[k, 2]

    @pl.when(me == last)
    def _():
        for k in range(8):
            next_ref[k, cx + 2] = next_ref[k, cx + 1]
            next_ref[k, cx + 3] = next_ref[k, cx + 1]


def stage_two(next_ref, half_ref, rho_ref, vel_ref, mag_ref, prs_ref, end_ref):
    end_ref[...] = half_ref[0, 0, 0:8]
    cx = half_ref.shape[1]

    def put(x, step, q, change):
        final = [half_ref[k, step] + (0.5 * TIME_STEP) * change[k] for k in range(8)]
        q2 = primitive(final)
        rho_ref[step] = q2[0]
        for k in range(3):
            vel_ref[k, step] = q2[1 + k]
            mag_ref[k, step] = q2[4 + k]
        prs_ref[step] = q2[7]

    sweep_planes(next_ref, 2, cx, put, lambda step, q: sideways(q))


def pick_current(own_ref, cell_ref, strip_ref, edge_a, edge_b, out_ref):
    me = lax.axis_index("mag")
    last = lax.axis_size("mag") - 1
    even = me % 2 == 0
    cx, ny, nz = own_ref.shape[1:]
    rows = []
    for x in range(cx):
        bx, by, bz = (own_ref[4 + k, x] for k in range(3))

        def neighbour(k, step):
            if 0 <= x + step < cx:
                return own_ref[4 + k, x + step]
            if step < 0:
                below = jnp.where(even, edge_b[k - 1, 1], edge_a[k - 1, 1])
                return jnp.where(me == 0, own_ref[4 + k, x], below)
            above = jnp.where(even, edge_a[k - 1, 0], edge_b[k - 1, 0])
            return jnp.where(me == last, own_ref[4 + k, x], above)

        def along_x(k):
            return 0.5 * (neighbour(k, 1) - neighbour(k, -1))

        def along(v, axis):
            return 0.5 * (pltpu.roll(v, v.shape[axis] - 1, axis) - pltpu.roll(v, 1, axis))

        jx = along(bz, 0) - along(by, 1)
        jy = along(bx, 1) - along_x(2)
        jz = along_x(1) - along(bx, 0)
        norm = jnp.sqrt(bx * bx + by * by + bz * bz + 1.0)
        rows.append(SOURCE_GAIN * (jx * bx + jy * by + jz * bz) / norm)
    table = jnp.concatenate(rows, axis=0)
    count = table.shape[0]
    both = jnp.concatenate(pieces(table), axis=0)
    cells = cell_ref[...]
    hi, lo = cells // nz, (cells % nz).astype(F32)
    index = lax.broadcasted_iota(I32, (count, LANES), 0)
    points = cells.shape[0]
    for s in range(points):
        hot = rows_hot(lo[s : s + 1], nz)
        found = jnp.dot(both, hot, preferred_element_type=F32)
        found = found[:count] + found[count:]
        mine = jnp.where(index == hi[s : s + 1], found, 0.0)
        out_ref[s : s + 1, :] = jnp.sum(mine, axis=0, keepdims=True)
    out_ref[points:, :] = strip_ref[...]


def load_arguments(
    rho_ref, vel_ref, mag_ref, prs_ref, cell_ref, cond_ref, own_out, edge_out, cell_out, strip_out, rows, sems
):
    last = mag_ref.shape[1] - 1
    pairs = [
        (cond_ref, rows),
        (mag_ref.at[pl.ds(1, 2), pl.ds(0, 1)], edge_out.at[:, pl.ds(0, 1)]),
        (mag_ref.at[pl.ds(1, 2), pl.ds(last, 1)], edge_out.at[:, pl.ds(1, 1)]),
        (cell_ref, cell_out),
        (rho_ref, own_out.at[0]),
        (vel_ref, own_out.at[pl.ds(1, 3)]),
        (mag_ref, own_out.at[pl.ds(4, 3)]),
        (prs_ref, own_out.at[7]),
    ]
    copies = [
        pltpu.make_async_copy(source, target, sems.at[k])
        for k, (source, target) in enumerate(pairs)
    ]
    for copy in copies:
        copy.start()
    copies[0].wait()
    lat, columns = rows.shape
    strips = columns // LANES
    for r in range(lat):
        for strip in range(strips):
            place = r * strips + strip
            strip_out[place : place + 1, :] = rows[r : r + 1, strip * LANES : (strip + 1) * LANES]
    for copy in copies[1:]:
        copy.wait()


def east_of(v):
    lane = lax.broadcasted_iota(I32, v.shape, 2)
    turned = pltpu.roll(v, v.shape[2] - 1, 2)
    return jnp.where(lane == v.shape[2] - 1, pltpu.roll(turned, v.shape[1] - 1, 1), turned)


def west_of(v):
    lane = lax.broadcasted_iota(I32, v.shape, 2)
    turned = pltpu.roll(v, 1, 2)
    return jnp.where(lane == 0, pltpu.roll(turned, 1, 1), turned)


def scatter_block(value, hi, lo, count):
    hi, lo = hi.astype(F32), lo.astype(F32)
    high_piece = value.astype(BF16).astype(F32)
    low_piece = value - high_piece
    lefts, rights = [], []
    for s in range(value.shape[0]):
        lefts.append(rows_hot(hi[s : s + 1], count))
        hot = rows_hot(lo[s : s + 1], LANES)
        two = []
        for piece in (high_piece, low_piece):
            wide = jnp.broadcast_to(piece[s : s + 1], (16, LANES)).astype(BF16)
            two.append(hot * jnp.concatenate([wide] * (LANES // 16), axis=0))
        rights.append(jnp.concatenate(two, axis=0))
    left = jnp.concatenate(lefts, axis=1)
    right = jnp.concatenate(rights, axis=1)
    return lax.dot_general(left, right, (((1,), (1,)), ((), ())), preferred_element_type=F32)


def repeat(count, body):
    if count <= 8:
        for i in range(count):
            body(i)
    else:
        lax.fori_loop(0, count, lambda i, carry: (body(i), carry)[1], 0)


def origin(me, devices, j):
    mask, bit, k = 0, devices // 2, 0
    while bit > 1:
        mask = mask + ((j >> k) & 1) * bit
        bit, k = bit // 2, k + 1
    return jnp.bitwise_xor(me, mask)


def scatter_new(first, blocks, held, base, points, lat, strips):
    def kernel(*refs):
        *total_in, load_ref, owner_ref, row_ref, lon_ref, out_ref = refs
        me = lax.axis_index("mag")
        devices = lax.axis_size("mag")
        count = out_ref.shape[0]
        rows = min(count, 1024)
        stride = load_ref.shape[0] // held

        def part(j, g, base_ref):
            device = origin(me, devices, first + j)
            at = pl.ds(pl.multiple_of(device * points, points), points)
            start = (first - base + j) * stride
            value = load_ref[pl.ds(pl.multiple_of(start, 8), points), :]
            hi = (owner_ref[at, :] * lat + row_ref[at, :]) * strips + lon_ref[at, :] // LANES
            lo = lon_ref[at, :] % LANES
            new = scatter_block(value, hi - g * rows, lo, rows)
            place = pl.ds(pl.multiple_of(g * rows, rows), rows)
            out_ref[place, :] = new if base_ref is None else base_ref[place, :] + new

        def group(g):
            part(0, g, total_in[0] if total_in else None)
            repeat(blocks - 1, lambda j: part(j + 1, g, out_ref))

        repeat(count // rows, group)

    return kernel


def handing_on(kernel, count):
    def run(*refs):
        outs = count + 1
        given = refs[-outs - count : -outs]
        for source, target in zip(given, refs[-count:]):
            target[...] = source[...]
        kernel(*refs[: -outs - count], refs[-outs])

    return run


def join(first_ref, second_ref, own_ref, out_ref, own_out):
    size = first_ref.shape[0]
    out_ref[:size, :] = first_ref[...]
    out_ref[size:, :] = second_ref[...]
    own_out[...] = own_ref[...]


def scatter_last(blocks, points, lat, strips):
    def kernel(total_ref, before_ref, load_ref, owner_ref, row_ref, lon_ref, out_ref, work_ref):
        half = blocks // 2
        scatter_new(half, half, half, half, points, lat, strips)(
            total_ref, load_ref, owner_ref, row_ref, lon_ref, work_ref
        )
        count = work_ref.shape[0]
        out_ref[:count, :] = work_ref[:, :LANES] + work_ref[:, LANES:]
        cells = lat * strips
        stride = points + cells
        for j in range(blocks):
            ref = before_ref if j < half else load_ref
            start = (j % half) * stride + points
            out_ref[count + j * cells : count + (j + 1) * cells, :] = ref[start : start + cells, :]

    return kernel


def solve_and_read(blocks, points, lat, strips):
    def kernel(
        mine_ref, their_ref, owner_ref, row_ref, lon_ref, flat_ref, out_ref, s_ref, w_ref, phi_ref
    ):
        me = lax.axis_index("mag")
        devices = lax.axis_size("mag")
        rows = devices * lat
        count = rows * strips
        cells = lat * strips
        zeros = jnp.zeros((1, strips, LANES), F32)
        for ref in (s_ref, phi_ref.at[0], phi_ref.at[1]):
            ref[0:1] = zeros
            ref[rows + 1 : rows + 2] = zeros

        def place(j):
            at = pl.ds(pl.multiple_of(count + j * cells, cells), cells)
            for ref, who in ((mine_ref, me), (their_ref, jnp.bitwise_xor(me, 1))):
                device = origin(who, devices, j)
                s_ref[pl.ds(device * lat + 1, lat)] = ref[at, :].reshape(lat, strips, LANES)

        repeat(blocks, place)
        chunk = min(8, rows)

        def prepare(i):
            r = i * chunk
            s, above, below = (s_ref[pl.ds(r + k, chunk)] for k in (1, 0, 2))
            north, south = 0.5 * (s + above), 0.5 * (s + below)
            east = (0.5 * LON_WEIGHT) * (s + east_of(s))
            west = (0.5 * LON_WEIGHT) * (s + west_of(s))
            inverse = 1.0 / (north + south + east + west + LEAK_RATE * s)
            at = pl.ds(pl.multiple_of(r * strips, 8), chunk * strips)
            source = (mine_ref[at, :] + their_ref[at, :]).reshape(chunk, strips, LANES)
            for k, value in enumerate((source, north, south, east, west)):
                w_ref[k, pl.ds(r, chunk)] = value * inverse
            phi_ref[0, pl.ds(r + 1, chunk)] = source * inverse

        repeat(rows // chunk, prepare)
        for sweep in range(SWEEPS - 1):
            old, new = sweep % 2, 1 - sweep % 2

            def relax(i):
                r = i * chunk
                phi, above, below = (phi_ref[old, pl.ds(r + k, chunk)] for k in (1, 0, 2))
                source, north, south, east, west = (w_ref[k, pl.ds(r, chunk)] for k in range(5))
                phi_ref[new, pl.ds(r + 1, chunk)] = (
                    source
                    + north * above
                    + south * below
                    + east * east_of(phi)
                    + west * west_of(phi)
                )

            repeat(rows // chunk, relax)
        last = (SWEEPS - 1) % 2
        own = phi_ref[last, pl.ds(me * lat + 1, lat)]
        for strip in range(strips):
            flat_ref[:, strip * LANES : (strip + 1) * LANES] = own[:, strip, :]

        block = min(256, count)
        groups = count // block
        table = phi_ref[last, pl.ds(1, rows)].reshape(count, LANES)
        table = jnp.concatenate([table[g * block : (g + 1) * block] for g in range(groups)], axis=1)
        both = jnp.concatenate(pieces(table), axis=0)
        at = pl.ds(pl.multiple_of(me * points, points), points)
        owner, row, lon = owner_ref[at, :], row_ref[at, :], lon_ref[at, :]
        hi = (owner * lat + row) * strips + lon // LANES
        group, hi, lo = hi // block, hi % block, lon % LANES
        index = lax.broadcasted_iota(I32, (block, LANES), 0)
        columns = []
        for p in range(points):
            stack = []
            for g in range(groups):
                key = jnp.where(group[p : p + 1] == g, lo[p : p + 1], -1).astype(F32)
                stack.append(rows_hot(key, LANES))
            columns.append(jnp.concatenate(stack, axis=0))
        found = jnp.dot(both, jnp.concatenate(columns, axis=1), preferred_element_type=F32)
        found = found[:block] + found[block:]
        for p in range(points):
            part = found[:, p * LANES : (p + 1) * LANES]
            part = jnp.where(index == hi[p : p + 1], part, 0.0)
            out_ref[p : p + 1, :] = jnp.sum(part, axis=0, keepdims=True)

    return kernel


def swap(values, bit):
    devices = lax.axis_size("mag")
    return lax.ppermute(values, "mag", [(i, i ^ bit) for i in range(devices)])


def swap_next(values):
    devices = lax.axis_size("mag")
    pairs = [(i, (i + (1 if i % 2 else -1)) % devices) for i in range(devices)]
    return lax.ppermute(values, "mag", pairs)


def shards(
    density, velocity, mag_field, pressure, conductance, shell_cell, foot_owner, foot_row, foot_lon
):
    devices = lax.axis_size("mag")
    cx, ny, nz = density.shape
    lat, columns = conductance.shape
    strips = columns // LANES
    shell_count = shell_cell.shape[0]
    points = shell_count // LANES
    cells = lat * strips
    count = devices * cells
    shape = jax.ShapeDtypeStruct

    tile = shape((points, LANES), I32)
    slab = shape((8, cx, ny, nz), F32)
    own, edge, cell, strip = call(
        load_arguments,
        [slab, shape((2, 2, ny, nz), F32), tile, shape((cells, LANES), F32)],
        [pltpu.VMEM((lat, columns), F32), pltpu.SemaphoreType.DMA((8,))],
        [HBM] * 6,
    )(
        *(
            pltpu.with_memory_space_constraint(x, pltpu.HBM)
            for x in (
                density,
                velocity,
                mag_field,
                pressure,
                shell_cell.reshape(-1, LANES),
                conductance,
            )
        )
    )
    edge_a, edge_b = swap(edge, 1), swap_next(edge)
    own_side = call(stage_own, slab)(own)

    owner = foot_owner.reshape(-1, LANES)
    row = foot_row.reshape(-1, LANES)
    lon = foot_lon.reshape(-1, LANES)

    load = call(pick_current, shape((points + cells, LANES), F32), after=(own_side,))(
        own, cell, strip, edge_a, edge_b
    )

    grid = shape((count, 2 * LANES), F32)
    total, blocks, done = (), 1, 0
    bit = devices // 2
    while bit > 1:
        arrived = swap(load, bit)
        if blocks != 2:
            kernel = handing_on(scatter_new(done, blocks - done, blocks, 0, points, lat, strips), 1)
            total, load = call(kernel, [grid, shape(load.shape, F32)])(
                *total, load, owner, row, lon, load
            )
            total, done = (total,), blocks
        before, new = load, arrived
        if blocks == 1:
            load, own_too = call(join, [shape((2 * (points + cells), LANES), F32), slab])(
                load, arrived, own
            )
            eight_a, eight_b = swap(own_too, 1), swap_next(own_too)
        else:
            load = jnp.concatenate([load, arrived], axis=0)
        blocks, bit = blocks * 2, bit // 2

    following, half = call(
        stage_one,
        [shape((8, cx + 4, ny, nz), F32), slab],
        [pltpu.VMEM((8, 3 * cx, ny, nz), F32), pltpu.VMEM((8, cx + 4, ny, nz), F32)],
    )(own, eight_a, eight_b, own_side)

    grids = shape((count + count // 2, LANES), F32)
    mine = call(
        scatter_last(blocks, points, lat, strips),
        grids,
        [pltpu.VMEM((count, 2 * LANES), F32)],
        after=(half,),
    )(*total, before, new, owner, row, lon)
    theirs = swap(mine, 1)

    cell_shape = shape((cx, ny, nz), F32)
    vector_shape = shape((3, cx, ny, nz), F32)
    new_density, new_velocity, new_field, new_pressure, end = call(
        stage_two, [cell_shape, vector_shape, vector_shape, cell_shape, shape((8, LANES), F32)]
    )(following, half)

    potential, shell_potential = call(
        solve_and_read(blocks, points, lat, strips),
        [shape((lat, columns), F32), shape((points, LANES), F32)],
        [
            pltpu.VMEM((devices * lat + 2, strips, LANES), F32),
            pltpu.VMEM((5, devices * lat, strips, LANES), F32),
            pltpu.VMEM((2, devices * lat + 2, strips, LANES), F32),
        ],
        after=(end,),
    )(mine, theirs, owner, row, lon)
    return (
        new_density,
        new_velocity,
        new_field,
        new_pressure,
        potential,
        shell_potential.reshape(shell_count),
    )


def solution(mesh):
    both = ("parts", "mag")
    in_specs = (
        P(both, None, None),
        P(None, both, None, None),
        P(None, both, None, None),
        P(both, None, None),
        P(both, None),
        P("mag"),
        P(),
        P(),
        P(),
    )
    out_specs = (
        P(both, None, None),
        P(None, both, None, None),
        P(None, both, None, None),
        P(both, None, None),
        P(both, None),
        P(both),
    )
    return jax.shard_map(shards, mesh=mesh, in_specs=in_specs, out_specs=out_specs, check_vma=False)
```

```python
import jax
import jax.numpy as jnp
from jax import lax
from jax.experimental import pallas as pl
from jax.experimental.pallas import tpu as pltpu
from jax.sharding import PartitionSpec as P

SWEEPS = 4
ADIABATIC = 5.0 / 3.0
TIME_STEP = 0.02
LON_WEIGHT = 0.25
LEAK_RATE = 0.05
SOURCE_GAIN = 10.0
LANES = 128

F32 = jnp.float32
BF16 = jnp.bfloat16
I32 = jnp.int32
VMEM = pl.BlockSpec(memory_space=pltpu.VMEM)
ANY = pl.BlockSpec(memory_space=pl.ANY)
HBM = pl.BlockSpec(memory_space=pltpu.HBM)
MIB = 1024 * 1024


def call(kernel, outs, scratch=(), specs=None, after=()):
    many = isinstance(outs, (list, tuple))

    def body(*refs):
        kernel(*refs[len(after) :])

    def run(*operands):
        in_specs = [ANY] * len(after) + list(specs or [VMEM] * len(operands))
        return pallas(body if after else kernel, outs, many, scratch, in_specs)(*after, *operands)

    return run


def pallas(kernel, outs, many, scratch, in_specs):
    return pl.pallas_call(
        kernel,
        in_specs=in_specs,
        out_shape=outs,
        out_specs=[VMEM] * len(outs) if many else VMEM,
        scratch_shapes=list(scratch),
        compiler_params=pltpu.CompilerParams(
            vmem_limit_bytes=(32 if lax.axis_size("mag") <= 32 else 60) * MIB
        ),
    )


def pieces(values):
    first = values.astype(BF16)
    second = (values - first.astype(F32)).astype(BF16)
    return first, second


def rows_hot(key_row, count, group=256):
    lanes = key_row.shape[1]
    out = []
    for first in range(0, count, group):
        size = min(group, count - first)
        key = jnp.broadcast_to(key_row - first, (16, lanes)).astype(BF16)
        keys = jnp.concatenate([key] * (size // 16), axis=0)
        index = lax.broadcasted_iota(I32, (size, lanes), 0).astype(F32).astype(BF16)
        out.append(jnp.where(keys == index, jnp.ones((), BF16), jnp.zeros((), BF16)))
    return jnp.concatenate(out, axis=0) if len(out) > 1 else out[0]


def half_slope(lower, centre, upper):
    out = []
    for a, b, c in zip(lower, centre, upper):
        s, t = b - a, c - b
        out.append(0.5 * (jnp.maximum(jnp.minimum(s, t), 0.0) + jnp.minimum(jnp.maximum(s, t), 0.0)))
    return out


def dot3(a, b):
    return a[0] * b[0] + a[1] * b[1] + a[2] * b[2]


def conserved(q):
    rho, v, b, p = q[0], q[1:4], q[4:7], q[7]
    energy = p * (1.0 / (ADIABATIC - 1.0)) + 0.5 * rho * dot3(v, v) + 0.5 * dot3(b, b)
    return [rho, rho * v[0], rho * v[1], rho * v[2], b[0], b[1], b[2], energy]


def primitive(u):
    rho, b = u[0], u[4:7]
    inverse = 1.0 / rho
    v = [u[k] * inverse for k in (1, 2, 3)]
    p = (ADIABATIC - 1.0) * (u[7] - 0.5 * rho * dot3(v, v) - 0.5 * dot3(b, b))
    return [rho] + v + list(b) + [p]


def side(q, d):
    rho, v, b, p = q[0], q[1:4], q[4:7], q[7]
    b2 = dot3(b, b)
    half_b2 = 0.5 * b2
    total = p + half_b2
    mom = [rho * x for x in v]
    energy = p * (1.0 / (ADIABATIC - 1.0)) + 0.5 * dot3(mom, v) + half_b2
    vn, bn, mn = v[d], b[d], mom[d]
    flux = [mn]
    for k in range(3):
        f = mn * v[k] - bn * b[k]
        flux.append(f + total if k == d else f)
    for k in range(3):
        flux.append(None if k == d else vn * b[k] - bn * v[k])
    flux.append((energy + total) * vn - bn * dot3(v, b))
    speed = jnp.abs(vn) + jnp.sqrt((ADIABATIC * jnp.abs(p) + b2) / rho)
    return [rho] + mom + list(b) + [energy], flux, speed


def face(left, right, d):
    cons_l, flux_l, speed_l = side(left, d)
    cons_r, flux_r, speed_r = side(right, d)
    half_c = 0.5 * jnp.maximum(speed_l, speed_r)
    out = []
    for k in range(8):
        jump = half_c * (cons_r[k] - cons_l[k])
        out.append(-jump if flux_l[k] is None else 0.5 * (flux_l[k] + flux_r[k]) - jump)
    return out


def periodic(q, axis, d):
    size = q[0].shape[axis]
    back = [pltpu.roll(x, 1, axis) for x in q]
    ahead = [pltpu.roll(x, size - 1, axis) for x in q]
    slope = half_slope(back, q, ahead)
    left = [x + s for x, s in zip(q, slope)]
    right = [pltpu.roll(x - s, size - 1, axis) for x, s in zip(q, slope)]
    flux = face(left, right, d)
    return [pltpu.roll(f, 1, axis) - f for f in flux]


def add(a, b):
    return [x + y for x, y in zip(a, b)]


def plane(ref, x):
    return [ref[k, x] for k in range(8)]


def upper_face(ref, x):
    a, b, c, d = (plane(ref, x + k) for k in (-1, 0, 1, 2))
    left = add(b, half_slope(a, b, c))
    right = [v - s for v, s in zip(c, half_slope(b, c, d))]
    return face(left, right, 0)


def sideways(q):
    return add(periodic(q, 0, 1), periodic(q, 1, 2))


def sweep_planes(ref, first, count, put, others):
    def body(step, below):
        x = first + step
        above = upper_face(ref, x)
        q = plane(ref, x)
        change = [f - g for f, g in zip(below, above)]
        put(x, step, q, add(change, others(step, q)))
        return above

    lax.fori_loop(0, count, body, upper_face(ref, first - 1))


def stage_own(own_ref, side_ref):
    def body(x, carry):
        for k, value in enumerate(sideways(plane(own_ref, x))):
            side_ref[k, x] = value
        return carry

    lax.fori_loop(0, own_ref.shape[1], body, 0)


def split_planes(ref, out_a, out_b):
    odd = lax.axis_index("mag") % 2
    top = ref.shape[1] - 2
    for k in range(8):
        out_a[k] = ref[k, pl.ds((1 - odd) * top, 2)]
        out_b[k] = ref[k, pl.ds(odd * top, 2)]


def pad_planes(ref, from_a, from_b, pad_ref):
    me = lax.axis_index("mag")
    last = lax.axis_size("mag") - 1
    even = me % 2 == 0
    cx = ref.shape[1]
    for k in range(8):
        for x in range(2):
            low = jnp.where(even, from_b[k, x], from_a[k, x])
            high = jnp.where(even, from_a[k, x], from_b[k, x])
            pad_ref[k, x] = jnp.where(me == 0, ref[k, 0], low)
            pad_ref[k, cx + 2 + x] = jnp.where(me == last, ref[k, cx - 1], high)
        for x in range(cx):
            pad_ref[k, 2 + x] = ref[k, x]


def stage_one(own_ref, from_a, from_b, side_ref, load_ref, next_ref, half_ref, out_a, out_b, load_out, pad_ref):
    pad_planes(own_ref, from_a, from_b, pad_ref)
    load_out[...] = load_ref[...]

    def put(x, step, q, change):
        start = conserved(q)
        first = [s + TIME_STEP * c for s, c in zip(start, change)]
        q1 = primitive(first)
        for k in range(8):
            next_ref[k, step] = q1[k]
            half_ref[k, step] = 0.5 * (start[k] + first[k])

    sweep_planes(pad_ref, 2, own_ref.shape[1], put, lambda step, q: plane(side_ref, step))
    split_planes(next_ref, out_a, out_b)


def stage_two(next_ref, half_ref, from_a, from_b, rho_ref, vel_ref, mag_ref, prs_ref, end_ref, pad_ref):
    end_ref[...] = half_ref[0, 0, 0:8]
    pad_planes(next_ref, from_a, from_b, pad_ref)

    def put(x, step, q, change):
        final = [half_ref[k, step] + (0.5 * TIME_STEP) * change[k] for k in range(8)]
        q2 = primitive(final)
        rho_ref[step] = q2[0]
        for k in range(3):
            vel_ref[k, step] = q2[1 + k]
            mag_ref[k, step] = q2[4 + k]
        prs_ref[step] = q2[7]

    sweep_planes(pad_ref, 2, half_ref.shape[1], put, lambda step, q: sideways(q))


def pick_current(own_ref, cell_ref, strip_ref, from_a, from_b, out_ref):
    me = lax.axis_index("mag")
    last = lax.axis_size("mag") - 1
    even = me % 2 == 0
    cx, ny, nz = own_ref.shape[1:]
    rows = []
    for x in range(cx):
        bx, by, bz = (own_ref[4 + k, x] for k in range(3))

        def neighbour(k, step):
            if 0 <= x + step < cx:
                return own_ref[4 + k, x + step]
            if step < 0:
                below = jnp.where(even, from_b[4 + k, 1], from_a[4 + k, 1])
                return jnp.where(me == 0, own_ref[4 + k, x], below)
            above = jnp.where(even, from_a[4 + k, 0], from_b[4 + k, 0])
            return jnp.where(me == last, own_ref[4 + k, x], above)

        def along_x(k):
            return 0.5 * (neighbour(k, 1) - neighbour(k, -1))

        def along(v, axis):
            return 0.5 * (pltpu.roll(v, v.shape[axis] - 1, axis) - pltpu.roll(v, 1, axis))

        jx = along(bz, 0) - along(by, 1)
        jy = along(bx, 1) - along_x(2)
        jz = along_x(1) - along(bx, 0)
        norm = jnp.sqrt(bx * bx + by * by + bz * bz + 1.0)
        rows.append(SOURCE_GAIN * (jx * bx + jy * by + jz * bz) / norm)
    table = jnp.concatenate(rows, axis=0)
    count = table.shape[0]
    both = jnp.concatenate(pieces(table), axis=0)
    cells = cell_ref[...]
    hi, lo = cells // nz, (cells % nz).astype(F32)
    index = lax.broadcasted_iota(I32, (count, LANES), 0)
    points = cells.shape[0]
    for s in range(points):
        hot = rows_hot(lo[s : s + 1], nz)
        found = jnp.dot(both, hot, preferred_element_type=F32)
        found = found[:count] + found[count:]
        mine = jnp.where(index == hi[s : s + 1], found, 0.0)
        out_ref[s : s + 1, :] = jnp.sum(mine, axis=0, keepdims=True)
    out_ref[points:, :] = strip_ref[...]


def load_arguments(
    rho_ref, vel_ref, mag_ref, prs_ref, cell_ref, cond_ref, own_out, a_out, b_out, cell_out, strip_out, rows, sems
):
    pairs = [
        (cond_ref, rows),
        (cell_ref, cell_out),
        (rho_ref, own_out.at[0]),
        (vel_ref, own_out.at[pl.ds(1, 3)]),
        (mag_ref, own_out.at[pl.ds(4, 3)]),
        (prs_ref, own_out.at[7]),
    ]
    copies = [
        pltpu.make_async_copy(source, target, sems.at[k])
        for k, (source, target) in enumerate(pairs)
    ]
    for copy in copies:
        copy.start()
    copies[0].wait()
    lat, columns = rows.shape
    strips = columns // LANES
    for r in range(lat):
        for strip in range(strips):
            place = r * strips + strip
            strip_out[place : place + 1, :] = rows[r : r + 1, strip * LANES : (strip + 1) * LANES]
    for copy in copies[1:]:
        copy.wait()
    split_planes(own_out, a_out, b_out)


def east_of(v):
    lane = lax.broadcasted_iota(I32, v.shape, 2)
    turned = pltpu.roll(v, v.shape[2] - 1, 2)
    return jnp.where(lane == v.shape[2] - 1, pltpu.roll(turned, v.shape[1] - 1, 1), turned)


def west_of(v):
    lane = lax.broadcasted_iota(I32, v.shape, 2)
    turned = pltpu.roll(v, 1, 2)
    return jnp.where(lane == 0, pltpu.roll(turned, 1, 1), turned)


def scatter_block(value, hi, lo, count):
    hi, lo = hi.astype(F32), lo.astype(F32)
    high_piece = value.astype(BF16).astype(F32)
    low_piece = value - high_piece
    lefts, rights = [], []
    for s in range(value.shape[0]):
        lefts.append(rows_hot(hi[s : s + 1], count))
        hot = rows_hot(lo[s : s + 1], LANES)
        two = []
        for piece in (high_piece, low_piece):
            wide = jnp.broadcast_to(piece[s : s + 1], (16, LANES)).astype(BF16)
            two.append(hot * jnp.concatenate([wide] * (LANES // 16), axis=0))
        rights.append(jnp.concatenate(two, axis=0))
    left = jnp.concatenate(lefts, axis=1)
    right = jnp.concatenate(rights, axis=1)
    return lax.dot_general(left, right, (((1,), (1,)), ((), ())), preferred_element_type=F32)


def repeat(count, body):
    if count <= 8:
        for i in range(count):
            body(i)
    else:
        lax.fori_loop(0, count, lambda i, carry: (body(i), carry)[1], 0)


def origin(me, devices, j):
    mask, bit, k = 0, devices // 2, 0
    while bit > 1:
        mask = mask + ((j >> k) & 1) * bit
        bit, k = bit // 2, k + 1
    return jnp.bitwise_xor(me, mask)


def scatter_new(first, blocks, points, lat, strips):
    def kernel(*refs):
        *total_in, load_ref, owner_ref, row_ref, lon_ref, out_ref = refs
        me = lax.axis_index("mag")
        devices = lax.axis_size("mag")
        count = out_ref.shape[0]
        rows = min(count, 1024)
        stride = load_ref.shape[0] // blocks

        def part(j, g, base_ref):
            device = origin(me, devices, first + j)
            at = pl.ds(pl.multiple_of(device * points, points), points)
            value = load_ref[pl.ds(pl.multiple_of(j * stride, 8), points), :]
            hi = (owner_ref[at, :] * lat + row_ref[at, :]) * strips + lon_ref[at, :] // LANES
            lo = lon_ref[at, :] % LANES
            new = scatter_block(value, hi - g * rows, lo, rows)
            place = pl.ds(pl.multiple_of(g * rows, rows), rows)
            out_ref[place, :] = new if base_ref is None else base_ref[place, :] + new

        def group(g):
            part(0, g, total_in[0] if total_in else None)
            repeat(blocks - 1, lambda j: part(j + 1, g, out_ref))

        repeat(count // rows, group)

    return kernel


def handing_on(kernel, count):
    def run(*refs):
        outs = count + 1
        given = refs[-outs - count : -outs]
        for source, target in zip(given, refs[-count:]):
            target[...] = source[...]
        kernel(*refs[: -outs - count], refs[-outs])

    return run


def join(first_ref, second_ref, out_ref):
    size = first_ref.shape[0]
    out_ref[:size, :] = first_ref[...]
    out_ref[size:, :] = second_ref[...]


def scatter_last(blocks, points, lat, strips):
    def kernel(total_ref, before_ref, load_ref, owner_ref, row_ref, lon_ref, out_ref, work_ref):
        half = blocks // 2
        scatter_new(half, half, points, lat, strips)(
            total_ref, load_ref, owner_ref, row_ref, lon_ref, work_ref
        )
        count = work_ref.shape[0]
        out_ref[:count, :] = work_ref[:, :LANES] + work_ref[:, LANES:]
        cells = lat * strips
        stride = points + cells
        for j in range(blocks):
            ref = before_ref if j < half else load_ref
            start = (j % half) * stride + points
            out_ref[count + j * cells : count + (j + 1) * cells, :] = ref[start : start + cells, :]

    return kernel


def solve_and_read(blocks, points, lat, strips):
    def kernel(
        mine_ref, their_ref, owner_ref, row_ref, lon_ref, flat_ref, out_ref, s_ref, w_ref, phi_ref
    ):
        me = lax.axis_index("mag")
        devices = lax.axis_size("mag")
        rows = devices * lat
        count = rows * strips
        cells = lat * strips
        zeros = jnp.zeros((1, strips, LANES), F32)
        for ref in (s_ref, phi_ref.at[0], phi_ref.at[1]):
            ref[0:1] = zeros
            ref[rows + 1 : rows + 2] = zeros

        def place(j):
            at = pl.ds(pl.multiple_of(count + j * cells, cells), cells)
            for ref, who in ((mine_ref, me), (their_ref, jnp.bitwise_xor(me, 1))):
                device = origin(who, devices, j)
                s_ref[pl.ds(device * lat + 1, lat)] = ref[at, :].reshape(lat, strips, LANES)

        repeat(blocks, place)
        chunk = min(8, rows)

        def prepare(i):
            r = i * chunk
            s, above, below = (s_ref[pl.ds(r + k, chunk)] for k in (1, 0, 2))
            north, south = 0.5 * (s + above), 0.5 * (s + below)
            east = (0.5 * LON_WEIGHT) * (s + east_of(s))
            west = (0.5 * LON_WEIGHT) * (s + west_of(s))
            inverse = 1.0 / (north + south + east + west + LEAK_RATE * s)
            at = pl.ds(pl.multiple_of(r * strips, 8), chunk * strips)
            source = (mine_ref[at, :] + their_ref[at, :]).reshape(chunk, strips, LANES)
            for k, value in enumerate((source, north, south, east, west)):
                w_ref[k, pl.ds(r, chunk)] = value * inverse
            phi_ref[0, pl.ds(r + 1, chunk)] = source * inverse

        repeat(rows // chunk, prepare)
        for sweep in range(SWEEPS - 1):
            old, new = sweep % 2, 1 - sweep % 2

            def relax(i):
                r = i * chunk
                phi, above, below = (phi_ref[old, pl.ds(r + k, chunk)] for k in (1, 0, 2))
                source, north, south, east, west = (w_ref[k, pl.ds(r, chunk)] for k in range(5))
                phi_ref[new, pl.ds(r + 1, chunk)] = (
                    source
                    + north * above
                    + south * below
                    + east * east_of(phi)
                    + west * west_of(phi)
                )

            repeat(rows // chunk, relax)
        last = (SWEEPS - 1) % 2
        own = phi_ref[last, pl.ds(me * lat + 1, lat)]
        for strip in range(strips):
            flat_ref[:, strip * LANES : (strip + 1) * LANES] = own[:, strip, :]

        block = min(256, count)
        groups = count // block
        table = phi_ref[last, pl.ds(1, rows)].reshape(count, LANES)
        table = jnp.concatenate([table[g * block : (g + 1) * block] for g in range(groups)], axis=1)
        both = jnp.concatenate(pieces(table), axis=0)
        at = pl.ds(pl.multiple_of(me * points, points), points)
        owner, row, lon = owner_ref[at, :], row_ref[at, :], lon_ref[at, :]
        hi = (owner * lat + row) * strips + lon // LANES
        group, hi, lo = hi // block, hi % block, lon % LANES
        index = lax.broadcasted_iota(I32, (block, LANES), 0)
        columns = []
        for p in range(points):
            stack = []
            for g in range(groups):
                key = jnp.where(group[p : p + 1] == g, lo[p : p + 1], -1).astype(F32)
                stack.append(rows_hot(key, LANES))
            columns.append(jnp.concatenate(stack, axis=0))
        found = jnp.dot(both, jnp.concatenate(columns, axis=1), preferred_element_type=F32)
        found = found[:block] + found[block:]
        for p in range(points):
            part = found[:, p * LANES : (p + 1) * LANES]
            part = jnp.where(index == hi[p : p + 1], part, 0.0)
            out_ref[p : p + 1, :] = jnp.sum(part, axis=0, keepdims=True)

    return kernel


def swap(values, bit):
    devices = lax.axis_size("mag")
    return lax.ppermute(values, "mag", [(i, i ^ bit) for i in range(devices)])


def swap_next(values):
    devices = lax.axis_size("mag")
    pairs = [(i, (i + (1 if i % 2 else -1)) % devices) for i in range(devices)]
    return lax.ppermute(values, "mag", pairs)


def shards(
    density, velocity, mag_field, pressure, conductance, shell_cell, foot_owner, foot_row, foot_lon
):
    devices = lax.axis_size("mag")
    cx, ny, nz = density.shape
    lat, columns = conductance.shape
    strips = columns // LANES
    shell_count = shell_cell.shape[0]
    points = shell_count // LANES
    cells = lat * strips
    count = devices * cells
    shape = jax.ShapeDtypeStruct

    tile = shape((points, LANES), I32)
    slab = shape((8, cx, ny, nz), F32)
    two = shape((8, 2, ny, nz), F32)
    own, to_a, to_b, cell, strip = call(
        load_arguments,
        [slab, two, two, tile, shape((cells, LANES), F32)],
        [pltpu.VMEM((lat, columns), F32), pltpu.SemaphoreType.DMA((6,))],
        [HBM] * 6,
    )(
        *(
            pltpu.with_memory_space_constraint(x, pltpu.HBM)
            for x in (
                density,
                velocity,
                mag_field,
                pressure,
                shell_cell.reshape(-1, LANES),
                conductance,
            )
        )
    )
    from_a, from_b = swap(to_a, 1), swap_next(to_b)
    own_side = call(stage_own, slab)(own)

    owner = foot_owner.reshape(-1, LANES)
    row = foot_row.reshape(-1, LANES)
    lon = foot_lon.reshape(-1, LANES)

    payload = shape((points + cells, LANES), F32)
    load = call(pick_current, payload, after=(own_side,))(own, cell, strip, from_a, from_b)
    pad = [pltpu.VMEM((8, cx + 4, ny, nz), F32)]
    following, half, next_a, next_b, after_one = call(
        stage_one, [slab, slab, two, two, payload], pad
    )(own, from_a, from_b, own_side, load)
    next_a, next_b = swap(next_a, 1), swap_next(next_b)

    grid = shape((count, 2 * LANES), F32)
    total, blocks, done = (), 1, 0
    bit = devices // 2
    while bit > 1:
        arrived = swap(load, bit)
        if blocks > 1:
            kernel = handing_on(scatter_new(done, blocks - done, points, lat, strips), 1)
            total, load = call(kernel, [grid, shape(load.shape, F32)])(
                *total, new, owner, row, lon, load
            )
            total, done = (total,), blocks
        before, new = load, arrived
        if blocks == 1:
            new = load = call(
                join, shape((2 * (points + cells), LANES), F32), after=(next_a, next_b)
            )(after_one, arrived)
        else:
            load = jnp.concatenate([load, arrived], axis=0)
        blocks, bit = blocks * 2, bit // 2

    cell_shape = shape((cx, ny, nz), F32)
    vector_shape = shape((3, cx, ny, nz), F32)
    new_density, new_velocity, new_field, new_pressure, end = call(
        stage_two, [cell_shape, vector_shape, vector_shape, cell_shape, shape((8, LANES), F32)], pad
    )(following, half, next_a, next_b)

    grids = shape((count + count // 2, LANES), F32)
    mine = call(
        scatter_last(blocks, points, lat, strips),
        grids,
        [pltpu.VMEM((count, 2 * LANES), F32)],
        after=(end,),
    )(*total, before, new, owner, row, lon)
    theirs = swap(mine, 1)

    potential, shell_potential = call(
        solve_and_read(blocks, points, lat, strips),
        [shape((lat, columns), F32), shape((points, LANES), F32)],
        [
            pltpu.VMEM((devices * lat + 2, strips, LANES), F32),
            pltpu.VMEM((5, devices * lat, strips, LANES), F32),
            pltpu.VMEM((2, devices * lat + 2, strips, LANES), F32),
        ],
    )(mine, theirs, owner, row, lon)
    return (
        new_density,
        new_velocity,
        new_field,
        new_pressure,
        potential,
        shell_potential.reshape(shell_count),
    )


def solution(mesh):
    both = ("parts", "mag")
    in_specs = (
        P(both, None, None),
        P(None, both, None, None),
        P(None, both, None, None),
        P(both, None, None),
        P(both, None),
        P("mag"),
        P(),
        P(),
        P(),
    )
    out_specs = (
        P(both, None, None),
        P(None, both, None, None),
        P(None, both, None, None),
        P(both, None, None),
        P(both, None),
        P(both),
    )
    return jax.shard_map(shards, mesh=mesh, in_specs=in_specs, out_specs=out_specs, check_vma=False)
```

```python
import jax
import jax.numpy as jnp
from jax import lax
from jax.experimental import pallas as pl
from jax.experimental.pallas import tpu as pltpu
from jax.sharding import PartitionSpec as P

SWEEPS = 4
ADIABATIC = 5.0 / 3.0
TIME_STEP = 0.02
LON_WEIGHT = 0.25
LEAK_RATE = 0.05
SOURCE_GAIN = 10.0
LANES = 128

F32 = jnp.float32
BF16 = jnp.bfloat16
I32 = jnp.int32
VMEM = pl.BlockSpec(memory_space=pltpu.VMEM)
ANY = pl.BlockSpec(memory_space=pl.ANY)
HBM = pl.BlockSpec(memory_space=pltpu.HBM)
MIB = 1024 * 1024


def call(kernel, outs, scratch=(), specs=None, after=()):
    many = isinstance(outs, (list, tuple))

    def body(*refs):
        kernel(*refs[len(after) :])

    def run(*operands):
        in_specs = [ANY] * len(after) + list(specs or [VMEM] * len(operands))
        return pallas(body if after else kernel, outs, many, scratch, in_specs)(*after, *operands)

    return run


def pallas(kernel, outs, many, scratch, in_specs):
    return pl.pallas_call(
        kernel,
        in_specs=in_specs,
        out_shape=outs,
        out_specs=[VMEM] * len(outs) if many else VMEM,
        scratch_shapes=list(scratch),
        compiler_params=pltpu.CompilerParams(
            vmem_limit_bytes=(32 if lax.axis_size("mag") <= 32 else 60) * MIB
        ),
    )


def pieces(values):
    first = values.astype(BF16)
    second = (values - first.astype(F32)).astype(BF16)
    return first, second


def rows_hot(key_row, count, group=256):
    lanes = key_row.shape[1]
    out = []
    for first in range(0, count, group):
        size = min(group, count - first)
        key = jnp.broadcast_to(key_row - first, (16, lanes)).astype(BF16)
        keys = jnp.concatenate([key] * (size // 16), axis=0)
        index = lax.broadcasted_iota(I32, (size, lanes), 0).astype(F32).astype(BF16)
        out.append(jnp.where(keys == index, jnp.ones((), BF16), jnp.zeros((), BF16)))
    return jnp.concatenate(out, axis=0) if len(out) > 1 else out[0]


def half_slope(lower, centre, upper):
    out = []
    for a, b, c in zip(lower, centre, upper):
        s, t = b - a, c - b
        out.append(0.5 * (jnp.maximum(jnp.minimum(s, t), 0.0) + jnp.minimum(jnp.maximum(s, t), 0.0)))
    return out


def dot3(a, b):
    return a[0] * b[0] + a[1] * b[1] + a[2] * b[2]


def conserved(q):
    rho, v, b, p = q[0], q[1:4], q[4:7], q[7]
    energy = p * (1.0 / (ADIABATIC - 1.0)) + 0.5 * rho * dot3(v, v) + 0.5 * dot3(b, b)
    return [rho, rho * v[0], rho * v[1], rho * v[2], b[0], b[1], b[2], energy]


def primitive(u):
    rho, b = u[0], u[4:7]
    inverse = 1.0 / rho
    v = [u[k] * inverse for k in (1, 2, 3)]
    p = (ADIABATIC - 1.0) * (u[7] - 0.5 * rho * dot3(v, v) - 0.5 * dot3(b, b))
    return [rho] + v + list(b) + [p]


def side(q, d):
    rho, v, b, p = q[0], q[1:4], q[4:7], q[7]
    b2 = dot3(b, b)
    half_b2 = 0.5 * b2
    total = p + half_b2
    mom = [rho * x for x in v]
    energy = p * (1.0 / (ADIABATIC - 1.0)) + 0.5 * dot3(mom, v) + half_b2
    vn, bn, mn = v[d], b[d], mom[d]
    flux = [mn]
    for k in range(3):
        f = mn * v[k] - bn * b[k]
        flux.append(f + total if k == d else f)
    for k in range(3):
        flux.append(None if k == d else vn * b[k] - bn * v[k])
    flux.append((energy + total) * vn - bn * dot3(v, b))
    speed = jnp.abs(vn) + jnp.sqrt((ADIABATIC * jnp.abs(p) + b2) / rho)
    return [rho] + mom + list(b) + [energy], flux, speed


def face(left, right, d):
    cons_l, flux_l, speed_l = side(left, d)
    cons_r, flux_r, speed_r = side(right, d)
    half_c = 0.5 * jnp.maximum(speed_l, speed_r)
    out = []
    for k in range(8):
        jump = half_c * (cons_r[k] - cons_l[k])
        out.append(-jump if flux_l[k] is None else 0.5 * (flux_l[k] + flux_r[k]) - jump)
    return out


def periodic(q, axis, d):
    size = q[0].shape[axis]
    back = [pltpu.roll(x, 1, axis) for x in q]
    ahead = [pltpu.roll(x, size - 1, axis) for x in q]
    slope = half_slope(back, q, ahead)
    left = [x + s for x, s in zip(q, slope)]
    right = [pltpu.roll(x - s, size - 1, axis) for x, s in zip(q, slope)]
    flux = face(left, right, d)
    return [pltpu.roll(f, 1, axis) - f for f in flux]


def add(a, b):
    return [x + y for x, y in zip(a, b)]


def plane(ref, x):
    return [ref[k, x] for k in range(8)]


def upper_face(ref, x):
    a, b, c, d = (plane(ref, x + k) for k in (-1, 0, 1, 2))
    left = add(b, half_slope(a, b, c))
    right = [v - s for v, s in zip(c, half_slope(b, c, d))]
    return face(left, right, 0)


def sideways(q):
    return add(periodic(q, 0, 1), periodic(q, 1, 2))


def sweep_planes(ref, first, count, put, others):
    def body(step, below):
        x = first + step
        above = upper_face(ref, x)
        q = plane(ref, x)
        change = [f - g for f, g in zip(below, above)]
        put(x, step, q, add(change, others(step, q)))
        return above

    lax.fori_loop(0, count, body, upper_face(ref, first - 1))


def stage_own(own_ref, side_ref):
    def body(x, carry):
        for k, value in enumerate(sideways(plane(own_ref, x))):
            side_ref[k, x] = value
        return carry

    lax.fori_loop(0, own_ref.shape[1], body, 0)


def stage_one(own_ref, eight_a, eight_b, own_side_ref, next_ref, half_ref, pad_ref, side_ref):
    me = lax.axis_index("mag")
    last = lax.axis_size("mag") - 1
    even = me % 2 == 0
    cx = own_ref.shape[1]
    for k in range(8):
        for x in range(cx):
            low = jnp.where(even, eight_b[k, x], eight_a[k, x])
            high = jnp.where(even, eight_a[k, x], eight_b[k, x])
            pad_ref[k, x] = jnp.where(me == 0, own_ref[k, 0], low)
            pad_ref[k, cx + x] = own_ref[k, x]
            pad_ref[k, 2 * cx + x] = jnp.where(me == last, own_ref[k, cx - 1], high)
            side_ref[k, 2 + x] = own_side_ref[k, x]

    def beside(i, carry):
        step = jnp.where(i < 2, i, cx + i)
        for k, value in enumerate(sideways(plane(pad_ref, cx - 2 + step))):
            side_ref[k, step] = value
        return carry

    lax.fori_loop(0, 4, beside, 0)

    def put(x, step, q, change):
        start = conserved(q)
        first = [s + TIME_STEP * c for s, c in zip(start, change)]
        q1 = primitive(first)
        for k in range(8):
            next_ref[k, step] = q1[k]

        @pl.when(jnp.logical_and(step >= 2, step < cx + 2))
        def _():
            for k in range(8):
                half_ref[k, step - 2] = 0.5 * (start[k] + first[k])

    sweep_planes(pad_ref, cx - 2, cx + 4, put, lambda step, q: plane(side_ref, step))

    @pl.when(me == 0)
    def _():
        for k in range(8):
            next_ref[k, 0] = next_ref[k, 2]
            next_ref[k, 1] = next_ref[k, 2]

    @pl.when(me == last)
    def _():
        for k in range(8):
            next_ref[k, cx + 2] = next_ref[k, cx + 1]
            next_ref[k, cx + 3] = next_ref[k, cx + 1]


def stage_two(next_ref, half_ref, rho_ref, vel_ref, mag_ref, prs_ref, end_ref):
    end_ref[...] = half_ref[0, 0, 0:8]
    cx = half_ref.shape[1]

    def put(x, step, q, change):
        final = [half_ref[k, step] + (0.5 * TIME_STEP) * change[k] for k in range(8)]
        q2 = primitive(final)
        rho_ref[step] = q2[0]
        for k in range(3):
            vel_ref[k, step] = q2[1 + k]
            mag_ref[k, step] = q2[4 + k]
        prs_ref[step] = q2[7]

    sweep_planes(next_ref, 2, cx, put, lambda step, q: sideways(q))


def pick_current(own_ref, cell_ref, strip_ref, edge_a, edge_b, out_ref, own_out):
    me = lax.axis_index("mag")
    last = lax.axis_size("mag") - 1
    even = me % 2 == 0
    cx, ny, nz = own_ref.shape[1:]
    own_out[...] = own_ref[...]
    rows = []
    for x in range(cx):
        bx, by, bz = (own_ref[4 + k, x] for k in range(3))

        def neighbour(k, step):
            if 0 <= x + step < cx:
                return own_ref[4 + k, x + step]
            if step < 0:
                below = jnp.where(even, edge_b[k - 1, 1], edge_a[k - 1, 1])
                return jnp.where(me == 0, own_ref[4 + k, x], below)
            above = jnp.where(even, edge_a[k - 1, 0], edge_b[k - 1, 0])
            return jnp.where(me == last, own_ref[4 + k, x], above)

        def along_x(k):
            return 0.5 * (neighbour(k, 1) - neighbour(k, -1))

        def along(v, axis):
            return 0.5 * (pltpu.roll(v, v.shape[axis] - 1, axis) - pltpu.roll(v, 1, axis))

        jx = along(bz, 0) - along(by, 1)
        jy = along(bx, 1) - along_x(2)
        jz = along_x(1) - along(bx, 0)
        norm = jnp.sqrt(bx * bx + by * by + bz * bz + 1.0)
        rows.append(SOURCE_GAIN * (jx * bx + jy * by + jz * bz) / norm)
    table = jnp.concatenate(rows, axis=0)
    count = table.shape[0]
    both = jnp.concatenate(pieces(table), axis=0)
    cells = cell_ref[...]
    hi, lo = cells // nz, (cells % nz).astype(F32)
    index = lax.broadcasted_iota(I32, (count, LANES), 0)
    points = cells.shape[0]
    for s in range(points):
        hot = rows_hot(lo[s : s + 1], nz)
        found = jnp.dot(both, hot, preferred_element_type=F32)
        found = found[:count] + found[count:]
        mine = jnp.where(index == hi[s : s + 1], found, 0.0)
        out_ref[s : s + 1, :] = jnp.sum(mine, axis=0, keepdims=True)
    out_ref[points:, :] = strip_ref[...]


def load_arguments(
    rho_ref, vel_ref, mag_ref, prs_ref, cell_ref, cond_ref, own_out, edge_out, cell_out, strip_out, rows, sems
):
    last = mag_ref.shape[1] - 1
    pairs = [
        (cond_ref, rows),
        (mag_ref.at[pl.ds(1, 2), pl.ds(0, 1)], edge_out.at[:, pl.ds(0, 1)]),
        (mag_ref.at[pl.ds(1, 2), pl.ds(last, 1)], edge_out.at[:, pl.ds(1, 1)]),
        (cell_ref, cell_out),
        (rho_ref, own_out.at[0]),
        (vel_ref, own_out.at[pl.ds(1, 3)]),
        (mag_ref, own_out.at[pl.ds(4, 3)]),
        (prs_ref, own_out.at[7]),
    ]
    copies = [
        pltpu.make_async_copy(source, target, sems.at[k])
        for k, (source, target) in enumerate(pairs)
    ]
    for copy in copies:
        copy.start()
    copies[0].wait()
    lat, columns = rows.shape
    strips = columns // LANES
    for r in range(lat):
        for strip in range(strips):
            place = r * strips + strip
            strip_out[place : place + 1, :] = rows[r : r + 1, strip * LANES : (strip + 1) * LANES]
    for copy in copies[1:]:
        copy.wait()


def east_of(v):
    lane = lax.broadcasted_iota(I32, v.shape, 2)
    turned = pltpu.roll(v, v.shape[2] - 1, 2)
    return jnp.where(lane == v.shape[2] - 1, pltpu.roll(turned, v.shape[1] - 1, 1), turned)


def west_of(v):
    lane = lax.broadcasted_iota(I32, v.shape, 2)
    turned = pltpu.roll(v, 1, 2)
    return jnp.where(lane == 0, pltpu.roll(turned, 1, 1), turned)


def scatter_block(value, hi, lo, count):
    hi, lo = hi.astype(F32), lo.astype(F32)
    high_piece = value.astype(BF16).astype(F32)
    low_piece = value - high_piece
    lefts, rights = [], []
    for s in range(value.shape[0]):
        lefts.append(rows_hot(hi[s : s + 1], count))
        hot = rows_hot(lo[s : s + 1], LANES)
        two = []
        for piece in (high_piece, low_piece):
            wide = jnp.broadcast_to(piece[s : s + 1], (16, LANES)).astype(BF16)
            two.append(hot * jnp.concatenate([wide] * (LANES // 16), axis=0))
        rights.append(jnp.concatenate(two, axis=0))
    left = jnp.concatenate(lefts, axis=1)
    right = jnp.concatenate(rights, axis=1)
    return lax.dot_general(left, right, (((1,), (1,)), ((), ())), preferred_element_type=F32)


def repeat(count, body):
    if count <= 8:
        for i in range(count):
            body(i)
    else:
        lax.fori_loop(0, count, lambda i, carry: (body(i), carry)[1], 0)


def origin(me, devices, j):
    mask, bit, k = 0, devices // 2, 0
    while bit > 1:
        mask = mask + ((j >> k) & 1) * bit
        bit, k = bit // 2, k + 1
    return jnp.bitwise_xor(me, mask)


def scatter_new(first, blocks, points, lat, strips):
    def kernel(*refs):
        *total_in, load_ref, owner_ref, row_ref, lon_ref, out_ref = refs
        me = lax.axis_index("mag")
        devices = lax.axis_size("mag")
        count = out_ref.shape[0]
        rows = min(count, 1024)
        stride = load_ref.shape[0] // blocks

        def part(j, g, base_ref):
            device = origin(me, devices, first + j)
            at = pl.ds(pl.multiple_of(device * points, points), points)
            value = load_ref[pl.ds(pl.multiple_of(j * stride, 8), points), :]
            hi = (owner_ref[at, :] * lat + row_ref[at, :]) * strips + lon_ref[at, :] // LANES
            lo = lon_ref[at, :] % LANES
            new = scatter_block(value, hi - g * rows, lo, rows)
            place = pl.ds(pl.multiple_of(g * rows, rows), rows)
            out_ref[place, :] = new if base_ref is None else base_ref[place, :] + new

        def group(g):
            part(0, g, total_in[0] if total_in else None)
            repeat(blocks - 1, lambda j: part(j + 1, g, out_ref))

        repeat(count // rows, group)

    return kernel


def read_hot(points, lat, strips):
    def kernel(owner_ref, row_ref, lon_ref, hot_ref):
        block = min(256, lax.axis_size("mag") * lat * strips)
        me = lax.axis_index("mag")
        groups = hot_ref.shape[0] // LANES
        at = pl.ds(pl.multiple_of(me * points, points), points)
        owner, row, lon = owner_ref[at, :], row_ref[at, :], lon_ref[at, :]
        group = ((owner * lat + row) * strips + lon // LANES) // block
        lo = lon % LANES
        for p in range(points):
            for g in range(groups):
                key = jnp.where(group[p : p + 1] == g, lo[p : p + 1], -1).astype(F32)
                place = slice(p * LANES, (p + 1) * LANES)
                hot_ref[g * LANES : (g + 1) * LANES, place] = rows_hot(key, LANES)

    return kernel


def handing_on(kernel, count):
    def run(*refs):
        outs = count + 1
        given = refs[-outs - count : -outs]
        for source, target in zip(given, refs[-count:]):
            target[...] = source[...]
        kernel(*refs[: -outs - count], refs[-outs])

    return run


def and_read_hot(kernel, other):
    def run(*refs):
        *given, load_ref, total_out, load_out, hot_out = refs
        kernel(*given, load_ref, total_out, load_out)
        other(*given[-3:], hot_out)

    return run


def scatter_last(blocks, points, lat, strips):
    def kernel(total_ref, before_ref, load_ref, owner_ref, row_ref, lon_ref, out_ref, work_ref):
        half = blocks // 2
        scatter_new(half, half, points, lat, strips)(
            total_ref, load_ref, owner_ref, row_ref, lon_ref, work_ref
        )
        count = work_ref.shape[0]
        out_ref[:count, :] = work_ref[:, :LANES] + work_ref[:, LANES:]
        cells = lat * strips
        stride = points + cells
        for j in range(blocks):
            ref = before_ref if j < half else load_ref
            start = (j % half) * stride + points
            out_ref[count + j * cells : count + (j + 1) * cells, :] = ref[start : start + cells, :]

    return kernel


def solve_and_read(blocks, points, lat, strips):
    def kernel(
        mine_ref,
        their_ref,
        owner_ref,
        row_ref,
        lon_ref,
        hot_ref,
        flat_ref,
        out_ref,
        s_ref,
        w_ref,
        phi_ref,
    ):
        me = lax.axis_index("mag")
        devices = lax.axis_size("mag")
        rows = devices * lat
        count = rows * strips
        cells = lat * strips
        zeros = jnp.zeros((1, strips, LANES), F32)
        for ref in (s_ref, phi_ref.at[0], phi_ref.at[1]):
            ref[0:1] = zeros
            ref[rows + 1 : rows + 2] = zeros

        def place(j):
            at = pl.ds(pl.multiple_of(count + j * cells, cells), cells)
            for ref, who in ((mine_ref, me), (their_ref, jnp.bitwise_xor(me, 1))):
                device = origin(who, devices, j)
                s_ref[pl.ds(device * lat + 1, lat)] = ref[at, :].reshape(lat, strips, LANES)

        repeat(blocks, place)
        chunk = min(8, rows)

        def prepare(i):
            r = i * chunk
            s, above, below = (s_ref[pl.ds(r + k, chunk)] for k in (1, 0, 2))
            north, south = 0.5 * (s + above), 0.5 * (s + below)
            east = (0.5 * LON_WEIGHT) * (s + east_of(s))
            west = (0.5 * LON_WEIGHT) * (s + west_of(s))
            inverse = 1.0 / (north + south + east + west + LEAK_RATE * s)
            at = pl.ds(pl.multiple_of(r * strips, 8), chunk * strips)
            source = (mine_ref[at, :] + their_ref[at, :]).reshape(chunk, strips, LANES)
            for k, value in enumerate((source, north, south, east, west)):
                w_ref[k, pl.ds(r, chunk)] = value * inverse
            phi_ref[0, pl.ds(r + 1, chunk)] = source * inverse

        repeat(rows // chunk, prepare)
        for sweep in range(SWEEPS - 1):
            old, new = sweep % 2, 1 - sweep % 2

            def relax(i):
                r = i * chunk
                phi, above, below = (phi_ref[old, pl.ds(r + k, chunk)] for k in (1, 0, 2))
                source, north, south, east, west = (w_ref[k, pl.ds(r, chunk)] for k in range(5))
                phi_ref[new, pl.ds(r + 1, chunk)] = (
                    source
                    + north * above
                    + south * below
                    + east * east_of(phi)
                    + west * west_of(phi)
                )

            repeat(rows // chunk, relax)
        last = (SWEEPS - 1) % 2
        own = phi_ref[last, pl.ds(me * lat + 1, lat)]
        for strip in range(strips):
            flat_ref[:, strip * LANES : (strip + 1) * LANES] = own[:, strip, :]

        block = min(256, count)
        groups = count // block
        table = phi_ref[last, pl.ds(1, rows)].reshape(count, LANES)
        table = jnp.concatenate([table[g * block : (g + 1) * block] for g in range(groups)], axis=1)
        both = jnp.concatenate(pieces(table), axis=0)
        at = pl.ds(pl.multiple_of(me * points, points), points)
        owner, row, lon = owner_ref[at, :], row_ref[at, :], lon_ref[at, :]
        hi = ((owner * lat + row) * strips + lon // LANES) % block
        index = lax.broadcasted_iota(I32, (block, LANES), 0)
        found = jnp.dot(both, hot_ref[...], preferred_element_type=F32)
        found = found[:block] + found[block:]
        for p in range(points):
            part = found[:, p * LANES : (p + 1) * LANES]
            part = jnp.where(index == hi[p : p + 1], part, 0.0)
            out_ref[p : p + 1, :] = jnp.sum(part, axis=0, keepdims=True)

    return kernel


def swap(values, bit):
    devices = lax.axis_size("mag")
    return lax.ppermute(values, "mag", [(i, i ^ bit) for i in range(devices)])


def swap_next(values, ring):
    devices = lax.axis_size("mag")
    pairs = [(i, (i + (1 if i % 2 else -1)) % devices) for i in range(devices)]
    return lax.ppermute(values, "mag", pairs if ring else pairs[1:-1])


def shards(
    density, velocity, mag_field, pressure, conductance, shell_cell, foot_owner, foot_row, foot_lon
):
    devices = lax.axis_size("mag")
    cx, ny, nz = density.shape
    lat, columns = conductance.shape
    strips = columns // LANES
    shell_count = shell_cell.shape[0]
    points = shell_count // LANES
    cells = lat * strips
    count = devices * cells
    shape = jax.ShapeDtypeStruct

    tile = shape((points, LANES), I32)
    slab = shape((8, cx, ny, nz), F32)
    own, edge, cell, strip = call(
        load_arguments,
        [slab, shape((2, 2, ny, nz), F32), tile, shape((cells, LANES), F32)],
        [pltpu.VMEM((lat, columns), F32), pltpu.SemaphoreType.DMA((8,))],
        [HBM] * 6,
    )(
        *(
            pltpu.with_memory_space_constraint(x, pltpu.HBM)
            for x in (
                density,
                velocity,
                mag_field,
                pressure,
                shell_cell.reshape(-1, LANES),
                conductance,
            )
        )
    )
    edge_a, edge_b = swap(edge, 1), swap_next(edge, True)
    own_side = call(stage_own, slab)(own)

    owner = foot_owner.reshape(-1, LANES)
    row = foot_row.reshape(-1, LANES)
    lon = foot_lon.reshape(-1, LANES)

    load, own = call(
        pick_current, [shape((points + cells, LANES), F32), slab], after=(own_side,)
    )(own, cell, strip, edge_a, edge_b)
    eight_a, eight_b = swap(own, 1), swap_next(own, False)

    grid = shape((count, 2 * LANES), F32)
    hots = shape((count // min(256, count) * LANES, shell_count), BF16)
    total, blocks, done = (), 1, 0
    bit = devices // 2
    while bit > 1:
        arrived = swap(load, bit)
        if blocks > 1:
            kernel = handing_on(scatter_new(done, blocks - done, points, lat, strips), 1)
            outs = [grid, shape(load.shape, F32)]
            if blocks == 2:
                kernel = and_read_hot(kernel, read_hot(points, lat, strips))
                outs.append(hots)
            total, load, *rest = call(kernel, outs)(*total, new, owner, row, lon, load)
            hot = rest[0] if rest else hot
            total, done = (total,), blocks
        before, new = load, arrived
        load = jnp.concatenate([load, arrived], axis=0)
        if blocks == 1:
            new = load
        blocks, bit = blocks * 2, bit // 2

    following, half = call(
        stage_one,
        [shape((8, cx + 4, ny, nz), F32), slab],
        [pltpu.VMEM((8, 3 * cx, ny, nz), F32), pltpu.VMEM((8, cx + 4, ny, nz), F32)],
    )(own, eight_a, eight_b, own_side)

    grids = shape((count + count // 2, LANES), F32)
    mine = call(
        scatter_last(blocks, points, lat, strips),
        grids,
        [pltpu.VMEM((count, 2 * LANES), F32)],
        after=(half,),
    )(*total, before, new, owner, row, lon)
    theirs = swap(mine, 1)

    cell_shape = shape((cx, ny, nz), F32)
    vector_shape = shape((3, cx, ny, nz), F32)
    new_density, new_velocity, new_field, new_pressure, end = call(
        stage_two, [cell_shape, vector_shape, vector_shape, cell_shape, shape((8, LANES), F32)]
    )(following, half)

    potential, shell_potential = call(
        solve_and_read(blocks, points, lat, strips),
        [shape((lat, columns), F32), shape((points, LANES), F32)],
        [
            pltpu.VMEM((devices * lat + 2, strips, LANES), F32),
            pltpu.VMEM((5, devices * lat, strips, LANES), F32),
            pltpu.VMEM((2, devices * lat + 2, strips, LANES), F32),
        ],
        after=(end,),
    )(mine, theirs, owner, row, lon, hot)
    return (
        new_density,
        new_velocity,
        new_field,
        new_pressure,
        potential,
        shell_potential.reshape(shell_count),
    )


def solution(mesh):
    both = ("parts", "mag")
    in_specs = (
        P(both, None, None),
        P(None, both, None, None),
        P(None, both, None, None),
        P(both, None, None),
        P(both, None),
        P("mag"),
        P(),
        P(),
        P(),
    )
    out_specs = (
        P(both, None, None),
        P(None, both, None, None),
        P(None, both, None, None),
        P(both, None, None),
        P(both, None),
        P(both),
    )
    return jax.shard_map(shards, mesh=mesh, in_specs=in_specs, out_specs=out_specs, check_vma=False)
```

```python
import jax
import jax.numpy as jnp
from jax import lax
from jax.experimental import pallas as pl
from jax.experimental.pallas import tpu as pltpu
from jax.sharding import PartitionSpec as P

SWEEPS = 4
ADIABATIC = 5.0 / 3.0
TIME_STEP = 0.02
LON_WEIGHT = 0.25
LEAK_RATE = 0.05
SOURCE_GAIN = 10.0
LANES = 128

F32 = jnp.float32
BF16 = jnp.bfloat16
I32 = jnp.int32
VMEM = pl.BlockSpec(memory_space=pltpu.VMEM)
ANY = pl.BlockSpec(memory_space=pl.ANY)
HBM = pl.BlockSpec(memory_space=pltpu.HBM)
MIB = 1024 * 1024


def call(kernel, outs, scratch=(), specs=None, after=()):
    many = isinstance(outs, (list, tuple))

    def body(*refs):
        kernel(*refs[len(after) :])

    def run(*operands):
        in_specs = [ANY] * len(after) + list(specs or [VMEM] * len(operands))
        return pallas(body if after else kernel, outs, many, scratch, in_specs)(*after, *operands)

    return run


def pallas(kernel, outs, many, scratch, in_specs):
    return pl.pallas_call(
        kernel,
        in_specs=in_specs,
        out_shape=outs,
        out_specs=[VMEM] * len(outs) if many else VMEM,
        scratch_shapes=list(scratch),
        compiler_params=pltpu.CompilerParams(
            vmem_limit_bytes=(32 if lax.axis_size("mag") <= 32 else 60) * MIB
        ),
    )


def pieces(values):
    first = values.astype(BF16)
    second = (values - first.astype(F32)).astype(BF16)
    return first, second


def rows_hot(key_row, count, group=256):
    lanes = key_row.shape[1]
    out = []
    for first in range(0, count, group):
        size = min(group, count - first)
        key = jnp.broadcast_to(key_row - first, (16, lanes)).astype(BF16)
        keys = jnp.concatenate([key] * (size // 16), axis=0)
        index = lax.broadcasted_iota(I32, (size, lanes), 0).astype(F32).astype(BF16)
        out.append(jnp.where(keys == index, jnp.ones((), BF16), jnp.zeros((), BF16)))
    return jnp.concatenate(out, axis=0) if len(out) > 1 else out[0]


def half_slope(lower, centre, upper):
    out = []
    for a, b, c in zip(lower, centre, upper):
        s, t = b - a, c - b
        out.append(0.5 * (jnp.maximum(jnp.minimum(s, t), 0.0) + jnp.minimum(jnp.maximum(s, t), 0.0)))
    return out


def dot3(a, b):
    return a[0] * b[0] + a[1] * b[1] + a[2] * b[2]


def conserved(q):
    rho, v, b, p = q[0], q[1:4], q[4:7], q[7]
    energy = p * (1.0 / (ADIABATIC - 1.0)) + 0.5 * rho * dot3(v, v) + 0.5 * dot3(b, b)
    return [rho, rho * v[0], rho * v[1], rho * v[2], b[0], b[1], b[2], energy]


def primitive(u):
    rho, b = u[0], u[4:7]
    inverse = 1.0 / rho
    v = [u[k] * inverse for k in (1, 2, 3)]
    p = (ADIABATIC - 1.0) * (u[7] - 0.5 * rho * dot3(v, v) - 0.5 * dot3(b, b))
    return [rho] + v + list(b) + [p]


def side(q, d):
    rho, v, b, p = q[0], q[1:4], q[4:7], q[7]
    b2 = dot3(b, b)
    half_b2 = 0.5 * b2
    total = p + half_b2
    mom = [rho * x for x in v]
    energy = p * (1.0 / (ADIABATIC - 1.0)) + 0.5 * dot3(mom, v) + half_b2
    vn, bn, mn = v[d], b[d], mom[d]
    flux = [mn]
    for k in range(3):
        f = mn * v[k] - bn * b[k]
        flux.append(f + total if k == d else f)
    for k in range(3):
        flux.append(None if k == d else vn * b[k] - bn * v[k])
    flux.append((energy + total) * vn - bn * dot3(v, b))
    speed = jnp.abs(vn) + jnp.sqrt((ADIABATIC * jnp.abs(p) + b2) / rho)
    return [rho] + mom + list(b) + [energy], flux, speed


def face(left, right, d):
    cons_l, flux_l, speed_l = side(left, d)
    cons_r, flux_r, speed_r = side(right, d)
    half_c = 0.5 * jnp.maximum(speed_l, speed_r)
    out = []
    for k in range(8):
        jump = half_c * (cons_r[k] - cons_l[k])
        out.append(-jump if flux_l[k] is None else 0.5 * (flux_l[k] + flux_r[k]) - jump)
    return out


def periodic(q, axis, d):
    size = q[0].shape[axis]
    back = [pltpu.roll(x, 1, axis) for x in q]
    ahead = [pltpu.roll(x, size - 1, axis) for x in q]
    slope = half_slope(back, q, ahead)
    left = [x + s for x, s in zip(q, slope)]
    right = [pltpu.roll(x - s, size - 1, axis) for x, s in zip(q, slope)]
    flux = face(left, right, d)
    return [pltpu.roll(f, 1, axis) - f for f in flux]


def add(a, b):
    return [x + y for x, y in zip(a, b)]


def plane(ref, x):
    return [ref[k, x] for k in range(8)]


def upper_face(ref, x):
    a, b, c, d = (plane(ref, x + k) for k in (-1, 0, 1, 2))
    left = add(b, half_slope(a, b, c))
    right = [v - s for v, s in zip(c, half_slope(b, c, d))]
    return face(left, right, 0)


def sideways(q):
    return add(periodic(q, 0, 1), periodic(q, 1, 2))


def sweep_planes(ref, first, count, put, others):
    def body(step, below):
        x = first + step
        above = upper_face(ref, x)
        q = plane(ref, x)
        change = [f - g for f, g in zip(below, above)]
        put(x, step, q, add(change, others(step, q)))
        return above

    lax.fori_loop(0, count, body, upper_face(ref, first - 1))


def stage_own(own_ref, side_ref):
    def body(x, carry):
        for k, value in enumerate(sideways(plane(own_ref, x))):
            side_ref[k, x] = value
        return carry

    lax.fori_loop(0, own_ref.shape[1], body, 0)


def stage_one(
    own_ref, mag_a, mag_b, five_a, five_b, own_side_ref, next_ref, half_ref, pad_ref, side_ref
):
    me = lax.axis_index("mag")
    last = lax.axis_size("mag") - 1
    even = me % 2 == 0
    cx = own_ref.shape[1]
    for k in range(8):
        for x in range(cx):
            in_field = 4 <= k < 7
            from_a = mag_a[k - 4, x] if in_field else five_a[min(k, 4), x]
            from_b = mag_b[k - 4, x] if in_field else five_b[min(k, 4), x]
            low = jnp.where(even, from_b, from_a)
            high = jnp.where(even, from_a, from_b)
            pad_ref[k, x] = jnp.where(me == 0, own_ref[k, 0], low)
            pad_ref[k, cx + x] = own_ref[k, x]
            pad_ref[k, 2 * cx + x] = jnp.where(me == last, own_ref[k, cx - 1], high)
            side_ref[k, 2 + x] = own_side_ref[k, x]

    def beside(i, carry):
        step = jnp.where(i < 2, i, cx + i)
        for k, value in enumerate(sideways(plane(pad_ref, cx - 2 + step))):
            side_ref[k, step] = value
        return carry

    lax.fori_loop(0, 4, beside, 0)

    def put(x, step, q, change):
        start = conserved(q)
        first = [s + TIME_STEP * c for s, c in zip(start, change)]
        q1 = primitive(first)
        for k in range(8):
            next_ref[k, step] = q1[k]

        @pl.when(jnp.logical_and(step >= 2, step < cx + 2))
        def _():
            for k in range(8):
                half_ref[k, step - 2] = 0.5 * (start[k] + first[k])

    sweep_planes(pad_ref, cx - 2, cx + 4, put, lambda step, q: plane(side_ref, step))

    @pl.when(me == 0)
    def _():
        for k in range(8):
            next_ref[k, 0] = next_ref[k, 2]
            next_ref[k, 1] = next_ref[k, 2]

    @pl.when(me == last)
    def _():
        for k in range(8):
            next_ref[k, cx + 2] = next_ref[k, cx + 1]
            next_ref[k, cx + 3] = next_ref[k, cx + 1]


def stage_two(next_ref, half_ref, rho_ref, vel_ref, mag_ref, prs_ref, end_ref):
    end_ref[...] = half_ref[0, 0, 0:8]
    cx = half_ref.shape[1]

    def put(x, step, q, change):
        final = [half_ref[k, step] + (0.5 * TIME_STEP) * change[k] for k in range(8)]
        q2 = primitive(final)
        rho_ref[step] = q2[0]
        for k in range(3):
            vel_ref[k, step] = q2[1 + k]
            mag_ref[k, step] = q2[4 + k]
        prs_ref[step] = q2[7]

    sweep_planes(next_ref, 2, cx, put, lambda step, q: sideways(q))


def pick_current(own_ref, cell_ref, strip_ref, mag_a, mag_b, out_ref, five_out):
    me = lax.axis_index("mag")
    last = lax.axis_size("mag") - 1
    even = me % 2 == 0
    cx, ny, nz = own_ref.shape[1:]
    five_out[0:4] = own_ref[0:4]
    five_out[4] = own_ref[7]
    rows = []
    for x in range(cx):
        bx, by, bz = (own_ref[4 + k, x] for k in range(3))

        def neighbour(k, step):
            if 0 <= x + step < cx:
                return own_ref[4 + k, x + step]
            if step < 0:
                below = jnp.where(even, mag_b[k, cx - 1], mag_a[k, cx - 1])
                return jnp.where(me == 0, own_ref[4 + k, x], below)
            above = jnp.where(even, mag_a[k, 0], mag_b[k, 0])
            return jnp.where(me == last, own_ref[4 + k, x], above)

        def along_x(k):
            return 0.5 * (neighbour(k, 1) - neighbour(k, -1))

        def along(v, axis):
            return 0.5 * (pltpu.roll(v, v.shape[axis] - 1, axis) - pltpu.roll(v, 1, axis))

        jx = along(bz, 0) - along(by, 1)
        jy = along(bx, 1) - along_x(2)
        jz = along_x(1) - along(bx, 0)
        norm = jnp.sqrt(bx * bx + by * by + bz * bz + 1.0)
        rows.append(SOURCE_GAIN * (jx * bx + jy * by + jz * bz) / norm)
    table = jnp.concatenate(rows, axis=0)
    count = table.shape[0]
    both = jnp.concatenate(pieces(table), axis=0)
    cells = cell_ref[...]
    hi, lo = cells // nz, (cells % nz).astype(F32)
    index = lax.broadcasted_iota(I32, (count, LANES), 0)
    points = cells.shape[0]
    for s in range(points):
        hot = rows_hot(lo[s : s + 1], nz)
        found = jnp.dot(both, hot, preferred_element_type=F32)
        found = found[:count] + found[count:]
        mine = jnp.where(index == hi[s : s + 1], found, 0.0)
        out_ref[s : s + 1, :] = jnp.sum(mine, axis=0, keepdims=True)
    out_ref[points:, :] = strip_ref[...]


def load_arguments(
    rho_ref, vel_ref, mag_ref, prs_ref, cell_ref, cond_ref, own_out, cell_out, strip_out, rows, sems
):
    pairs = [
        (cond_ref, rows),
        (cell_ref, cell_out),
        (rho_ref, own_out.at[0]),
        (vel_ref, own_out.at[pl.ds(1, 3)]),
        (mag_ref, own_out.at[pl.ds(4, 3)]),
        (prs_ref, own_out.at[7]),
    ]
    copies = [
        pltpu.make_async_copy(source, target, sems.at[k])
        for k, (source, target) in enumerate(pairs)
    ]
    for copy in copies:
        copy.start()
    copies[0].wait()
    lat, columns = rows.shape
    strips = columns // LANES
    for r in range(lat):
        for strip in range(strips):
            place = r * strips + strip
            strip_out[place : place + 1, :] = rows[r : r + 1, strip * LANES : (strip + 1) * LANES]
    for copy in copies[1:]:
        copy.wait()


def east_of(v):
    lane = lax.broadcasted_iota(I32, v.shape, 2)
    turned = pltpu.roll(v, v.shape[2] - 1, 2)
    return jnp.where(lane == v.shape[2] - 1, pltpu.roll(turned, v.shape[1] - 1, 1), turned)


def west_of(v):
    lane = lax.broadcasted_iota(I32, v.shape, 2)
    turned = pltpu.roll(v, 1, 2)
    return jnp.where(lane == 0, pltpu.roll(turned, 1, 1), turned)


def scatter_block(value, hi, lo, count):
    hi, lo = hi.astype(F32), lo.astype(F32)
    high_piece = value.astype(BF16).astype(F32)
    low_piece = value - high_piece
    lefts, rights = [], []
    for s in range(value.shape[0]):
        lefts.append(rows_hot(hi[s : s + 1], count))
        hot = rows_hot(lo[s : s + 1], LANES)
        two = []
        for piece in (high_piece, low_piece):
            wide = jnp.broadcast_to(piece[s : s + 1], (16, LANES)).astype(BF16)
            two.append(hot * jnp.concatenate([wide] * (LANES // 16), axis=0))
        rights.append(jnp.concatenate(two, axis=0))
    left = jnp.concatenate(lefts, axis=1)
    right = jnp.concatenate(rights, axis=1)
    return lax.dot_general(left, right, (((1,), (1,)), ((), ())), preferred_element_type=F32)


def repeat(count, body):
    if count <= 8:
        for i in range(count):
            body(i)
    else:
        lax.fori_loop(0, count, lambda i, carry: (body(i), carry)[1], 0)


def origin(me, devices, j):
    mask, bit, k = 0, devices // 2, 0
    while bit > 1:
        mask = mask + ((j >> k) & 1) * bit
        bit, k = bit // 2, k + 1
    return jnp.bitwise_xor(me, mask)


def scatter_new(first, blocks, points, lat, strips):
    def kernel(*refs):
        *total_in, load_ref, owner_ref, row_ref, lon_ref, out_ref = refs
        me = lax.axis_index("mag")
        devices = lax.axis_size("mag")
        count = out_ref.shape[0]
        rows = min(count, 1024)
        stride = load_ref.shape[0] // blocks

        def part(j, g, base_ref):
            device = origin(me, devices, first + j)
            at = pl.ds(pl.multiple_of(device * points, points), points)
            value = load_ref[pl.ds(pl.multiple_of(j * stride, 8), points), :]
            hi = (owner_ref[at, :] * lat + row_ref[at, :]) * strips + lon_ref[at, :] // LANES
            lo = lon_ref[at, :] % LANES
            new = scatter_block(value, hi - g * rows, lo, rows)
            place = pl.ds(pl.multiple_of(g * rows, rows), rows)
            out_ref[place, :] = new if base_ref is None else base_ref[place, :] + new

        def group(g):
            part(0, g, total_in[0] if total_in else None)
            repeat(blocks - 1, lambda j: part(j + 1, g, out_ref))

        repeat(count // rows, group)

    return kernel


def handing_on(kernel, count):
    def run(*refs):
        outs = count + 1
        given = refs[-outs - count : -outs]
        for source, target in zip(given, refs[-count:]):
            target[...] = source[...]
        kernel(*refs[: -outs - count], refs[-outs])

    return run


def scatter_last(blocks, points, lat, strips):
    def kernel(total_ref, before_ref, load_ref, owner_ref, row_ref, lon_ref, out_ref, work_ref):
        half = blocks // 2
        scatter_new(half, half, points, lat, strips)(
            total_ref, load_ref, owner_ref, row_ref, lon_ref, work_ref
        )
        count = work_ref.shape[0]
        out_ref[:count, :] = work_ref[:, :LANES] + work_ref[:, LANES:]
        cells = lat * strips
        stride = points + cells
        for j in range(blocks):
            ref = before_ref if j < half else load_ref
            start = (j % half) * stride + points
            out_ref[count + j * cells : count + (j + 1) * cells, :] = ref[start : start + cells, :]

    return kernel


def solve_and_read(blocks, points, lat, strips):
    def kernel(
        mine_ref, their_ref, owner_ref, row_ref, lon_ref, flat_ref, out_ref, s_ref, w_ref, phi_ref
    ):
        me = lax.axis_index("mag")
        devices = lax.axis_size("mag")
        rows = devices * lat
        count = rows * strips
        cells = lat * strips
        zeros = jnp.zeros((1, strips, LANES), F32)
        for ref in (s_ref, phi_ref.at[0], phi_ref.at[1]):
            ref[0:1] = zeros
            ref[rows + 1 : rows + 2] = zeros

        def place(j):
            at = pl.ds(pl.multiple_of(count + j * cells, cells), cells)
            for ref, who in ((mine_ref, me), (their_ref, jnp.bitwise_xor(me, 1))):
                device = origin(who, devices, j)
                s_ref[pl.ds(device * lat + 1, lat)] = ref[at, :].reshape(lat, strips, LANES)

        repeat(blocks, place)
        chunk = min(8, rows)

        def prepare(i):
            r = i * chunk
            s, above, below = (s_ref[pl.ds(r + k, chunk)] for k in (1, 0, 2))
            north, south = 0.5 * (s + above), 0.5 * (s + below)
            east = (0.5 * LON_WEIGHT) * (s + east_of(s))
            west = (0.5 * LON_WEIGHT) * (s + west_of(s))
            inverse = 1.0 / (north + south + east + west + LEAK_RATE * s)
            at = pl.ds(pl.multiple_of(r * strips, 8), chunk * strips)
            source = (mine_ref[at, :] + their_ref[at, :]).reshape(chunk, strips, LANES)
            for k, value in enumerate((source, north, south, east, west)):
                w_ref[k, pl.ds(r, chunk)] = value * inverse
            phi_ref[0, pl.ds(r + 1, chunk)] = source * inverse

        repeat(rows // chunk, prepare)
        for sweep in range(SWEEPS - 1):
            old, new = sweep % 2, 1 - sweep % 2

            def relax(i):
                r = i * chunk
                phi, above, below = (phi_ref[old, pl.ds(r + k, chunk)] for k in (1, 0, 2))
                source, north, south, east, west = (w_ref[k, pl.ds(r, chunk)] for k in range(5))
                phi_ref[new, pl.ds(r + 1, chunk)] = (
                    source
                    + north * above
                    + south * below
                    + east * east_of(phi)
                    + west * west_of(phi)
                )

            repeat(rows // chunk, relax)
        last = (SWEEPS - 1) % 2
        own = phi_ref[last, pl.ds(me * lat + 1, lat)]
        for strip in range(strips):
            flat_ref[:, strip * LANES : (strip + 1) * LANES] = own[:, strip, :]

        block = min(256, count)
        groups = count // block
        table = phi_ref[last, pl.ds(1, rows)].reshape(count, LANES)
        table = jnp.concatenate([table[g * block : (g + 1) * block] for g in range(groups)], axis=1)
        both = jnp.concatenate(pieces(table), axis=0)
        at = pl.ds(pl.multiple_of(me * points, points), points)
        owner, row, lon = owner_ref[at, :], row_ref[at, :], lon_ref[at, :]
        hi = (owner * lat + row) * strips + lon // LANES
        group, hi, lo = hi // block, hi % block, lon % LANES
        index = lax.broadcasted_iota(I32, (block, LANES), 0)
        columns = []
        for p in range(points):
            stack = []
            for g in range(groups):
                key = jnp.where(group[p : p + 1] == g, lo[p : p + 1], -1).astype(F32)
                stack.append(rows_hot(key, LANES))
            columns.append(jnp.concatenate(stack, axis=0))
        found = jnp.dot(both, jnp.concatenate(columns, axis=1), preferred_element_type=F32)
        found = found[:block] + found[block:]
        for p in range(points):
            part = found[:, p * LANES : (p + 1) * LANES]
            part = jnp.where(index == hi[p : p + 1], part, 0.0)
            out_ref[p : p + 1, :] = jnp.sum(part, axis=0, keepdims=True)

    return kernel


def swap(values, bit):
    devices = lax.axis_size("mag")
    return lax.ppermute(values, "mag", [(i, i ^ bit) for i in range(devices)])


def swap_next(values):
    devices = lax.axis_size("mag")
    pairs = [(i, (i + (1 if i % 2 else -1)) % devices) for i in range(devices)]
    return lax.ppermute(values, "mag", pairs)


def shards(
    density, velocity, mag_field, pressure, conductance, shell_cell, foot_owner, foot_row, foot_lon
):
    devices = lax.axis_size("mag")
    cx, ny, nz = density.shape
    lat, columns = conductance.shape
    strips = columns // LANES
    shell_count = shell_cell.shape[0]
    points = shell_count // LANES
    cells = lat * strips
    count = devices * cells
    shape = jax.ShapeDtypeStruct

    tile = shape((points, LANES), I32)
    slab = shape((8, cx, ny, nz), F32)
    mag_a, mag_b = swap(mag_field, 1), swap_next(mag_field)
    own, cell, strip = call(
        load_arguments,
        [slab, tile, shape((cells, LANES), F32)],
        [pltpu.VMEM((lat, columns), F32), pltpu.SemaphoreType.DMA((6,))],
        [HBM] * 6,
    )(
        *(
            pltpu.with_memory_space_constraint(x, pltpu.HBM)
            for x in (
                density,
                velocity,
                mag_field,
                pressure,
                shell_cell.reshape(-1, LANES),
                conductance,
            )
        )
    )
    own_side = call(stage_own, slab)(own)

    owner = foot_owner.reshape(-1, LANES)
    row = foot_row.reshape(-1, LANES)
    lon = foot_lon.reshape(-1, LANES)

    load, five = call(
        pick_current,
        [shape((points + cells, LANES), F32), shape((5, cx, ny, nz), F32)],
        after=(own_side,),
    )(own, cell, strip, mag_a, mag_b)
    five_a, five_b = swap(five, 1), swap_next(five)

    grid = shape((count, 2 * LANES), F32)
    total, blocks, done = (), 1, 0
    bit = devices // 2
    while bit > 1:
        arrived = swap(load, bit)
        if blocks > 1:
            kernel = handing_on(scatter_new(done, blocks - done, points, lat, strips), 1)
            total, load = call(kernel, [grid, shape(load.shape, F32)])(
                *total, new, owner, row, lon, load
            )
            total, done = (total,), blocks
        before, new = load, arrived
        load = jnp.concatenate([load, arrived], axis=0)
        if blocks == 1:
            new = load
        blocks, bit = blocks * 2, bit // 2

    following, half = call(
        stage_one,
        [shape((8, cx + 4, ny, nz), F32), slab],
        [pltpu.VMEM((8, 3 * cx, ny, nz), F32), pltpu.VMEM((8, cx + 4, ny, nz), F32)],
    )(own, mag_a, mag_b, five_a, five_b, own_side)

    grids = shape((count + count // 2, LANES), F32)
    mine = call(
        scatter_last(blocks, points, lat, strips),
        grids,
        [pltpu.VMEM((count, 2 * LANES), F32)],
        after=(half,),
    )(*total, before, new, owner, row, lon)
    theirs = swap(mine, 1)

    cell_shape = shape((cx, ny, nz), F32)
    vector_shape = shape((3, cx, ny, nz), F32)
    new_density, new_velocity, new_field, new_pressure, end = call(
        stage_two, [cell_shape, vector_shape, vector_shape, cell_shape, shape((8, LANES), F32)]
    )(following, half)

    potential, shell_potential = call(
        solve_and_read(blocks, points, lat, strips),
        [shape((lat, columns), F32), shape((points, LANES), F32)],
        [
            pltpu.VMEM((devices * lat + 2, strips, LANES), F32),
            pltpu.VMEM((5, devices * lat, strips, LANES), F32),
            pltpu.VMEM((2, devices * lat + 2, strips, LANES), F32),
        ],
        after=(end,),
    )(mine, theirs, owner, row, lon)
    return (
        new_density,
        new_velocity,
        new_field,
        new_pressure,
        potential,
        shell_potential.reshape(shell_count),
    )


def solution(mesh):
    both = ("parts", "mag")
    in_specs = (
        P(both, None, None),
        P(None, both, None, None),
        P(None, both, None, None),
        P(both, None, None),
        P(both, None),
        P("mag"),
        P(),
        P(),
        P(),
    )
    out_specs = (
        P(both, None, None),
        P(None, both, None, None),
        P(None, both, None, None),
        P(both, None, None),
        P(both, None),
        P(both),
    )
    return jax.shard_map(shards, mesh=mesh, in_specs=in_specs, out_specs=out_specs, check_vma=False)
```
